32 devices in a mesh: fsdp: 4 (over y, x), heads: 4 (over z), tensor: 2 (over core).
Axes of the slice: x: 2, y: 2, z: 4, core: 2. Of those that a mesh axis runs over, the one named last changes fastest.
Arguments:
- tokens: bfloat16 [12608, 512], P(('fsdp', 'heads', 'tensor')), may hold values from -6 to 6
- cotangent: bfloat16 [12608, 512], P(('fsdp', 'heads', 'tensor')), may hold values from -6 to 6
- image_counts: int32 [4], P('fsdp'), may hold values from 15 to 16
- w_qkv: bfloat16 [1, 3, 512, 512], P(None, None, 'fsdp', ('heads', 'tensor')), may hold values from -0.25 to 0.25
- w_out: bfloat16 [1, 512, 512], P(None, ('heads', 'tensor'), 'fsdp'), may hold values from -1 to 1
- ln_gain: float32 [1, 2, 512], replicated, may hold values from 0.5 to 1.5
- ln_bias: float32 [1, 2, 512], replicated, may hold values from -1.75 to 1.75
- w_router: bfloat16 [1, 512, 32], replicated, may hold values from -0.1875 to 0.1875
- w_in: bfloat16 [1, 32, 512, 2048], P(None, 'heads', 'fsdp', 'tensor'), may hold values from -0.25 to 0.25
- w_back: bfloat16 [1, 32, 2048, 512], P(None, 'heads', 'tensor', 'fsdp'), may hold values from -2 to 2
- expert_ids: int32 [1, 12608, 2], P(None, 'fsdp'), may hold values from 0 to 31, as said below
- slots: int32 [1, 12608, 2], P(None, 'fsdp'), may hold values from -1 to 255, as said below
Outputs:
- output: bfloat16 [12608, 512], P(('fsdp', 'heads', 'tensor'))
- tokens_grad: float32 [12608, 512], P(('fsdp', 'heads', 'tensor'))
- w_qkv_grad: float32 [1, 3, 512, 512], P(None, None, 'fsdp', ('heads', 'tensor'))
- w_out_grad: float32 [1, 512, 512], P(None, ('heads', 'tensor'), 'fsdp')
- ln_gain_grad: float32 [1, 2, 512], replicated
- ln_bias_grad: float32 [1, 2, 512], replicated
- w_router_grad: float32 [1, 512, 32], replicated
- w_in_grad: float32 [1, 32, 512, 2048], P(None, 'heads', 'fsdp', 'tensor')
- w_back_grad: float32 [1, 32, 2048, 512], P(None, 'heads', 'tensor', 'fsdp')
The draws below stay inside these ranges and needn't reach their ends.
Inputs may be any that keep to these rules, and one draw needn't show every extreme that they name: `expert_ids`: each token names two different experts. `slots`: a choice's slot is its place, in token order, among the choices of its group and block that name the same expert, or -1 where that place is 256 or more; in every group and block some expert is named more than 256 times.
All inputs are finite; a program needn't handle non-finite values.
Results may differ from the reference program's by a relative error of at most 0.012.
Values may be sent and summed in bfloat16 or wider, within the bound.
A program may use at most 192 MiB of HBM per device.

```python
import jax
import jax.numpy as jnp
from jax import lax

D = 512
HEADS = 8
HEAD = 64
FF = 2048
E = 32
SEQ = 197
LAYERS = 1
IMG_DEV = 16
CAP = 256
GROUPS = 4
TOKENS = 12608


def route_tables(key):
    group_rows = IMG_DEV * SEQ

    def one_group(group_key):
        draw_keys = jax.random.split(group_key, 4)
        heavy_expert = jax.random.randint(draw_keys[0], (), 0, E)
        forced = jax.random.permutation(draw_keys[1], group_rows) <= CAP
        first_pick = jnp.where(forced, heavy_expert, jax.random.randint(draw_keys[2], (group_rows,), 0, E))
        second = (first_pick + 1 + jax.random.randint(draw_keys[3], (group_rows,), 0, E - 1)) % E
        named_expert = jnp.stack([first_pick, second], axis=1).reshape(-1).astype(jnp.int32)
        choice_total = 2 * group_rows
        positions = jnp.arange(choice_total, dtype=jnp.int32)
        sorted_order = jnp.argsort(named_expert * choice_total + positions)
        tallies = jnp.sum((named_expert[:, None] == jnp.arange(E, dtype=jnp.int32)[None, :]).astype(jnp.int32), axis=0)
        starts = jnp.cumsum(tallies) - tallies
        ranked = positions - starts[named_expert[sorted_order]]
        rank_back = jnp.zeros((choice_total,), jnp.int32).at[sorted_order].set(ranked)
        slot_rows = jnp.where(rank_back < CAP, rank_back, -1).astype(jnp.int32)
        return (named_expert.reshape(group_rows, 2), slot_rows.reshape(group_rows, 2))
    group_keys = jax.random.split(key, LAYERS * GROUPS)
    named_all, slot_all = jax.vmap(one_group)(group_keys)
    return (named_all.reshape(LAYERS, GROUPS * group_rows, 2), slot_all.reshape(LAYERS, GROUPS * group_rows, 2))


def draw_expert_ids(key, part):
    tables = route_tables(key)
    return tables[0]


def draw_slots(key, part):
    tables = route_tables(key)
    return tables[1]


def with_ends(array, stream_key, low, high):
    spot = [jax.random.randint(jax.random.fold_in(stream_key, axis), (), 0, length) for axis, length in enumerate(array.shape)]
    main_axis = array.shape.index(max(array.shape))
    next_to = spot[:main_axis] + [(spot[main_axis] + 1) % array.shape[main_axis]] + spot[main_axis + 1:]
    return array.at[tuple(spot)].set(low).at[tuple(next_to)].set(high)


def steps_of(rng, shape, cuts, low, largest):
    loudness, own = 1.0, jax.random.fold_in(rng, 6)
    for position, parts in cuts:
        heights = jnp.exp(jax.random.uniform(jax.random.fold_in(own, position), (parts,), jnp.float32, low / len(cuts), largest / len(cuts)))
        loudness = loudness * jnp.repeat(heights, shape[position] // parts).reshape([-1 if axis == position else 1 for axis in range(len(shape))])
    return loudness


def scatter_about(own_key, shape, width, most, shards=(), kind=jnp.bfloat16):
    entries = width * jax.random.normal(own_key, shape, jnp.float32)
    if shards:
        entries = entries * steps_of(own_key, shape, shards, -0.22, 0.18)
    return jnp.clip(entries, -most, most).astype(kind)


def setup_inputs(seed: int = 0) -> dict:
    arg_keys = jax.random.split(jax.random.key(seed), 13)
    return {
        "tokens": scatter_about(arg_keys[0], (TOKENS, D), 1.0, 6.0, ((0, 32),)),
        "cotangent": scatter_about(arg_keys[1], (TOKENS, D), 1.0, 6.0, ((0, 32),)),
        "image_counts": with_ends(jax.random.randint(arg_keys[2], (GROUPS,), IMG_DEV - 1, IMG_DEV + 1), jax.random.fold_in(arg_keys[2], 1), IMG_DEV - 1, IMG_DEV).astype(jnp.int32),
        "w_qkv": scatter_about(arg_keys[3], (LAYERS, 3, D, D), D ** -0.5, 0.25, ((2, 4), (3, 8))),
        "w_out": scatter_about(arg_keys[4], (LAYERS, D, D), (D // 16) ** -0.5, 1.0, ((1, 8), (2, 4))),
        "ln_gain": jnp.clip(1.0 + 0.1 * jax.random.normal(arg_keys[5], (LAYERS, 2, D), jnp.float32), 0.5, 1.5),
        "ln_bias": scatter_about(arg_keys[6], (LAYERS, 2, D), 0.3, 1.75, (), jnp.float32),
        "w_router": scatter_about(arg_keys[7], (LAYERS, D, E), (2 * D) ** -0.5, 0.1875),
        "w_in": scatter_about(arg_keys[8], (LAYERS, E, D, FF), D ** -0.5, 0.25, ((1, 4), (2, 4), (3, 2))),
        "w_back": scatter_about(arg_keys[9], (LAYERS, E, FF, D), (max(FF // 256, 1)) ** -0.5, 2.0, ((1, 4), (2, 2), (3, 4))),
        "expert_ids": draw_expert_ids(jax.random.fold_in(arg_keys[12], 71), 0),
        "slots": draw_slots(jax.random.fold_in(arg_keys[12], 71), 0),
    }


@jax.custom_vjp
def low(v):
    return lax.optimization_barrier(v.astype(jnp.bfloat16)).astype(jnp.float32)

@jax.custom_vjp
def low_back(v):
    return v

def low_keep(v):
    return (low(v), None)

def low_pass(kept, grad):
    return (grad,)

def back_keep(v):
    return (v, None)

def back_low(kept, grad):
    return (low(grad),)
low.defvjp(low_keep, low_pass)
low_back.defvjp(back_keep, back_low)
precise = lax.Precision.HIGHEST

def matmul(left, right):
    return jnp.dot(left, right, precision=precise, preferred_element_type=jnp.float32)

def layer_norm(value, ln_gains, ln_shift):
    centred = value - lax.optimization_barrier(jnp.mean(value, axis=-1, keepdims=True))
    spread = lax.optimization_barrier(jnp.mean(centred * centred, axis=-1, keepdims=True))
    return centred * lax.rsqrt(spread + 1e-06) * ln_gains + ln_shift

def slot_tables(named_expert, slot_rows):
    group_rows = named_expert.shape[0]
    places = jnp.where(slot_rows >= 0, named_expert * CAP + slot_rows, E * CAP).astype(jnp.int32)
    token_ids = (jnp.arange(2 * group_rows) // 2).astype(jnp.int32)
    owners = jnp.full((E * CAP + 1,), group_rows, jnp.int32).at[places.reshape(-1)].set(token_ids)
    return (places, owners[:E * CAP])

def moe_block(residual, qkv_weight, out_weight, ln_gains, ln_shift, router_weight, in_weight, back_weight, named_expert, places, owners):
    q_scale = HEAD ** (-0.5)
    head_shape = (IMG_DEV, SEQ, HEADS, HEAD)
    normed = low(layer_norm(residual, ln_gains[0], ln_shift[0]))
    queries = low(low_back(matmul(normed, qkv_weight[0]) * q_scale))
    key_rows = low(low_back(matmul(normed, qkv_weight[1])))
    value_rows = low(low_back(matmul(normed, qkv_weight[2])))
    scores = low_back(jnp.einsum('bqhd,bkhd->bhqk', queries.reshape(head_shape), key_rows.reshape(head_shape), precision=precise))
    attn_probs = low(jax.nn.softmax(scores, axis=-1))
    mixed_rows = jnp.einsum('bhqk,bkhd->bqhd', attn_probs, value_rows.reshape(head_shape), precision=precise)
    mixed_rows = low(low_back(mixed_rows.reshape(IMG_DEV * SEQ, D)))
    middle = residual + low_back(matmul(mixed_rows, out_weight))
    normed_two = low(layer_norm(middle, ln_gains[1], ln_shift[1]))
    router = jax.nn.softmax(low_back(matmul(normed_two, router_weight)), axis=-1)
    gate_values = jnp.take_along_axis(router, named_expert, axis=1) * (places < E * CAP)
    padded = jnp.concatenate([normed_two, jnp.zeros((1, D), jnp.float32)], axis=0)
    routed = padded[owners].reshape(E, CAP, D)
    hidden = low_back(jnp.einsum('ecd,edf->ecf', routed, in_weight, precision=precise))
    active = low(jax.nn.gelu(hidden, approximate=False))
    result = low_back(jnp.einsum('ecf,efd->ecd', active, back_weight, precision=precise))
    flat_result = jnp.concatenate([result.reshape(E * CAP, D), jnp.zeros((1, D), jnp.float32)], axis=0)
    expert_out = low_back(lax.optimization_barrier(jnp.sum(flat_result[places] * gate_values[:, :, None], axis=1)))
    return middle + expert_out

def reference(tokens, cotangent, image_counts, w_qkv, w_out, ln_gain, ln_bias, w_router, w_in, w_back, expert_ids, slots):
    params = tuple((weight.astype(jnp.float32) for weight in (w_qkv, w_out, ln_gain, ln_bias, w_router, w_in, w_back)))
    group_rows = IMG_DEV * SEQ
    group_tokens = tokens.astype(jnp.float32).reshape(GROUPS, group_rows, D)
    group_cots = cotangent.astype(jnp.float32).reshape(GROUPS, group_rows, D)
    group_ids = jnp.transpose(expert_ids.reshape(LAYERS, GROUPS, group_rows, 2), (1, 0, 2, 3))
    group_slots = jnp.transpose(slots.reshape(LAYERS, GROUPS, group_rows, 2), (1, 0, 2, 3))

    def one_group(running, inputs):
        residual, cot_rows, live_count, named_expert, slot_rows = inputs
        tables = [slot_tables(named_expert[block_index], slot_rows[block_index]) for block_index in range(LAYERS)]

        def forward(stream, qkv_all, out_all, gain_all, shift_all, router_all, in_all, back_all):
            for block_index in range(LAYERS):
                stream = moe_block(stream, qkv_all[block_index], out_all[block_index], gain_all[block_index], shift_all[block_index], router_all[block_index], in_all[block_index], back_all[block_index], named_expert[block_index], tables[block_index][0], tables[block_index][1])
            return stream
        block_out, pull_back = jax.vjp(forward, residual, *params)
        live_rows = (jnp.arange(group_rows) // SEQ < live_count).astype(jnp.float32)
        grad_list = pull_back(cot_rows * live_rows[:, None])
        running = tuple((total_grad + new_grad for total_grad, new_grad in zip(running, grad_list[1:])))
        return (running, (block_out, grad_list[0]))
    start_grads = tuple((jnp.zeros_like(weight) for weight in params))
    running, stacked = lax.scan(one_group, start_grads, (group_tokens, group_cots, image_counts, group_ids, group_slots))
    outputs, input_grads = stacked
    return (outputs.reshape(TOKENS, D).astype(jnp.bfloat16), input_grads.reshape(TOKENS, D), running[0], running[1], running[2], running[3], running[4], running[5], running[6])
```

```python
import jax
import jax.numpy as jnp
from jax import lax
from jax.sharding import PartitionSpec as P

HEAD = 64
SEQ = 197
LAYERS = 1
CAP = 256


def layer_norm(value, ln_gains, ln_shift):
    centred = value - jnp.mean(value, axis=-1, keepdims=True)
    spread = jnp.mean(centred * centred, axis=-1, keepdims=True)
    return centred * lax.rsqrt(spread + 1e-06) * ln_gains + ln_shift


def gelu_exact(value):
    return jax.nn.gelu(value, approximate=False)


def with_zero_row(matrix):
    return jnp.concatenate([matrix, jnp.zeros((1,) + matrix.shape[1:], matrix.dtype)], axis=0)


def slot_tables(named_expert, slot_rows, first_expert, local_experts):
    group_rows = named_expert.shape[0]
    is_local = (
        (slot_rows >= 0)
        & (named_expert >= first_expert)
        & (named_expert < first_expert + local_experts)
    )
    places = jnp.where(
        is_local, (named_expert - first_expert) * CAP + slot_rows, local_experts * CAP
    )
    picked = jnp.full((local_experts * CAP + 1,), 2 * group_rows, jnp.int32)
    picked = picked.at[places.reshape(-1)].set(jnp.arange(2 * group_rows, dtype=jnp.int32))
    return (places, picked[: local_experts * CAP])


def joined_qkv(qkv_weight):
    head_cols = qkv_weight.shape[2]
    return jnp.transpose(qkv_weight, (1, 0, 2)).reshape(qkv_weight.shape[1], 3 * head_cols)


def forward_block(
    residual, weights, ln_gains, ln_shift, router_weight, named_expert, slot_rows, first_expert
):
    qkv_weight, out_weight, in_weight, back_weight = weights
    own_rows, widths = residual.shape
    group_rows = named_expert.shape[0]
    head_cols = qkv_weight.shape[2]
    local_experts = in_weight.shape[0]
    head_shape = (group_rows // SEQ, SEQ, head_cols // HEAD, HEAD)
    q_scale = HEAD ** (-0.5)
    flat_qkv = joined_qkv(qkv_weight)
    normed_rows = layer_norm(residual, ln_gains[0], ln_shift[0]).astype(jnp.bfloat16)
    normed = lax.all_gather(normed_rows, ("heads", "tensor"), axis=0, tiled=True)
    projected = jnp.dot(normed, flat_qkv, preferred_element_type=jnp.float32)
    queries = (projected[:, :head_cols] * q_scale).astype(jnp.bfloat16).reshape(head_shape)
    key_rows = projected[:, head_cols : 2 * head_cols].astype(jnp.bfloat16).reshape(head_shape)
    value_rows = projected[:, 2 * head_cols :].astype(jnp.bfloat16).reshape(head_shape)
    scores = jnp.einsum("bqhd,bkhd->bhqk", queries, key_rows, preferred_element_type=jnp.float32)
    log_total = jax.nn.logsumexp(scores, axis=-1)
    attn_probs = jax.nn.softmax(scores, axis=-1).astype(jnp.bfloat16)
    mixed_rows = jnp.einsum(
        "bhqk,bkhd->bqhd", attn_probs, value_rows, preferred_element_type=jnp.float32
    )
    mixed_rows = mixed_rows.reshape(group_rows, head_cols).astype(jnp.bfloat16)
    middle = residual + lax.psum_scatter(
        jnp.dot(mixed_rows, out_weight, preferred_element_type=jnp.float32),
        ("heads", "tensor"),
        scatter_dimension=0,
        tiled=True,
    )
    head_full = ()
    normed_two_rows = layer_norm(middle, ln_gains[1], ln_shift[1]).astype(jnp.bfloat16)
    normed_two = lax.all_gather(normed_two_rows, ("heads", "tensor"), axis=0, tiled=True)
    router = jax.nn.softmax(
        jnp.dot(normed_two, router_weight, preferred_element_type=jnp.float32), axis=-1
    )
    gate_values = jnp.take_along_axis(router, named_expert, axis=1) * (slot_rows >= 0)
    places, picked = slot_tables(named_expert, slot_rows, first_expert, local_experts)
    routed = with_zero_row(normed_two)[picked // 2].reshape(local_experts, CAP, widths)
    hidden = jnp.einsum("ecd,edf->ecf", routed, in_weight, preferred_element_type=jnp.float32)
    active = gelu_exact(hidden).astype(jnp.bfloat16)
    result = jnp.einsum("ecf,efd->ecd", active, back_weight, preferred_element_type=jnp.float32)
    flat_result = with_zero_row(result.reshape(local_experts * CAP, widths))
    block_out = middle + lax.psum_scatter(
        (
            flat_result[places[:, 0]] * gate_values[:, 0:1]
            + flat_result[places[:, 1]] * gate_values[:, 1:2]
        ).astype(jnp.bfloat16),
        ("heads", "tensor"),
        scatter_dimension=0,
        tiled=True,
    ).astype(jnp.float32)
    stored = (
        residual,
        middle,
        normed,
        queries,
        key_rows,
        value_rows,
        log_total,
        mixed_rows,
        normed_two_rows,
        router,
        gate_values,
        places,
        picked,
        routed,
        hidden,
        active,
        flat_result,
    )
    return (block_out, stored, head_full)


def backward_block(
    grad_rows, stored, weights, ln_gains, ln_shift, router_weight, named_expert, row_start
):
    qkv_weight, out_weight, in_weight, back_weight = weights
    (
        residual,
        middle,
        normed,
        queries,
        key_rows,
        value_rows,
        log_total,
        mixed_rows,
        normed_two_rows,
        router,
        gate_values,
        places,
        picked,
        routed,
        hidden,
        active,
        flat_result,
    ) = stored
    own_rows, widths = residual.shape
    group_rows = named_expert.shape[0]
    head_cols = qkv_weight.shape[2]
    local_experts = in_weight.shape[0]
    expert_count = router.shape[1]
    q_scale = HEAD ** (-0.5)
    flat_qkv = joined_qkv(qkv_weight)
    grad_moe = lax.all_gather(
        grad_rows.astype(jnp.bfloat16), ("heads", "tensor"), axis=0, tiled=True
    )
    back_rows = with_zero_row(grad_moe)[picked // 2].astype(jnp.float32)
    gate_slots = with_zero_row(gate_values.reshape(-1))[picked]
    gate_grad_slots = jnp.sum(back_rows * flat_result[:-1], axis=1)
    gate_grads = with_zero_row(gate_grad_slots)[places]
    expert_range = jnp.arange(expert_count, dtype=jnp.int32)
    router_part = jnp.sum(
        gate_grads[:, :, None]
        * (named_expert[:, :, None] == expert_range[None, None, :]).astype(jnp.float32),
        axis=1,
    )
    grad_result = (
        (gate_slots[:, None] * back_rows).astype(jnp.bfloat16).reshape(local_experts, CAP, widths)
    )
    grad_active = jnp.einsum(
        "ecd,efd->ecf", grad_result, back_weight, preferred_element_type=jnp.float32
    )
    gelu_value, gelu_pull = jax.vjp(gelu_exact, hidden)
    grad_hidden = gelu_pull(grad_active)[0].astype(jnp.bfloat16)
    back_grad = jnp.einsum("ecf,ecd->efd", active, grad_result, preferred_element_type=jnp.float32)
    in_grad = jnp.einsum("ecd,ecf->edf", routed, grad_hidden, preferred_element_type=jnp.float32)
    grad_routed = jnp.einsum(
        "ecf,edf->ecd", grad_hidden, in_weight, preferred_element_type=jnp.float32
    )
    grad_routed = with_zero_row(grad_routed.reshape(local_experts * CAP, widths))
    token_part = grad_routed[places[:, 0]] + grad_routed[places[:, 1]]
    grad_normed_two, router_rows = (
        lax.psum_scatter(token_part, ("heads", "tensor"), scatter_dimension=0, tiled=True),
        lax.psum_scatter(router_part, ("heads", "tensor"), scatter_dimension=0, tiled=True),
    )
    router_own = lax.dynamic_slice_in_dim(router, row_start, own_rows, 0)
    grad_logits = (
        router_own * (router_rows - jnp.sum(router_own * router_rows, axis=-1, keepdims=True))
    ).astype(jnp.bfloat16)
    router_grad = jnp.einsum(
        "td,te->de", normed_two_rows, grad_logits, preferred_element_type=jnp.float32
    )
    grad_normed_two = grad_normed_two + jnp.einsum(
        "te,de->td", grad_logits, router_weight, preferred_element_type=jnp.float32
    )
    norm_value, norm_pull = jax.vjp(layer_norm, middle, ln_gains[1], ln_shift[1])
    grad_middle, gain_two, shift_two = norm_pull(grad_normed_two)
    grad_middle = grad_middle + grad_rows
    grad_attn = lax.all_gather(
        grad_middle.astype(jnp.bfloat16), ("heads", "tensor"), axis=0, tiled=True
    )
    out_grad = jnp.einsum("tc,td->cd", mixed_rows, grad_attn, preferred_element_type=jnp.float32)
    grad_mixed = jnp.einsum("td,cd->tc", grad_attn, out_weight, preferred_element_type=jnp.float32)
    grad_mixed = grad_mixed.astype(jnp.bfloat16).reshape(queries.shape)
    scores = jnp.einsum("bqhd,bkhd->bhqk", queries, key_rows, preferred_element_type=jnp.float32)
    attn_probs = jnp.exp(scores - log_total[..., None])
    grad_values = jnp.einsum(
        "bhqk,bqhd->bkhd",
        attn_probs.astype(jnp.bfloat16),
        grad_mixed,
        preferred_element_type=jnp.float32,
    )
    grad_probs = jnp.einsum(
        "bqhd,bkhd->bhqk", grad_mixed, value_rows, preferred_element_type=jnp.float32
    )
    grad_scores = (
        attn_probs * (grad_probs - jnp.sum(attn_probs * grad_probs, axis=-1, keepdims=True))
    ).astype(jnp.bfloat16)
    grad_queries = jnp.einsum(
        "bhqk,bkhd->bqhd", grad_scores, key_rows, preferred_element_type=jnp.float32
    )
    grad_keys = jnp.einsum(
        "bhqk,bqhd->bkhd", grad_scores, queries, preferred_element_type=jnp.float32
    )
    grad_projected = jnp.concatenate(
        [
            grad_queries.reshape(group_rows, head_cols),
            grad_keys.reshape(group_rows, head_cols),
            grad_values.reshape(group_rows, head_cols),
        ],
        axis=1,
    ).astype(jnp.bfloat16)
    qkv_flat_grad = jnp.einsum(
        "td,tc->dc", normed, grad_projected, preferred_element_type=jnp.float32
    )
    column_scale = jnp.concatenate(
        [jnp.full((head_cols,), q_scale, jnp.float32), jnp.ones((2 * head_cols,), jnp.float32)]
    )
    qkv_grad = jnp.transpose(
        (qkv_flat_grad * column_scale).reshape(widths, 3, head_cols), (1, 0, 2)
    )
    query_term = (
        jnp.einsum(
            "tc,dc->td",
            grad_projected[:, :head_cols],
            flat_qkv[:, :head_cols],
            preferred_element_type=jnp.float32,
        )
        * q_scale
    )
    grad_normed = lax.psum_scatter(
        query_term
        + jnp.einsum(
            "tc,dc->td",
            grad_projected[:, head_cols:],
            flat_qkv[:, head_cols:],
            preferred_element_type=jnp.float32,
        ),
        ("heads", "tensor"),
        scatter_dimension=0,
        tiled=True,
    )
    first_value, first_pull = jax.vjp(layer_norm, residual, ln_gains[0], ln_shift[0])
    grad_input, gain_one, shift_one = first_pull(grad_normed)
    grad_input = grad_input + grad_middle
    matrix_grads = (qkv_grad, out_grad, in_grad, back_grad)
    small_grads = (jnp.stack([gain_one, gain_two]), jnp.stack([shift_one, shift_two]), router_grad)
    return (grad_input, matrix_grads, small_grads)


def on_device(
    tokens,
    cotangent,
    image_counts,
    w_qkv,
    w_out,
    ln_gain,
    ln_bias,
    w_router,
    w_in,
    w_back,
    expert_ids,
    slots,
):
    own_rows = tokens.shape[0]
    row_start = lax.axis_index(("heads", "tensor")) * own_rows
    first_expert = lax.axis_index("heads") * w_in.shape[1]
    residual = tokens.astype(jnp.float32)
    head_list = []
    block_index = 0
    weights = (
        lax.all_gather(w_qkv[block_index], "fsdp", axis=1, tiled=True),
        lax.all_gather(w_out[block_index], "fsdp", axis=1, tiled=True),
        lax.all_gather(w_in[block_index], "fsdp", axis=1, tiled=True),
        lax.all_gather(w_back[block_index], "fsdp", axis=2, tiled=True),
    )
    residual, stored, head_full = forward_block(
        residual,
        weights,
        ln_gain[block_index],
        ln_bias[block_index],
        w_router[block_index],
        expert_ids[block_index],
        slots[block_index],
        first_expert,
    )
    stored_list = [stored]
    head_list.append(head_full)
    image_index = (row_start + jnp.arange(own_rows, dtype=jnp.int32)) // SEQ
    live_rows = (image_index < image_counts[0]).astype(jnp.float32)
    grad_rows = cotangent.astype(jnp.float32) * live_rows[:, None]
    matrix_list = [None] * LAYERS
    small_list = [None] * LAYERS
    for block_index in reversed(range(LAYERS)):
        weights = (
            lax.all_gather(w_qkv[block_index], "fsdp", axis=1, tiled=True),
            lax.all_gather(w_out[block_index], "fsdp", axis=1, tiled=True),
            lax.all_gather(w_in[block_index], "fsdp", axis=1, tiled=True),
            lax.all_gather(w_back[block_index], "fsdp", axis=2, tiled=True),
        )
        grad_rows, matrix_grads, small_grads = backward_block(
            grad_rows,
            stored_list[block_index],
            weights,
            ln_gain[block_index],
            ln_bias[block_index],
            w_router[block_index],
            expert_ids[block_index],
            row_start,
        )
        matrix_list[block_index] = (
            lax.psum_scatter(matrix_grads[0], "fsdp", scatter_dimension=1, tiled=True),
            lax.psum_scatter(matrix_grads[1], "fsdp", scatter_dimension=1, tiled=True),
            lax.psum_scatter(matrix_grads[2], "fsdp", scatter_dimension=1, tiled=True),
            lax.psum_scatter(matrix_grads[3], "fsdp", scatter_dimension=2, tiled=True),
        )
        small_list[block_index] = small_grads
    gain_grads, shift_grads, router_grads = lax.psum(
        (
            jnp.stack([entry[0] for entry in small_list]),
            jnp.stack([entry[1] for entry in small_list]),
            jnp.stack([entry[2] for entry in small_list]),
        ),
        ("fsdp", "heads", "tensor"),
    )
    qkv_grads = jnp.stack([entry[0] for entry in matrix_list])
    out_grads = jnp.stack([entry[1] for entry in matrix_list])
    in_grads = jnp.stack([entry[2] for entry in matrix_list])
    back_grads = jnp.stack([entry[3] for entry in matrix_list])
    return (
        residual.astype(jnp.bfloat16),
        grad_rows,
        qkv_grads,
        out_grads,
        gain_grads,
        shift_grads,
        router_grads,
        in_grads,
        back_grads,
    )

def fast_device(
    tokens,
    cotangent,
    image_counts,
    w_qkv,
    w_out,
    ln_gain,
    ln_bias,
    w_router,
    w_in,
    w_back,
    expert_ids,
    slots,
):
    group_axes = ("heads", "tensor")
    own_rows, widths = tokens.shape
    images = own_rows // SEQ
    own_group = lax.axis_size("fsdp")
    cores = lax.axis_size("tensor")
    core = lax.axis_index("tensor")
    heads_index = lax.axis_index("heads")
    local_experts = w_in.shape[1]
    my_expert = heads_index * local_experts + lax.axis_index("fsdp") * cores + core
    row_start = lax.axis_index(group_axes) * own_rows
    q_scale = HEAD ** (-0.5)
    f32, bf16 = jnp.float32, jnp.bfloat16

    qkv_full = lax.all_gather(w_qkv[0], "fsdp", axis=1, tiled=True)
    qkv_full = lax.all_gather(qkv_full, group_axes, axis=2, tiled=True)
    out_full = lax.all_gather(w_out[0], "fsdp", axis=1, tiled=True)
    out_full = lax.all_gather(out_full, group_axes, axis=0, tiled=True)
    flat_qkv = joined_qkv(qkv_full)

    def to_expert(weight):
        return lax.all_to_all(weight, ("fsdp", "tensor"), 0, 0, tiled=True)

    def from_expert(blocks):
        return lax.all_to_all(blocks, ("fsdp", "tensor"), 0, 0, tiled=True)

    depth, width = w_in.shape[2], w_in.shape[3]
    in_blocks = to_expert(w_in[0]).reshape(own_group, cores, depth, width)
    in_full = jnp.transpose(in_blocks, (0, 2, 1, 3)).reshape(own_group * depth, cores * width)
    back_blocks = to_expert(w_back[0]).reshape(own_group, cores, width, depth)
    back_full = jnp.transpose(back_blocks, (1, 2, 0, 3)).reshape(cores * width, own_group * depth)

    image_index = (row_start + jnp.arange(own_rows, dtype=jnp.int32)) // SEQ
    live_rows = (image_index < image_counts[0]).astype(f32)
    grad_rows = cotangent.astype(f32) * live_rows[:, None]
    grad_all = lax.all_gather(grad_rows.astype(bf16), group_axes, axis=0, tiled=True)

    relative = expert_ids[0] - heads_index * local_experts
    wanted = (
        (slots[0] >= 0) & (relative >= 0) & (relative < local_experts) & (relative % cores == core)
    )
    places = jnp.where(wanted, (relative // cores) * CAP + slots[0], -1)
    slot_range = jnp.arange(own_group * CAP, dtype=jnp.int32)[None, :]
    chosen = (
        (places[:, 0:1] == slot_range) | (places[:, 1:2] == slot_range)
    ).astype(bf16)

    def dispatch(rows):
        picked = jnp.einsum("ts,td->sd", chosen, rows, preferred_element_type=f32).astype(bf16)
        return lax.all_to_all(picked, "fsdp", 0, 0, tiled=True)

    def combine(rows):
        back = lax.all_to_all(rows, "fsdp", 0, 0, tiled=True)
        part = jnp.einsum("ts,sd->td", chosen, back, preferred_element_type=f32).astype(bf16)
        return lax.psum_scatter(part, group_axes, scatter_dimension=0, tiled=True).astype(f32)

    routed_grad = dispatch(grad_all)

    residual = tokens.astype(f32)
    head_shape = (images, SEQ, widths // HEAD, HEAD)
    normed = layer_norm(residual, ln_gain[0, 0], ln_bias[0, 0]).astype(bf16)
    projected = jnp.dot(normed, flat_qkv, preferred_element_type=f32)
    queries = (projected[:, :widths] * q_scale).astype(bf16).reshape(head_shape)
    key_rows = projected[:, widths : 2 * widths].astype(bf16).reshape(head_shape)
    value_rows = projected[:, 2 * widths :].astype(bf16).reshape(head_shape)
    scores = jnp.einsum("bqhd,bkhd->bhqk", queries, key_rows, preferred_element_type=f32)
    attn_probs = jax.nn.softmax(scores, axis=-1)
    probs_low = attn_probs.astype(bf16)
    mixed_rows = jnp.einsum("bhqk,bkhd->bqhd", probs_low, value_rows, preferred_element_type=f32)
    mixed_rows = mixed_rows.reshape(own_rows, widths).astype(bf16)
    middle = residual + jnp.dot(mixed_rows, out_full, preferred_element_type=f32)
    normed_two = layer_norm(middle, ln_gain[0, 1], ln_bias[0, 1]).astype(bf16)

    routed = dispatch(lax.all_gather(normed_two, group_axes, axis=0, tiled=True))

    router = jax.nn.softmax(jnp.dot(routed, w_router[0], preferred_element_type=f32), axis=-1)
    mine = (jnp.arange(router.shape[1], dtype=jnp.int32) == my_expert).astype(f32)[None, :]
    gates = jnp.sum(router * mine, axis=1, keepdims=True)
    hidden = jnp.dot(routed, in_full, preferred_element_type=f32)
    gelu_value, gelu_pull = jax.vjp(gelu_exact, hidden)
    active = gelu_value.astype(bf16)
    result = jnp.dot(active, back_full, preferred_element_type=f32)
    gate_grads = jnp.sum(routed_grad.astype(f32) * result, axis=1, keepdims=True)
    grad_result = (gates * routed_grad.astype(f32)).astype(bf16)
    grad_active = jnp.einsum("cd,fd->cf", grad_result, back_full, preferred_element_type=f32)
    grad_hidden = gelu_pull(grad_active)[0].astype(bf16)
    grad_logits = (gate_grads * gates * (mine - router)).astype(bf16)
    grad_routed = jnp.einsum("cf,df->cd", grad_hidden, in_full, preferred_element_type=f32)
    grad_routed += jnp.einsum("ce,de->cd", grad_logits, w_router[0], preferred_element_type=f32)
    grad_normed_two = combine(grad_routed.astype(bf16))
    block_out = middle + combine((gates * result).astype(bf16))

    back_grad = jnp.einsum("cf,cd->fd", active, grad_result, preferred_element_type=f32).astype(bf16)
    in_grad = jnp.einsum("cd,cf->df", routed, grad_hidden, preferred_element_type=f32).astype(bf16)
    router_grad = jnp.einsum("cd,ce->de", routed, grad_logits, preferred_element_type=f32)
    in_parts = jnp.transpose(in_grad.reshape(own_group, depth, cores, width), (0, 2, 1, 3))
    in_grads = from_expert(in_parts.reshape(w_in.shape[1:])).astype(f32)
    back_parts = jnp.transpose(back_grad.reshape(cores, width, own_group, depth), (2, 0, 1, 3))
    back_grads = from_expert(back_parts.reshape(w_back.shape[1:])).astype(f32)

    norm_value, norm_pull = jax.vjp(layer_norm, middle, ln_gain[0, 1], ln_bias[0, 1])
    grad_middle, gain_two, shift_two = norm_pull(grad_normed_two)
    grad_middle = grad_middle + grad_rows
    grad_attn = grad_middle.astype(bf16)
    out_grad = jnp.einsum("tc,td->cd", mixed_rows, grad_attn, preferred_element_type=f32)
    grad_mixed = jnp.einsum("td,cd->tc", grad_attn, out_full, preferred_element_type=f32)
    grad_mixed = grad_mixed.astype(bf16).reshape(head_shape)
    grad_values = jnp.einsum("bhqk,bqhd->bkhd", probs_low, grad_mixed, preferred_element_type=f32)
    grad_probs = jnp.einsum("bqhd,bkhd->bhqk", grad_mixed, value_rows, preferred_element_type=f32)
    grad_scores = (
        attn_probs * (grad_probs - jnp.sum(attn_probs * grad_probs, axis=-1, keepdims=True))
    ).astype(bf16)
    grad_queries = jnp.einsum("bhqk,bkhd->bqhd", grad_scores, key_rows, preferred_element_type=f32)
    grad_keys = jnp.einsum("bhqk,bqhd->bkhd", grad_scores, queries, preferred_element_type=f32)
    grad_projected = jnp.concatenate(
        [
            grad_queries.reshape(own_rows, widths) * q_scale,
            grad_keys.reshape(own_rows, widths),
            grad_values.reshape(own_rows, widths),
        ],
        axis=1,
    ).astype(bf16)
    qkv_grad = jnp.einsum("td,tc->dc", normed, grad_projected, preferred_element_type=f32)
    qkv_grad = jnp.transpose(qkv_grad.reshape(widths, 3, widths), (1, 0, 2))
    grad_normed = jnp.einsum("tc,dc->td", grad_projected, flat_qkv, preferred_element_type=f32)
    first_value, first_pull = jax.vjp(layer_norm, residual, ln_gain[0, 0], ln_bias[0, 0])
    grad_input, gain_one, shift_one = first_pull(grad_normed)
    grad_input = grad_input + grad_middle

    qkv_grads = lax.psum_scatter(
        qkv_grad.astype(bf16), group_axes, scatter_dimension=2, tiled=True
    )
    qkv_grads = lax.psum_scatter(qkv_grads, "fsdp", scatter_dimension=1, tiled=True)
    out_grads = lax.psum_scatter(
        out_grad.astype(bf16), group_axes, scatter_dimension=0, tiled=True
    )
    out_grads = lax.psum_scatter(out_grads, "fsdp", scatter_dimension=1, tiled=True)
    gain_grads, shift_grads, router_grads = lax.psum(
        (
            jnp.stack([gain_one, gain_two])[None],
            jnp.stack([shift_one, shift_two])[None],
            router_grad[None],
        ),
        ("fsdp", "heads", "tensor"),
    )
    return (
        block_out.astype(bf16),
        grad_input,
        qkv_grads.astype(f32)[None],
        out_grads.astype(f32)[None],
        gain_grads,
        shift_grads,
        router_grads,
        in_grads[None],
        back_grads[None],
    )


def solution(mesh):
    def program(*arrays):
        sizes = dict(mesh.shape)
        planes = sizes["fsdp"] * sizes["tensor"]
        own_rows = arrays[0].shape[0] // (planes * sizes["heads"])
        experts = arrays[8].shape[1] // sizes["heads"]
        own_expert = experts == planes and own_rows % SEQ == 0
        return placed(mesh, fast_device if own_expert else on_device)(*arrays)

    return program


def placed(mesh, on_device):
    return jax.shard_map(
        on_device,
        mesh=mesh,
        in_specs=(
            P(("fsdp", "heads", "tensor"), None),
            P(("fsdp", "heads", "tensor"), None),
            P("fsdp"),
            P(None, None, "fsdp", ("heads", "tensor")),
            P(None, ("heads", "tensor"), "fsdp"),
            P(),
            P(),
            P(),
            P(None, "heads", "fsdp", "tensor"),
            P(None, "heads", "tensor", "fsdp"),
            P(None, "fsdp", None),
            P(None, "fsdp", None),
        ),
        out_specs=(
            P(("fsdp", "heads", "tensor"), None),
            P(("fsdp", "heads", "tensor"), None),
            P(None, None, "fsdp", ("heads", "tensor")),
            P(None, ("heads", "tensor"), "fsdp"),
            P(),
            P(),
            P(),
            P(None, "heads", "fsdp", "tensor"),
            P(None, "heads", "tensor", "fsdp"),
        ),
        check_vma=False,
    )
```

```python
import jax
import jax.numpy as jnp
from jax import lax
from jax.experimental import pallas as pl
from jax.experimental.pallas import tpu as pltpu
from jax.sharding import PartitionSpec as P

HEAD = 64
SEQ = 197
LAYERS = 1
CAP = 256


def layer_norm(value, ln_gains, ln_shift):
    centred = value - jnp.mean(value, axis=-1, keepdims=True)
    spread = jnp.mean(centred * centred, axis=-1, keepdims=True)
    return centred * lax.rsqrt(spread + 1e-06) * ln_gains + ln_shift


def gelu_exact(value):
    return jax.nn.gelu(value, approximate=False)


def with_zero_row(matrix):
    return jnp.concatenate([matrix, jnp.zeros((1,) + matrix.shape[1:], matrix.dtype)], axis=0)


def slot_tables(named_expert, slot_rows, first_expert, local_experts):
    group_rows = named_expert.shape[0]
    is_local = (
        (slot_rows >= 0)
        & (named_expert >= first_expert)
        & (named_expert < first_expert + local_experts)
    )
    places = jnp.where(
        is_local, (named_expert - first_expert) * CAP + slot_rows, local_experts * CAP
    )
    picked = jnp.full((local_experts * CAP + 1,), 2 * group_rows, jnp.int32)
    picked = picked.at[places.reshape(-1)].set(jnp.arange(2 * group_rows, dtype=jnp.int32))
    return (places, picked[: local_experts * CAP])


def joined_qkv(qkv_weight):
    head_cols = qkv_weight.shape[2]
    return jnp.transpose(qkv_weight, (1, 0, 2)).reshape(qkv_weight.shape[1], 3 * head_cols)


def forward_block(
    residual, weights, ln_gains, ln_shift, router_weight, named_expert, slot_rows, first_expert
):
    qkv_weight, out_weight, in_weight, back_weight = weights
    own_rows, widths = residual.shape
    group_rows = named_expert.shape[0]
    head_cols = qkv_weight.shape[2]
    local_experts = in_weight.shape[0]
    head_shape = (group_rows // SEQ, SEQ, head_cols // HEAD, HEAD)
    q_scale = HEAD ** (-0.5)
    flat_qkv = joined_qkv(qkv_weight)
    normed_rows = layer_norm(residual, ln_gains[0], ln_shift[0]).astype(jnp.bfloat16)
    normed = lax.all_gather(normed_rows, ("heads", "tensor"), axis=0, tiled=True)
    projected = jnp.dot(normed, flat_qkv, preferred_element_type=jnp.float32)
    queries = (projected[:, :head_cols] * q_scale).astype(jnp.bfloat16).reshape(head_shape)
    key_rows = projected[:, head_cols : 2 * head_cols].astype(jnp.bfloat16).reshape(head_shape)
    value_rows = projected[:, 2 * head_cols :].astype(jnp.bfloat16).reshape(head_shape)
    scores = jnp.einsum("bqhd,bkhd->bhqk", queries, key_rows, preferred_element_type=jnp.float32)
    log_total = jax.nn.logsumexp(scores, axis=-1)
    attn_probs = jax.nn.softmax(scores, axis=-1).astype(jnp.bfloat16)
    mixed_rows = jnp.einsum(
        "bhqk,bkhd->bqhd", attn_probs, value_rows, preferred_element_type=jnp.float32
    )
    mixed_rows = mixed_rows.reshape(group_rows, head_cols).astype(jnp.bfloat16)
    middle = residual + lax.psum_scatter(
        jnp.dot(mixed_rows, out_weight, preferred_element_type=jnp.float32),
        ("heads", "tensor"),
        scatter_dimension=0,
        tiled=True,
    )
    head_full = ()
    normed_two_rows = layer_norm(middle, ln_gains[1], ln_shift[1]).astype(jnp.bfloat16)
    normed_two = lax.all_gather(normed_two_rows, ("heads", "tensor"), axis=0, tiled=True)
    router = jax.nn.softmax(
        jnp.dot(normed_two, router_weight, preferred_element_type=jnp.float32), axis=-1
    )
    gate_values = jnp.take_along_axis(router, named_expert, axis=1) * (slot_rows >= 0)
    places, picked = slot_tables(named_expert, slot_rows, first_expert, local_experts)
    routed = with_zero_row(normed_two)[picked // 2].reshape(local_experts, CAP, widths)
    hidden = jnp.einsum("ecd,edf->ecf", routed, in_weight, preferred_element_type=jnp.float32)
    active = gelu_exact(hidden).astype(jnp.bfloat16)
    result = jnp.einsum("ecf,efd->ecd", active, back_weight, preferred_element_type=jnp.float32)
    flat_result = with_zero_row(result.reshape(local_experts * CAP, widths))
    block_out = middle + lax.psum_scatter(
        (
            flat_result[places[:, 0]] * gate_values[:, 0:1]
            + flat_result[places[:, 1]] * gate_values[:, 1:2]
        ).astype(jnp.bfloat16),
        ("heads", "tensor"),
        scatter_dimension=0,
        tiled=True,
    ).astype(jnp.float32)
    stored = (
        residual,
        middle,
        normed,
        queries,
        key_rows,
        value_rows,
        log_total,
        mixed_rows,
        normed_two_rows,
        router,
        gate_values,
        places,
        picked,
        routed,
        hidden,
        active,
        flat_result,
    )
    return (block_out, stored, head_full)


def backward_block(
    grad_rows, stored, weights, ln_gains, ln_shift, router_weight, named_expert, row_start
):
    qkv_weight, out_weight, in_weight, back_weight = weights
    (
        residual,
        middle,
        normed,
        queries,
        key_rows,
        value_rows,
        log_total,
        mixed_rows,
        normed_two_rows,
        router,
        gate_values,
        places,
        picked,
        routed,
        hidden,
        active,
        flat_result,
    ) = stored
    own_rows, widths = residual.shape
    group_rows = named_expert.shape[0]
    head_cols = qkv_weight.shape[2]
    local_experts = in_weight.shape[0]
    expert_count = router.shape[1]
    q_scale = HEAD ** (-0.5)
    flat_qkv = joined_qkv(qkv_weight)
    grad_moe = lax.all_gather(
        grad_rows.astype(jnp.bfloat16), ("heads", "tensor"), axis=0, tiled=True
    )
    back_rows = with_zero_row(grad_moe)[picked // 2].astype(jnp.float32)
    gate_slots = with_zero_row(gate_values.reshape(-1))[picked]
    gate_grad_slots = jnp.sum(back_rows * flat_result[:-1], axis=1)
    gate_grads = with_zero_row(gate_grad_slots)[places]
    expert_range = jnp.arange(expert_count, dtype=jnp.int32)
    router_part = jnp.sum(
        gate_grads[:, :, None]
        * (named_expert[:, :, None] == expert_range[None, None, :]).astype(jnp.float32),
        axis=1,
    )
    grad_result = (
        (gate_slots[:, None] * back_rows).astype(jnp.bfloat16).reshape(local_experts, CAP, widths)
    )
    grad_active = jnp.einsum(
        "ecd,efd->ecf", grad_result, back_weight, preferred_element_type=jnp.float32
    )
    gelu_value, gelu_pull = jax.vjp(gelu_exact, hidden)
    grad_hidden = gelu_pull(grad_active)[0].astype(jnp.bfloat16)
    back_grad = jnp.einsum("ecf,ecd->efd", active, grad_result, preferred_element_type=jnp.float32)
    in_grad = jnp.einsum("ecd,ecf->edf", routed, grad_hidden, preferred_element_type=jnp.float32)
    grad_routed = jnp.einsum(
        "ecf,edf->ecd", grad_hidden, in_weight, preferred_element_type=jnp.float32
    )
    grad_routed = with_zero_row(grad_routed.reshape(local_experts * CAP, widths))
    token_part = grad_routed[places[:, 0]] + grad_routed[places[:, 1]]
    grad_normed_two, router_rows = (
        lax.psum_scatter(token_part, ("heads", "tensor"), scatter_dimension=0, tiled=True),
        lax.psum_scatter(router_part, ("heads", "tensor"), scatter_dimension=0, tiled=True),
    )
    router_own = lax.dynamic_slice_in_dim(router, row_start, own_rows, 0)
    grad_logits = (
        router_own * (router_rows - jnp.sum(router_own * router_rows, axis=-1, keepdims=True))
    ).astype(jnp.bfloat16)
    router_grad = jnp.einsum(
        "td,te->de", normed_two_rows, grad_logits, preferred_element_type=jnp.float32
    )
    grad_normed_two = grad_normed_two + jnp.einsum(
        "te,de->td", grad_logits, router_weight, preferred_element_type=jnp.float32
    )
    norm_value, norm_pull = jax.vjp(layer_norm, middle, ln_gains[1], ln_shift[1])
    grad_middle, gain_two, shift_two = norm_pull(grad_normed_two)
    grad_middle = grad_middle + grad_rows
    grad_attn = lax.all_gather(
        grad_middle.astype(jnp.bfloat16), ("heads", "tensor"), axis=0, tiled=True
    )
    out_grad = jnp.einsum("tc,td->cd", mixed_rows, grad_attn, preferred_element_type=jnp.float32)
    grad_mixed = jnp.einsum("td,cd->tc", grad_attn, out_weight, preferred_element_type=jnp.float32)
    grad_mixed = grad_mixed.astype(jnp.bfloat16).reshape(queries.shape)
    scores = jnp.einsum("bqhd,bkhd->bhqk", queries, key_rows, preferred_element_type=jnp.float32)
    attn_probs = jnp.exp(scores - log_total[..., None])
    grad_values = jnp.einsum(
        "bhqk,bqhd->bkhd",
        attn_probs.astype(jnp.bfloat16),
        grad_mixed,
        preferred_element_type=jnp.float32,
    )
    grad_probs = jnp.einsum(
        "bqhd,bkhd->bhqk", grad_mixed, value_rows, preferred_element_type=jnp.float32
    )
    grad_scores = (
        attn_probs * (grad_probs - jnp.sum(attn_probs * grad_probs, axis=-1, keepdims=True))
    ).astype(jnp.bfloat16)
    grad_queries = jnp.einsum(
        "bhqk,bkhd->bqhd", grad_scores, key_rows, preferred_element_type=jnp.float32
    )
    grad_keys = jnp.einsum(
        "bhqk,bqhd->bkhd", grad_scores, queries, preferred_element_type=jnp.float32
    )
    grad_projected = jnp.concatenate(
        [
            grad_queries.reshape(group_rows, head_cols),
            grad_keys.reshape(group_rows, head_cols),
            grad_values.reshape(group_rows, head_cols),
        ],
        axis=1,
    ).astype(jnp.bfloat16)
    qkv_flat_grad = jnp.einsum(
        "td,tc->dc", normed, grad_projected, preferred_element_type=jnp.float32
    )
    column_scale = jnp.concatenate(
        [jnp.full((head_cols,), q_scale, jnp.float32), jnp.ones((2 * head_cols,), jnp.float32)]
    )
    qkv_grad = jnp.transpose(
        (qkv_flat_grad * column_scale).reshape(widths, 3, head_cols), (1, 0, 2)
    )
    query_term = (
        jnp.einsum(
            "tc,dc->td",
            grad_projected[:, :head_cols],
            flat_qkv[:, :head_cols],
            preferred_element_type=jnp.float32,
        )
        * q_scale
    )
    grad_normed = lax.psum_scatter(
        query_term
        + jnp.einsum(
            "tc,dc->td",
            grad_projected[:, head_cols:],
            flat_qkv[:, head_cols:],
            preferred_element_type=jnp.float32,
        ),
        ("heads", "tensor"),
        scatter_dimension=0,
        tiled=True,
    )
    first_value, first_pull = jax.vjp(layer_norm, residual, ln_gains[0], ln_shift[0])
    grad_input, gain_one, shift_one = first_pull(grad_normed)
    grad_input = grad_input + grad_middle
    matrix_grads = (qkv_grad, out_grad, in_grad, back_grad)
    small_grads = (jnp.stack([gain_one, gain_two]), jnp.stack([shift_one, shift_two]), router_grad)
    return (grad_input, matrix_grads, small_grads)


def on_device(
    tokens,
    cotangent,
    image_counts,
    w_qkv,
    w_out,
    ln_gain,
    ln_bias,
    w_router,
    w_in,
    w_back,
    expert_ids,
    slots,
):
    own_rows = tokens.shape[0]
    row_start = lax.axis_index(("heads", "tensor")) * own_rows
    first_expert = lax.axis_index("heads") * w_in.shape[1]
    residual = tokens.astype(jnp.float32)
    head_list = []
    block_index = 0
    weights = (
        lax.all_gather(w_qkv[block_index], "fsdp", axis=1, tiled=True),
        lax.all_gather(w_out[block_index], "fsdp", axis=1, tiled=True),
        lax.all_gather(w_in[block_index], "fsdp", axis=1, tiled=True),
        lax.all_gather(w_back[block_index], "fsdp", axis=2, tiled=True),
    )
    residual, stored, head_full = forward_block(
        residual,
        weights,
        ln_gain[block_index],
        ln_bias[block_index],
        w_router[block_index],
        expert_ids[block_index],
        slots[block_index],
        first_expert,
    )
    stored_list = [stored]
    head_list.append(head_full)
    image_index = (row_start + jnp.arange(own_rows, dtype=jnp.int32)) // SEQ
    live_rows = (image_index < image_counts[0]).astype(jnp.float32)
    grad_rows = cotangent.astype(jnp.float32) * live_rows[:, None]
    matrix_list = [None] * LAYERS
    small_list = [None] * LAYERS
    for block_index in reversed(range(LAYERS)):
        weights = (
            lax.all_gather(w_qkv[block_index], "fsdp", axis=1, tiled=True),
            lax.all_gather(w_out[block_index], "fsdp", axis=1, tiled=True),
            lax.all_gather(w_in[block_index], "fsdp", axis=1, tiled=True),
            lax.all_gather(w_back[block_index], "fsdp", axis=2, tiled=True),
        )
        grad_rows, matrix_grads, small_grads = backward_block(
            grad_rows,
            stored_list[block_index],
            weights,
            ln_gain[block_index],
            ln_bias[block_index],
            w_router[block_index],
            expert_ids[block_index],
            row_start,
        )
        matrix_list[block_index] = (
            lax.psum_scatter(matrix_grads[0], "fsdp", scatter_dimension=1, tiled=True),
            lax.psum_scatter(matrix_grads[1], "fsdp", scatter_dimension=1, tiled=True),
            lax.psum_scatter(matrix_grads[2], "fsdp", scatter_dimension=1, tiled=True),
            lax.psum_scatter(matrix_grads[3], "fsdp", scatter_dimension=2, tiled=True),
        )
        small_list[block_index] = small_grads
    gain_grads, shift_grads, router_grads = lax.psum(
        (
            jnp.stack([entry[0] for entry in small_list]),
            jnp.stack([entry[1] for entry in small_list]),
            jnp.stack([entry[2] for entry in small_list]),
        ),
        ("fsdp", "heads", "tensor"),
    )
    qkv_grads = jnp.stack([entry[0] for entry in matrix_list])
    out_grads = jnp.stack([entry[1] for entry in matrix_list])
    in_grads = jnp.stack([entry[2] for entry in matrix_list])
    back_grads = jnp.stack([entry[3] for entry in matrix_list])
    return (
        residual.astype(jnp.bfloat16),
        grad_rows,
        qkv_grads,
        out_grads,
        gain_grads,
        shift_grads,
        router_grads,
        in_grads,
        back_grads,
    )


ROWS = -(-SEQ // 16) * 16
MESH = pl.DeviceIdType.MESH
F32, BF16 = jnp.float32, jnp.bfloat16
NN, NT, TN = (((1,), (0,)), ((), ())), (((1,), (1,)), ((), ())), (((0,), (0,)), ((), ()))


def mm(left, right, dims=NN):
    return lax.dot_general(left, right, dims, preferred_element_type=F32)


def whole(index, size):
    return pl.ds(pl.multiple_of(index * size, size), size)


def normal_parts(value):
    centred = value - jnp.mean(value, axis=-1, keepdims=True)
    scale = lax.rsqrt(jnp.mean(centred * centred, axis=-1, keepdims=True) + 1e-06)
    return centred * scale, scale


def normal_pull(grad, unit, scale, gains):
    grad_unit = grad * gains
    mean_grad = jnp.mean(grad_unit, axis=-1, keepdims=True)
    mean_both = jnp.mean(grad_unit * unit, axis=-1, keepdims=True)
    return scale * (grad_unit - mean_grad - unit * mean_both)


def gelu_parts(value):
    size = jnp.abs(value)
    step = 1.0 / (1.0 + 0.3275911 * 2.0**-0.5 * size)
    bell = jnp.exp(-0.5 * (value * value))
    series = 1.061405429 * step - 1.453152027
    series = series * step + 1.421413741
    series = series * step - 0.284496736
    series = series * step + 0.254829592
    tail = 0.5 * series * step * bell
    share = jnp.where(value < 0, tail, 1.0 - tail)
    return value * share, share + value * (bell * 0.3989422804014327)


class Exchange:
    def __init__(self, source, target, device, landing, send, recv):
        self.out = pltpu.make_async_remote_copy(
            source, target, send, recv, device_id=device, device_id_type=MESH
        )
        self.into = pltpu.make_async_remote_copy(
            landing, landing, send, recv, device_id=device, device_id_type=MESH
        )

    def start(self):
        self.out.start()
        return self

    def arrived(self):
        self.into.wait_recv()

    def sent(self):
        self.out.wait_send()


def block_kernel(depth_z, images, local_count, refs):
    H = depth_z
    (
        tokens, cot, counts, wq, wo, gain, bias, wr, win_hbm, wback_hbm, prow,
        out, tgrad, wqg, wog, lng, lnb, wrg, gin_out, gback_out,
        stage, wbuf, win, wback, rows_grad, rows_norm, big, wide,
        xsend, gsend, xrows, grows, xback, gback,
        normed, qkv, probs, mixed, middle, grad_mid, logit_grad,
        sib_out, sib_in, z_out, z_in, own_sum,
        att_in, plane_in, line_out, line_in,
        small_c, small_p, small_z, route_c, route_p, route_z,
        send_sems, recv_sems, local_sems,
    ) = refs
    own = images * ROWS
    width = tokens.shape[1]
    half = width // 128
    f, h, t = (lax.axis_index(name) for name in ("fsdp", "heads", "tensor"))
    s = 1 - t
    fx = [f, f + 1 - 2 * lax.rem(f, 2), lax.rem(f + 2, 4), 3 - f]
    hz = [lax.rem(h + d, H) for d in range(H)]
    hfrom = [lax.rem(h + H - d, H) for d in range(H)]
    counter = [0]
    pending = []

    def exchange(source, target, device, landing):
        index = counter[0]
        counter[0] += 1
        made = Exchange(
            source, target, device, landing, send_sems.at[index], recv_sems.at[index]
        )
        pending.append(made)
        return made.start()

    local_counter = [0]

    def local_copy(source, target):
        made = pltpu.make_async_copy(source, target, local_sems.at[local_counter[0]])
        local_counter[0] += 1
        made.start()
        return made

    barrier = pltpu.get_barrier_semaphore()
    peers = [(f, hz[d], t) for d in range(1, H)] + [(f, h, s)]
    peers += [(fx[d], h, c) for d in range(1, 4) for c in (t, s)]
    for peer in peers:
        pl.semaphore_signal(barrier, inc=1, device_id=peer, device_id_type=MESH)

    for i in range(3):
        wbuf[i, h, t, :, whole(f, 128)] = wq[i].astype(F32).T.astype(BF16)
    wbuf[3, h, t, :, whole(f, 128)] = wo[...]
    pl.semaphore_wait(barrier, len(peers))

    first = [
        exchange(*[wbuf.at[:, h, t, :, whole(f, 128)]] * 2, (f, hz[d], t),
                 wbuf.at[:, hfrom[d], t, :, whole(f, 128)])
        for d in range(1, H)
    ]

    row_index = lax.broadcasted_iota(jnp.int32, (ROWS, 1), 0)

    def image(source, b):
        if b == 0:
            stage[0 : images * SEQ, :] = source[...].astype(F32)
        return jnp.where(row_index < SEQ, stage[b * SEQ : b * SEQ + ROWS, :], 0.0)

    for b in range(images):
        live = ((h * 2 + t) * images + b < counts[0]).astype(F32)
        rows_grad[h * 2 + t, b * ROWS : (b + 1) * ROWS, :] = (image(cot, b) * live).astype(BF16)

    def spread(rows):
        mine = rows.at[h * 2 + t, 0:own]
        far = [
            exchange(mine, mine, (f, hz[d], t), rows.at[hfrom[d] * 2 + t, 0:own])
            for d in range(1, H)
        ]
        near = [exchange(mine, mine, (f, h, s), rows.at[h * 2 + s, 0:own])]
        return far, near

    def pass_on(rows, far, near, d):
        far[d - 1].arrived()
        block = rows.at[hfrom[d] * 2 + t, 0:own]
        near.append(exchange(block, block, (f, h, s), rows.at[hfrom[d] * 2 + s, 0:own]))

    grad_far, grad_near = spread(rows_grad)

    for b in range(images):
        unit, _ = normal_parts(image(tokens, b))
        normed[b * ROWS : (b + 1) * ROWS, :] = (unit * gain[0:1] + bias[0:1]).astype(BF16)

    for step in first:
        step.arrived()
    second = [
        exchange(*[wbuf.at[:, :, t, :, whole(f, 128)]] * 2, (fx[d], h, t),
                 wbuf.at[:, :, t, :, whole(fx[d], 128)])
        for d in range(1, 4)
    ]

    @pl.loop(0, 2 * H)
    def _(b):
        for part in range(4):
            spot = lax.broadcasted_iota(jnp.int32, (CAP, own), 0) + CAP * part
            named = (prow[b, 0:1, 0:own] == spot) | (prow[b, 1:2, 0:own] == spot)
            big[b, part * CAP : (part + 1) * CAP, 0:own] = jnp.where(named, 1.0, 0.0).astype(BF16)

    for step in second:
        step.arrived()
    third = exchange(*[wbuf.at[:, :, t]] * 2, (f, h, s), wbuf.at[:, :, s])

    expert_moves = []
    depth, span = win_hbm.shape[1], win_hbm.shape[2]
    mine = [
        local_copy(win_hbm.at[f * 2 + t], win.at[whole(f, depth), whole(t, span)]),
        local_copy(wback_hbm.at[f * 2 + t], wback.at[whole(t, span), whole(f, depth)]),
    ]
    for d in range(0, 4):
        for c in (t, s) if d else (s,):
            target = win.at[whole(f, depth), whole(t, span)]
            landing = win.at[whole(fx[d], depth), whole(c, span)]
            device = (fx[d], h, c)
            expert_moves.append(exchange(win_hbm.at[fx[d] * 2 + c], target, device, landing))
            target = wback.at[whole(t, span), whole(f, depth)]
            landing = wback.at[whole(c, span), whole(fx[d], depth)]
            expert_moves.append(exchange(wback_hbm.at[fx[d] * 2 + c], target, device, landing))

    for d in range(1, H):
        pass_on(rows_grad, grad_far, grad_near, d)
    third.arrived()

    for i in range(3):
        part = mm(normed[...], wbuf[i].reshape(width, width), NT)
        if i == 0:
            part = part * HEAD ** (-0.5)
        qkv[:, i * width : (i + 1) * width] = part.astype(BF16)
    lane = lax.broadcasted_iota(jnp.int32, (1, 128), 1)
    sides = [jnp.where(lane < HEAD, 1.0, 0.0).astype(BF16), jnp.where(lane < HEAD, 0.0, 1.0).astype(BF16)]
    key_index = lax.broadcasted_iota(jnp.int32, (1, ROWS), 1)

    def pair_of(index):
        b, pair = index // half, lax.rem(index, half)
        rows = whole(b, ROWS)
        cols = [whole(pair + i * half, 128) for i in range(3)]
        return rows, cols

    @pl.loop(0, images * half)
    def _(index):
        rows, cols = pair_of(index)
        query, key, value = (qkv[rows, col] for col in cols)
        total = jnp.zeros((ROWS, 128), F32)
        for side in range(2):
            score = mm(query * sides[side], key, NT)
            score = jnp.where(key_index < SEQ, score, -1e30)
            score = jnp.exp(score - jnp.max(score, axis=-1, keepdims=True))
            prob = score / jnp.sum(score, axis=-1, keepdims=True)
            probs[index * 2 + side] = prob
            total += mm(prob.astype(BF16), value * sides[side])
        mixed[rows, cols[0]] = total.astype(BF16)

    for b in range(images):
        rows = slice(b * ROWS, (b + 1) * ROWS)
        value = image(tokens, b) + mm(mixed[rows, :], wbuf[3].reshape(width, width))
        middle[rows, :] = value
        unit, _ = normal_parts(value)
        rows_norm[h * 2 + t, rows, :] = (unit * gain[1:2] + bias[1:2]).astype(BF16)

    norm_far, norm_near = spread(rows_norm)

    def accumulate(rows, b, begin):
        for part in range(4):
            span_rows = slice(part * CAP, (part + 1) * CAP)
            value = mm(big[b, span_rows, 0:own], rows[b, 0:own])
            wide[span_rows, :] = value if begin else wide[span_rows, :] + value

    def route(rows, far, near, wait_far, send, landing):
        accumulate(rows, h * 2 + t, True)
        for d in range(1, H):
            if wait_far:
                pass_on(rows, far, near, d)
            accumulate(rows, hfrom[d] * 2 + t, False)
        for d in range(H):
            near[d].arrived()
            accumulate(rows, hfrom[d] * 2 + s, False)
        for part in range(4):
            send[part] = wide[part * CAP : (part + 1) * CAP, :].astype(BF16)
        moved = [
            exchange(send.at[fx[d]], landing.at[f], (fx[d], h, t), landing.at[fx[d]])
            for d in range(1, 4)
        ]
        return moved, local_copy(send.at[f], landing.at[f])

    grad_moved, grad_kept = route(rows_grad, grad_far, grad_near, False, gsend, grows)
    norm_moved, norm_kept = route(rows_norm, norm_far, norm_near, True, xsend, xrows)

    for move in expert_moves:
        move.arrived()
    for move in mine:
        move.wait()
    for move in grad_moved + norm_moved:
        move.arrived()
        move.sent()
    grad_kept.wait()
    norm_kept.wait()

    expert = h * local_count + f * 2 + t
    router_lane = lax.broadcasted_iota(jnp.int32, (1, wr.shape[1]), 1)
    chosen = (router_lane == expert).astype(F32)
    chunk = 512
    chunks = win.shape[1] // chunk
    back_moves = []
    back_kept = []
    for d in (1, 2, 3, 0):
        group = fx[d]
        here = whole(group, CAP)
        rows = xrows[group]
        result = jnp.zeros((CAP, width), F32)
        for c in range(chunks):
            value, slope = gelu_parts(mm(rows, win[:, c * chunk : (c + 1) * chunk]))
            value = value.astype(BF16)
            big[c, here, :] = value
            wide[(4 + c) * CAP : (5 + c) * CAP, :] = slope
            result += mm(value, wback[c * chunk : (c + 1) * chunk, :])
        logits = mm(rows, wr[...])
        odds = jnp.exp(logits - jnp.max(logits, axis=-1, keepdims=True))
        odds = odds / jnp.sum(odds, axis=-1, keepdims=True)
        gate = jnp.sum(odds * chosen, axis=-1, keepdims=True)
        row_grad = grows[group].astype(F32)
        gate_grad = jnp.sum(row_grad * result, axis=-1, keepdims=True)
        gsend[group] = (gate * result).astype(BF16)
        result_grad = (gate * row_grad).astype(BF16)
        grows[group] = result_grad
        logit = (gate_grad * gate * (chosen - odds)).astype(BF16)
        logit_grad[here, :] = logit
        total = mm(logit, wr[...], NT)
        for c in range(chunks):
            grad = mm(result_grad, wback[c * chunk : (c + 1) * chunk, :], NT)
            grad = (grad * wide[(4 + c) * CAP : (5 + c) * CAP, :]).astype(BF16)
            big[4 + c, here, :] = grad
            total += mm(grad, win[:, c * chunk : (c + 1) * chunk], NT)
        xsend[group] = total.astype(BF16)
        if d:
            device = (group, h, t)
            back_moves.append(
                (exchange(xsend.at[group], xback.at[f], device, xback.at[group]),
                 exchange(gsend.at[group], gback.at[f], device, gback.at[group]))
            )
        else:
            back_kept = [
                local_copy(xsend.at[group], xback.at[f]),
                local_copy(gsend.at[group], gback.at[f]),
            ]

    for move in grad_far + grad_near + norm_far + norm_near:
        move.sent()
    flat_rows = xrows[...].reshape(4 * CAP, width)
    flat_grad = grows[...].reshape(4 * CAP, width)
    for c in range(chunks):
        rows_grad[c] = mm(flat_rows, big[4 + c], TN).astype(BF16)
        rows_norm[c] = mm(big[c], flat_grad, TN).astype(BF16)
    route_c[t] = mm(logit_grad[...], flat_rows, TN)
    grad_moves = []
    halves = chunks // 2
    for d in range(4):
        for c in (t, s):
            for part in range(halves):
                source_in = rows_grad.at[c * halves + part, whole(fx[d], depth), :]
                source_back = rows_norm.at[c * halves + part, :, whole(fx[d], depth)]
                target_in = gin_out.at[f * 2 + t, part]
                target_back = gback_out.at[f * 2 + t, part]
                if d == 0 and c is t:
                    grad_moves.append(local_copy(source_in, target_in))
                    grad_moves.append(local_copy(source_back, target_back))
                    continue
                device = (fx[d], h, c)
                landing = gin_out.at[fx[d] * 2 + c, part]
                grad_moves.append(exchange(source_in, target_in, device, landing))
                landing = gback_out.at[fx[d] * 2 + c, part]
                grad_moves.append(exchange(source_back, target_back, device, landing))
    route_near = exchange(route_c.at[t], route_c.at[t], (f, h, s), route_c.at[s])

    def share(b, back):
        spots = jnp.transpose(prow[b])[0:own]
        slot = lax.broadcasted_iota(jnp.int32, (own, 4 * CAP), 1)
        named = (spots[:, 0:1] == slot) | (spots[:, 1:2] == slot)
        return mm(jnp.where(named, 1.0, 0.0).astype(BF16), back[...].reshape(4 * CAP, width))

    def gather_sums(which, back, near_out, far_out):
        near, far = [], []
        for d in range(H):
            other = hz[H - 1 - d]
            near_out(other)[...] = share(other * 2 + s, back).astype(BF16)
            near.append(
                exchange(near_out(other), sib_in.at[which, other], (f, h, s), sib_in.at[which, other])
            )
        for d in range(H):
            other = hz[H - 1 - d]
            value = share(other * 2 + t, back)
            near[d].arrived()
            value = value + sib_in[which, other].astype(F32)
            if d == H - 1:
                own_sum[which] = value
            else:
                far_out(other)[...] = value.astype(BF16)
                hop = H - 1 - d
                far.append(
                    exchange(far_out(other), z_in.at[which, h], (f, other, t), z_in.at[which, hfrom[hop]])
                )
        return far

    for move, _ in back_moves:
        move.arrived()
    back_kept[0].wait()
    norm_sums = gather_sums(0, xback, lambda other: sib_out.at[other], lambda other: z_out.at[other])
    for _, move in back_moves:
        move.arrived()
    back_kept[1].wait()
    out_sums = gather_sums(
        1, gback, lambda other: big.at[other, 0:own], lambda other: big.at[H + other, 0:own]
    )

    route_near.arrived()
    route_p[f] = route_c[0] + route_c[1]
    route_plane = [
        exchange(route_p.at[f], route_p.at[f], (fx[d], h, t), route_p.at[fx[d]]) for d in range(1, 4)
    ]

    def group_sum(which, far, rows):
        total = own_sum[which, rows, :]
        for d in range(1, H):
            total = total + z_in[which, hfrom[d], rows, :].astype(F32)
        return total

    for move in norm_sums:
        move.arrived()
    small_c[t] = jnp.zeros(small_c.shape[1:], F32)
    for b in range(images):
        rows = slice(b * ROWS, (b + 1) * ROWS)
        grad = group_sum(0, norm_sums, rows)
        unit, scale = normal_parts(middle[rows, :])
        small_c[t, 1:2] += jnp.sum(grad * unit, axis=0, keepdims=True)
        small_c[t, 3:4] += jnp.sum(grad, axis=0, keepdims=True)
        live = ((h * 2 + t) * images + b < counts[0]).astype(F32)
        grad = normal_pull(grad, unit, scale, gain[1:2]) + image(cot, b) * live
        grad_mid[rows, :] = grad

    for move, _ in back_moves:
        move.sent()
    low = grad_mid[...].astype(BF16)
    count = H * 2 * 64
    wide[3 * count : 4 * count, :] = mm(mixed[...], low, TN)
    mixed[...] = mm(low, wbuf[3].reshape(width, width), NT).astype(BF16)

    @pl.loop(0, images * half)
    def _(index):
        rows, cols = pair_of(index)
        query, key, value = (qkv[rows, col] for col in cols)
        pulled = mixed[rows, cols[0]]
        grads = [jnp.zeros((ROWS, 128), F32) for _ in range(3)]
        for side in range(2):
            prob = probs[index * 2 + side]
            one = pulled * sides[side]
            prob_grad = mm(one, value, NT)
            grads[2] += mm(prob.astype(BF16), one, TN)
            inner = jnp.sum(prob * prob_grad, axis=-1, keepdims=True)
            score_grad = (prob * (prob_grad - inner)).astype(BF16)
            grads[0] += mm(score_grad, key * sides[side])
            grads[1] += mm(score_grad, query * sides[side], TN)
        grads[0] = grads[0] * HEAD ** (-0.5)
        for grad, col in zip(grads, cols):
            qkv[rows, col] = grad.astype(BF16)

    for i in range(3):
        wide[i * count : (i + 1) * count, :] = mm(
            qkv[:, i * width : (i + 1) * width], normed[...], TN
        )

    def wide_rows(i, other, core):
        return whole((i * H + other) * 2 + core, 64)

    for i in range(4):
        for other in range(H):
            xsend[i, other * 64 : (other + 1) * 64, :] = wide[wide_rows(i, other, s), :].astype(BF16)
    att_out = xsend.at[:, 0 : H * 64]
    att_near = exchange(att_out, att_in, (f, h, s), att_in)

    for b in range(images):
        rows = slice(b * ROWS, (b + 1) * ROWS)
        grad = jnp.zeros((ROWS, width), F32)
        for i in range(3):
            grad += mm(qkv[rows, i * width : (i + 1) * width], wbuf[i].reshape(width, width))
        unit, scale = normal_parts(image(tokens, b))
        small_c[t, 0:1] += jnp.sum(grad * unit, axis=0, keepdims=True)
        small_c[t, 2:3] += jnp.sum(grad, axis=0, keepdims=True)
        grad = normal_pull(grad, unit, scale, gain[0:1]) + grad_mid[rows, :]
        tgrad[b * SEQ : (b + 1) * SEQ, :] = grad[0:SEQ]
    small_near = exchange(small_c.at[t], small_c.at[t], (f, h, s), small_c.at[s])

    att_near.arrived()
    att_near.sent()
    for i in range(4):
        for other in range(H):
            here = wide_rows(i, other, t)
            here_low = slice(other * 64, (other + 1) * 64)
            value = wide[here, :] + att_in[i, here_low, :].astype(F32)
            wide[here, :] = value
            xsend[i, here_low, :] = value.astype(BF16)
    plane = [
        exchange(xsend.at[:, 0 : H * 64, whole(fx[d], 128)], plane_in.at[f], (fx[d], h, t), plane_in.at[fx[d]])
        for d in range(1, 4)
    ]
    small_near.arrived()
    small_p[f] = small_c[0] + small_c[1]
    small_plane = [
        exchange(small_p.at[f], small_p.at[f], (fx[d], h, t), small_p.at[fx[d]]) for d in range(1, 4)
    ]
    for move in route_plane:
        move.arrived()
    route_z[h] = (route_p[0] + route_p[1]) + (route_p[2] + route_p[3])
    route_line = [
        exchange(route_z.at[h], route_z.at[h], (f, hz[d], t), route_z.at[hfrom[d]]) for d in range(1, H)
    ]

    for move in out_sums:
        move.arrived()
    for b in range(images):
        rows = slice(b * ROWS, (b + 1) * ROWS)
        value = middle[rows, :] + group_sum(1, out_sums, rows)
        stage[b * SEQ : (b + 1) * SEQ, :] = value[0:SEQ]
    out[...] = stage[0 : images * SEQ, :].astype(BF16)

    for move in plane:
        move.arrived()
    for i in range(4):
        for other in range(H):
            value = wide[wide_rows(i, other, t), whole(f, 128)]
            for d in range(1, 4):
                value = value + plane_in[fx[d], i, other * 64 : (other + 1) * 64, :].astype(F32)
            wide[wide_rows(i, other, t), 0:128] = value
            line_out[other, i] = value.astype(BF16)
    line = [
        exchange(line_out.at[hz[d]], line_in.at[h], (f, hz[d], t), line_in.at[hfrom[d]])
        for d in range(1, H)
    ]
    for move in small_plane:
        move.arrived()
    small_z[h] = (small_p[0] + small_p[1]) + (small_p[2] + small_p[3])
    small_line = [
        exchange(small_z.at[h], small_z.at[h], (f, hz[d], t), small_z.at[hfrom[d]]) for d in range(1, H)
    ]
    for move in route_line:
        move.arrived()
    total = route_z[0]
    for d in range(1, H):
        total = total + route_z[d]
    wrg[...] = total.T

    for move in line:
        move.arrived()
    for i in range(4):
        value = wide[wide_rows(i, h, t), 0:128]
        for d in range(1, H):
            value = value + line_in[hfrom[d], i].astype(F32)
        if i < 3:
            wqg[i] = value.T
        else:
            wog[...] = value
    for move in small_line:
        move.arrived()
    total = small_z[0]
    for d in range(1, H):
        total = total + small_z[d]
    lng[...] = total[0:2]
    lnb[...] = total[2:4]

    for move in grad_moves:
        if isinstance(move, Exchange):
            move.arrived()
        else:
            move.wait()
    already = set(map(id, [att_near] + [move for move, _ in back_moves] + grad_far + grad_near + norm_far + norm_near + grad_moved + norm_moved))
    for move in pending:
        if id(move) not in already:
            move.sent()


def fast_device(
    tokens,
    cotangent,
    image_counts,
    w_qkv,
    w_out,
    ln_gain,
    ln_bias,
    w_router,
    w_in,
    w_back,
    expert_ids,
    slots,
):
    H = lax.axis_size("heads")
    own_rows, width = tokens.shape
    images = own_rows // SEQ
    own = images * ROWS
    local_count, depth, span = w_in.shape[1:]
    experts = w_router.shape[2]
    hidden = span * 2
    core = lax.axis_index("tensor")

    relative = expert_ids[0] - lax.axis_index("heads") * local_count
    wanted = (slots[0] >= 0) & (relative >= 0) & (relative < local_count) & (relative % 2 == core)
    places = jnp.where(wanted, (relative // 2) * CAP + slots[0], -1)
    places = jnp.transpose(places).reshape(2, 2 * H, images, SEQ)
    places = jnp.pad(places, ((0, 0), (0, 0), (0, 0), (0, ROWS - SEQ)), constant_values=-1)
    places = jnp.transpose(places.reshape(2, 2 * H, own), (1, 0, 2))
    places = jnp.pad(places, ((0, 0), (0, 6), (0, width - own)), constant_values=-1)

    vmem = pl.BlockSpec(memory_space=pltpu.VMEM)
    smem = pl.BlockSpec(memory_space=pltpu.SMEM)
    anywhere = pl.BlockSpec(memory_space=pl.ANY)
    shape = jax.ShapeDtypeStruct

    def low(*dims):
        return pltpu.VMEM(dims, BF16)

    def full(*dims):
        return pltpu.VMEM(dims, F32)

    outs = pl.pallas_call(
        lambda *refs: block_kernel(H, images, local_count, refs),
        out_shape=(
            shape((own_rows, width), BF16),
            shape((own_rows, width), F32),
            shape((3, depth, 64), F32),
            shape((64, depth), F32),
            shape((2, width), F32),
            shape((2, width), F32),
            shape((width, experts), F32),
            shape((local_count, hidden // 1024, depth, 512), BF16),
            shape((local_count, hidden // 1024, 512, depth), BF16),
        ),
        in_specs=[vmem, vmem, smem, vmem, vmem, vmem, vmem, vmem, anywhere, anywhere, vmem],
        out_specs=[vmem] * 7 + [anywhere] * 2,
        scratch_shapes=[
            full(images * SEQ + 16, width),
            low(4, H, 2, 64, width),
            low(width, hidden),
            low(hidden, width),
            low(2 * H, 512, width),
            low(2 * H, 512, width),
            low(8, 4 * CAP, 512),
            full(8 * CAP, width),
            low(4, CAP, width),
            low(4, CAP, width),
            low(4, CAP, width),
            low(4, CAP, width),
            low(4, CAP, width),
            low(4, CAP, width),
            low(own, width),
            low(own, 3 * width),
            full(images * width // HEAD, ROWS, ROWS),
            low(own, width),
            full(own, width),
            full(own, width),
            low(4 * CAP, experts),
            low(H, own, width),
            low(2, H, own, width),
            low(H, own, width),
            low(2, H, own, width),
            full(2, own, width),
            low(4, H * 64, width),
            low(4, 4, H * 64, 128),
            low(H, 4, 64, 128),
            low(H, 4, 64, 128),
            full(2, 8, width),
            full(4, 8, width),
            full(H, 8, width),
            full(2, experts, width),
            full(4, experts, width),
            full(H, experts, width),
            pltpu.SemaphoreType.DMA((128,)),
            pltpu.SemaphoreType.DMA((128,)),
            pltpu.SemaphoreType.DMA((16,)),
        ],
        compiler_params=pltpu.CompilerParams(
            collective_id=0, has_side_effects=True, vmem_limit_bytes=62 * 2**20
        ),
        name="block",
    )(
        tokens, cotangent, image_counts, w_qkv[0], w_out[0], ln_gain[0], ln_bias[0], w_router[0],
        w_in[0], w_back[0], places,
    )
    block_out, token_grad, qkv_grad, out_grad, gains, shifts, router, in_low, back_low = outs
    in_grad = jnp.transpose(in_low, (0, 2, 1, 3)).reshape(w_in.shape).astype(F32)
    back_grad = back_low.reshape(w_back.shape).astype(F32)
    return (
        block_out,
        token_grad,
        qkv_grad[None],
        out_grad[None],
        gains[None],
        shifts[None],
        router[None],
        in_grad,
        back_grad,
    )


def solution(mesh):
    def program(*arrays):
        sizes = dict(mesh.shape)
        devices = sizes["fsdp"] * sizes["heads"] * sizes["tensor"]
        own_rows = arrays[0].shape[0] // devices
        one_expert = sizes["fsdp"] == 4 and sizes["tensor"] == 2 and arrays[8].shape[1] == devices
        one_expert = one_expert and own_rows % SEQ == 0
        return placed(mesh, fast_device if one_expert else on_device)(*arrays)

    return program


def placed(mesh, on_device):
    return jax.shard_map(
        on_device,
        mesh=mesh,
        in_specs=(
            P(("fsdp", "heads", "tensor"), None),
            P(("fsdp", "heads", "tensor"), None),
            P("fsdp"),
            P(None, None, "fsdp", ("heads", "tensor")),
            P(None, ("heads", "tensor"), "fsdp"),
            P(),
            P(),
            P(),
            P(None, "heads", "fsdp", "tensor"),
            P(None, "heads", "tensor", "fsdp"),
            P(None, "fsdp", None),
            P(None, "fsdp", None),
        ),
        out_specs=(
            P(("fsdp", "heads", "tensor"), None),
            P(("fsdp", "heads", "tensor"), None),
            P(None, None, "fsdp", ("heads", "tensor")),
            P(None, ("heads", "tensor"), "fsdp"),
            P(),
            P(),
            P(),
            P(None, "heads", "fsdp", "tensor"),
            P(None, "heads", "tensor", "fsdp"),
        ),
        check_vma=False,
    )
```

```python
import jax
import jax.numpy as jnp
from jax import lax
from jax.experimental import pallas as pl
from jax.experimental.pallas import tpu as pltpu
from jax.sharding import PartitionSpec as P

HEAD = 64
SEQ = 197
LAYERS = 1
CAP = 256


def layer_norm(value, ln_gains, ln_shift):
    centred = value - jnp.mean(value, axis=-1, keepdims=True)
    spread = jnp.mean(centred * centred, axis=-1, keepdims=True)
    return centred * lax.rsqrt(spread + 1e-06) * ln_gains + ln_shift


def gelu_exact(value):
    return jax.nn.gelu(value, approximate=False)


def with_zero_row(matrix):
    return jnp.concatenate([matrix, jnp.zeros((1,) + matrix.shape[1:], matrix.dtype)], axis=0)


def slot_tables(named_expert, slot_rows, first_expert, local_experts):
    group_rows = named_expert.shape[0]
    is_local = (
        (slot_rows >= 0)
        & (named_expert >= first_expert)
        & (named_expert < first_expert + local_experts)
    )
    places = jnp.where(
        is_local, (named_expert - first_expert) * CAP + slot_rows, local_experts * CAP
    )
    picked = jnp.full((local_experts * CAP + 1,), 2 * group_rows, jnp.int32)
    picked = picked.at[places.reshape(-1)].set(jnp.arange(2 * group_rows, dtype=jnp.int32))
    return (places, picked[: local_experts * CAP])


def joined_qkv(qkv_weight):
    head_cols = qkv_weight.shape[2]
    return jnp.transpose(qkv_weight, (1, 0, 2)).reshape(qkv_weight.shape[1], 3 * head_cols)


def forward_block(
    residual, weights, ln_gains, ln_shift, router_weight, named_expert, slot_rows, first_expert
):
    qkv_weight, out_weight, in_weight, back_weight = weights
    own_rows, widths = residual.shape
    group_rows = named_expert.shape[0]
    head_cols = qkv_weight.shape[2]
    local_experts = in_weight.shape[0]
    head_shape = (group_rows // SEQ, SEQ, head_cols // HEAD, HEAD)
    q_scale = HEAD ** (-0.5)
    flat_qkv = joined_qkv(qkv_weight)
    normed_rows = layer_norm(residual, ln_gains[0], ln_shift[0]).astype(jnp.bfloat16)
    normed = lax.all_gather(normed_rows, ("heads", "tensor"), axis=0, tiled=True)
    projected = jnp.dot(normed, flat_qkv, preferred_element_type=jnp.float32)
    queries = (projected[:, :head_cols] * q_scale).astype(jnp.bfloat16).reshape(head_shape)
    key_rows = projected[:, head_cols : 2 * head_cols].astype(jnp.bfloat16).reshape(head_shape)
    value_rows = projected[:, 2 * head_cols :].astype(jnp.bfloat16).reshape(head_shape)
    scores = jnp.einsum("bqhd,bkhd->bhqk", queries, key_rows, preferred_element_type=jnp.float32)
    log_total = jax.nn.logsumexp(scores, axis=-1)
    attn_probs = jax.nn.softmax(scores, axis=-1).astype(jnp.bfloat16)
    mixed_rows = jnp.einsum(
        "bhqk,bkhd->bqhd", attn_probs, value_rows, preferred_element_type=jnp.float32
    )
    mixed_rows = mixed_rows.reshape(group_rows, head_cols).astype(jnp.bfloat16)
    middle = residual + lax.psum_scatter(
        jnp.dot(mixed_rows, out_weight, preferred_element_type=jnp.float32),
        ("heads", "tensor"),
        scatter_dimension=0,
        tiled=True,
    )
    head_full = ()
    normed_two_rows = layer_norm(middle, ln_gains[1], ln_shift[1]).astype(jnp.bfloat16)
    normed_two = lax.all_gather(normed_two_rows, ("heads", "tensor"), axis=0, tiled=True)
    router = jax.nn.softmax(
        jnp.dot(normed_two, router_weight, preferred_element_type=jnp.float32), axis=-1
    )
    gate_values = jnp.take_along_axis(router, named_expert, axis=1) * (slot_rows >= 0)
    places, picked = slot_tables(named_expert, slot_rows, first_expert, local_experts)
    routed = with_zero_row(normed_two)[picked // 2].reshape(local_experts, CAP, widths)
    hidden = jnp.einsum("ecd,edf->ecf", routed, in_weight, preferred_element_type=jnp.float32)
    active = gelu_exact(hidden).astype(jnp.bfloat16)
    result = jnp.einsum("ecf,efd->ecd", active, back_weight, preferred_element_type=jnp.float32)
    flat_result = with_zero_row(result.reshape(local_experts * CAP, widths))
    block_out = middle + lax.psum_scatter(
        (
            flat_result[places[:, 0]] * gate_values[:, 0:1]
            + flat_result[places[:, 1]] * gate_values[:, 1:2]
        ).astype(jnp.bfloat16),
        ("heads", "tensor"),
        scatter_dimension=0,
        tiled=True,
    ).astype(jnp.float32)
    stored = (
        residual,
        middle,
        normed,
        queries,
        key_rows,
        value_rows,
        log_total,
        mixed_rows,
        normed_two_rows,
        router,
        gate_values,
        places,
        picked,
        routed,
        hidden,
        active,
        flat_result,
    )
    return (block_out, stored, head_full)


def backward_block(
    grad_rows, stored, weights, ln_gains, ln_shift, router_weight, named_expert, row_start
):
    qkv_weight, out_weight, in_weight, back_weight = weights
    (
        residual,
        middle,
        normed,
        queries,
        key_rows,
        value_rows,
        log_total,
        mixed_rows,
        normed_two_rows,
        router,
        gate_values,
        places,
        picked,
        routed,
        hidden,
        active,
        flat_result,
    ) = stored
    own_rows, widths = residual.shape
    group_rows = named_expert.shape[0]
    head_cols = qkv_weight.shape[2]
    local_experts = in_weight.shape[0]
    expert_count = router.shape[1]
    q_scale = HEAD ** (-0.5)
    flat_qkv = joined_qkv(qkv_weight)
    grad_moe = lax.all_gather(
        grad_rows.astype(jnp.bfloat16), ("heads", "tensor"), axis=0, tiled=True
    )
    back_rows = with_zero_row(grad_moe)[picked // 2].astype(jnp.float32)
    gate_slots = with_zero_row(gate_values.reshape(-1))[picked]
    gate_grad_slots = jnp.sum(back_rows * flat_result[:-1], axis=1)
    gate_grads = with_zero_row(gate_grad_slots)[places]
    expert_range = jnp.arange(expert_count, dtype=jnp.int32)
    router_part = jnp.sum(
        gate_grads[:, :, None]
        * (named_expert[:, :, None] == expert_range[None, None, :]).astype(jnp.float32),
        axis=1,
    )
    grad_result = (
        (gate_slots[:, None] * back_rows).astype(jnp.bfloat16).reshape(local_experts, CAP, widths)
    )
    grad_active = jnp.einsum(
        "ecd,efd->ecf", grad_result, back_weight, preferred_element_type=jnp.float32
    )
    gelu_value, gelu_pull = jax.vjp(gelu_exact, hidden)
    grad_hidden = gelu_pull(grad_active)[0].astype(jnp.bfloat16)
    back_grad = jnp.einsum("ecf,ecd->efd", active, grad_result, preferred_element_type=jnp.float32)
    in_grad = jnp.einsum("ecd,ecf->edf", routed, grad_hidden, preferred_element_type=jnp.float32)
    grad_routed = jnp.einsum(
        "ecf,edf->ecd", grad_hidden, in_weight, preferred_element_type=jnp.float32
    )
    grad_routed = with_zero_row(grad_routed.reshape(local_experts * CAP, widths))
    token_part = grad_routed[places[:, 0]] + grad_routed[places[:, 1]]
    grad_normed_two, router_rows = (
        lax.psum_scatter(token_part, ("heads", "tensor"), scatter_dimension=0, tiled=True),
        lax.psum_scatter(router_part, ("heads", "tensor"), scatter_dimension=0, tiled=True),
    )
    router_own = lax.dynamic_slice_in_dim(router, row_start, own_rows, 0)
    grad_logits = (
        router_own * (router_rows - jnp.sum(router_own * router_rows, axis=-1, keepdims=True))
    ).astype(jnp.bfloat16)
    router_grad = jnp.einsum(
        "td,te->de", normed_two_rows, grad_logits, preferred_element_type=jnp.float32
    )
    grad_normed_two = grad_normed_two + jnp.einsum(
        "te,de->td", grad_logits, router_weight, preferred_element_type=jnp.float32
    )
    norm_value, norm_pull = jax.vjp(layer_norm, middle, ln_gains[1], ln_shift[1])
    grad_middle, gain_two, shift_two = norm_pull(grad_normed_two)
    grad_middle = grad_middle + grad_rows
    grad_attn = lax.all_gather(
        grad_middle.astype(jnp.bfloat16), ("heads", "tensor"), axis=0, tiled=True
    )
    out_grad = jnp.einsum("tc,td->cd", mixed_rows, grad_attn, preferred_element_type=jnp.float32)
    grad_mixed = jnp.einsum("td,cd->tc", grad_attn, out_weight, preferred_element_type=jnp.float32)
    grad_mixed = grad_mixed.astype(jnp.bfloat16).reshape(queries.shape)
    scores = jnp.einsum("bqhd,bkhd->bhqk", queries, key_rows, preferred_element_type=jnp.float32)
    attn_probs = jnp.exp(scores - log_total[..., None])
    grad_values = jnp.einsum(
        "bhqk,bqhd->bkhd",
        attn_probs.astype(jnp.bfloat16),
        grad_mixed,
        preferred_element_type=jnp.float32,
    )
    grad_probs = jnp.einsum(
        "bqhd,bkhd->bhqk", grad_mixed, value_rows, preferred_element_type=jnp.float32
    )
    grad_scores = (
        attn_probs * (grad_probs - jnp.sum(attn_probs * grad_probs, axis=-1, keepdims=True))
    ).astype(jnp.bfloat16)
    grad_queries = jnp.einsum(
        "bhqk,bkhd->bqhd", grad_scores, key_rows, preferred_element_type=jnp.float32
    )
    grad_keys = jnp.einsum(
        "bhqk,bqhd->bkhd", grad_scores, queries, preferred_element_type=jnp.float32
    )
    grad_projected = jnp.concatenate(
        [
            grad_queries.reshape(group_rows, head_cols),
            grad_keys.reshape(group_rows, head_cols),
            grad_values.reshape(group_rows, head_cols),
        ],
        axis=1,
    ).astype(jnp.bfloat16)
    qkv_flat_grad = jnp.einsum(
        "td,tc->dc", normed, grad_projected, preferred_element_type=jnp.float32
    )
    column_scale = jnp.concatenate(
        [jnp.full((head_cols,), q_scale, jnp.float32), jnp.ones((2 * head_cols,), jnp.float32)]
    )
    qkv_grad = jnp.transpose(
        (qkv_flat_grad * column_scale).reshape(widths, 3, head_cols), (1, 0, 2)
    )
    query_term = (
        jnp.einsum(
            "tc,dc->td",
            grad_projected[:, :head_cols],
            flat_qkv[:, :head_cols],
            preferred_element_type=jnp.float32,
        )
        * q_scale
    )
    grad_normed = lax.psum_scatter(
        query_term
        + jnp.einsum(
            "tc,dc->td",
            grad_projected[:, head_cols:],
            flat_qkv[:, head_cols:],
            preferred_element_type=jnp.float32,
        ),
        ("heads", "tensor"),
        scatter_dimension=0,
        tiled=True,
    )
    first_value, first_pull = jax.vjp(layer_norm, residual, ln_gains[0], ln_shift[0])
    grad_input, gain_one, shift_one = first_pull(grad_normed)
    grad_input = grad_input + grad_middle
    matrix_grads = (qkv_grad, out_grad, in_grad, back_grad)
    small_grads = (jnp.stack([gain_one, gain_two]), jnp.stack([shift_one, shift_two]), router_grad)
    return (grad_input, matrix_grads, small_grads)


def on_device(
    tokens,
    cotangent,
    image_counts,
    w_qkv,
    w_out,
    ln_gain,
    ln_bias,
    w_router,
    w_in,
    w_back,
    expert_ids,
    slots,
):
    own_rows = tokens.shape[0]
    row_start = lax.axis_index(("heads", "tensor")) * own_rows
    first_expert = lax.axis_index("heads") * w_in.shape[1]
    residual = tokens.astype(jnp.float32)
    head_list = []
    block_index = 0
    weights = (
        lax.all_gather(w_qkv[block_index], "fsdp", axis=1, tiled=True),
        lax.all_gather(w_out[block_index], "fsdp", axis=1, tiled=True),
        lax.all_gather(w_in[block_index], "fsdp", axis=1, tiled=True),
        lax.all_gather(w_back[block_index], "fsdp", axis=2, tiled=True),
    )
    residual, stored, head_full = forward_block(
        residual,
        weights,
        ln_gain[block_index],
        ln_bias[block_index],
        w_router[block_index],
        expert_ids[block_index],
        slots[block_index],
        first_expert,
    )
    stored_list = [stored]
    head_list.append(head_full)
    image_index = (row_start + jnp.arange(own_rows, dtype=jnp.int32)) // SEQ
    live_rows = (image_index < image_counts[0]).astype(jnp.float32)
    grad_rows = cotangent.astype(jnp.float32) * live_rows[:, None]
    matrix_list = [None] * LAYERS
    small_list = [None] * LAYERS
    for block_index in reversed(range(LAYERS)):
        weights = (
            lax.all_gather(w_qkv[block_index], "fsdp", axis=1, tiled=True),
            lax.all_gather(w_out[block_index], "fsdp", axis=1, tiled=True),
            lax.all_gather(w_in[block_index], "fsdp", axis=1, tiled=True),
            lax.all_gather(w_back[block_index], "fsdp", axis=2, tiled=True),
        )
        grad_rows, matrix_grads, small_grads = backward_block(
            grad_rows,
            stored_list[block_index],
            weights,
            ln_gain[block_index],
            ln_bias[block_index],
            w_router[block_index],
            expert_ids[block_index],
            row_start,
        )
        matrix_list[block_index] = (
            lax.psum_scatter(matrix_grads[0], "fsdp", scatter_dimension=1, tiled=True),
            lax.psum_scatter(matrix_grads[1], "fsdp", scatter_dimension=1, tiled=True),
            lax.psum_scatter(matrix_grads[2], "fsdp", scatter_dimension=1, tiled=True),
            lax.psum_scatter(matrix_grads[3], "fsdp", scatter_dimension=2, tiled=True),
        )
        small_list[block_index] = small_grads
    gain_grads, shift_grads, router_grads = lax.psum(
        (
            jnp.stack([entry[0] for entry in small_list]),
            jnp.stack([entry[1] for entry in small_list]),
            jnp.stack([entry[2] for entry in small_list]),
        ),
        ("fsdp", "heads", "tensor"),
    )
    qkv_grads = jnp.stack([entry[0] for entry in matrix_list])
    out_grads = jnp.stack([entry[1] for entry in matrix_list])
    in_grads = jnp.stack([entry[2] for entry in matrix_list])
    back_grads = jnp.stack([entry[3] for entry in matrix_list])
    return (
        residual.astype(jnp.bfloat16),
        grad_rows,
        qkv_grads,
        out_grads,
        gain_grads,
        shift_grads,
        router_grads,
        in_grads,
        back_grads,
    )


ROWS = -(-SEQ // 16) * 16
MESH = pl.DeviceIdType.MESH
F32, BF16 = jnp.float32, jnp.bfloat16
NN, NT, TN = (((1,), (0,)), ((), ())), (((1,), (1,)), ((), ())), (((0,), (0,)), ((), ()))


def mm(left, right, dims=NN):
    return lax.dot_general(left, right, dims, preferred_element_type=F32)


def whole(index, size):
    return pl.ds(pl.multiple_of(index * size, size), size)


def normal_parts(value):
    centred = value - jnp.mean(value, axis=-1, keepdims=True)
    scale = lax.rsqrt(jnp.mean(centred * centred, axis=-1, keepdims=True) + 1e-06)
    return centred * scale, scale


def normal_pull(grad, unit, scale, gains):
    grad_unit = grad * gains
    mean_grad = jnp.mean(grad_unit, axis=-1, keepdims=True)
    mean_both = jnp.mean(grad_unit * unit, axis=-1, keepdims=True)
    return scale * (grad_unit - mean_grad - unit * mean_both)


def gelu_parts(value):
    size = jnp.abs(value)
    step = 1.0 / (1.0 + 0.3275911 * 2.0**-0.5 * size)
    bell = jnp.exp(-0.5 * (value * value))
    series = 1.061405429 * step - 1.453152027
    series = series * step + 1.421413741
    series = series * step - 0.284496736
    series = series * step + 0.254829592
    tail = 0.5 * series * step * bell
    share = jnp.where(value < 0, tail, 1.0 - tail)
    return value * share, share + value * (bell * 0.3989422804014327)


class Exchange:
    def __init__(self, source, target, device, landing, send, recv):
        self.out = pltpu.make_async_remote_copy(
            source, target, send, recv, device_id=device, device_id_type=MESH
        )
        self.into = pltpu.make_async_remote_copy(
            landing, landing, send, recv, device_id=device, device_id_type=MESH
        )

        self.open = [True, True]
        self.out.start()

    def arrived(self):
        if self.open[0]:
            self.into.wait_recv()
        self.open[0] = False

    def sent(self):
        if self.open[1]:
            self.out.wait_send()
        self.open[1] = False

    def finish(self):
        self.arrived()
        self.sent()


class Kept:
    def __init__(self, source, target, semaphore):
        self.copy = pltpu.make_async_copy(source, target, semaphore)
        self.open = True
        self.copy.start()

    def arrived(self):
        if self.open:
            self.copy.wait()
        self.open = False

    sent = finish = arrived


def block_kernel(depth_z, images, local_count, refs):
    H = depth_z
    (
        tokens, cot, counts, wq, wo, gain, bias, wr, win_hbm, wback_hbm, prow,
        out, tgrad, wqg, wog, lng, lnb, wrg, gin_out, gback_out,
        stage, wbuf, win, wback, rows_grad, rows_norm, big, wide,
        xsend, gsend, xrows, grows, xback, gback,
        normed, qkv, probs, mixed, middle, grad_mid, logit_grad,
        sib_out, sib_in, z_out, z_in, own_sum,
        att_in, plane_in, line_out, line_in,
        small_c, small_p, small_z, route_out, route_in, route_z, route_all,
        send_sems, recv_sems, local_sems,
    ) = refs
    own = images * ROWS
    width = tokens.shape[1]
    half = width // 128
    f, h, t = (lax.axis_index(name) for name in ("fsdp", "heads", "tensor"))
    s = 1 - t
    fx = [f, f + 1 - 2 * lax.rem(f, 2), lax.rem(f + 2, 4), 3 - f]
    hz = [lax.rem(h + d, H) for d in range(H)]
    hfrom = [lax.rem(h + H - d, H) for d in range(H)]
    after, before, across = lax.rem(2 * h + 1, 5), lax.rem(3 * h + 2, 5), 3 - h
    counter = [0]
    pending = []

    def exchange(source, target, device, landing):
        index = counter[0]
        counter[0] += 1
        made = Exchange(
            source, target, device, landing, send_sems.at[index], recv_sems.at[index]
        )
        pending.append(made)
        return made

    local_counter = [0]

    def kept(source, target):
        made = Kept(source, target, local_sems.at[local_counter[0]])
        local_counter[0] += 1
        pending.append(made)
        return made

    barrier = pltpu.get_barrier_semaphore()
    peers = [(f, hz[d], t) for d in range(1, H)] + [(f, h, s)]
    peers += [(fx[d], h, c) for d in range(1, 4) for c in (t, s)]
    for peer in peers:
        pl.semaphore_signal(barrier, inc=1, device_id=peer, device_id_type=MESH)

    for i in range(3):
        wbuf[i, h, t, :, whole(f, 128)] = wq[i]
    wbuf[3, h, t, :, whole(f, 128)] = wo[...]
    pl.semaphore_wait(barrier, len(peers))

    first = [
        exchange(*[wbuf.at[:, h, t, :, whole(f, 128)]] * 2, (f, hz[d], t),
                 wbuf.at[:, hfrom[d], t, :, whole(f, 128)])
        for d in range(1, H)
    ]

    row_index = lax.broadcasted_iota(jnp.int32, (ROWS, 1), 0)

    def image(source, b):
        if b == 0:
            stage[0 : images * SEQ, :] = source[...].astype(F32)
        return jnp.where(row_index < SEQ, stage[b * SEQ : b * SEQ + ROWS, :], 0.0)

    for b in range(images):
        live = ((h * 2 + t) * images + b < counts[0]).astype(F32)
        rows_grad[h * 2 + t, b * ROWS : (b + 1) * ROWS, :] = (image(cot, b) * live).astype(BF16)

    parts = [slice(0, own // 2), slice(own // 2, own)]

    def hop(rows, line, part, to, source):
        here = rows.at[line * 2 + t, parts[part]]
        return exchange(here, here, (f, to, t), rows.at[source * 2 + t, parts[part]])

    def beside(rows, line):
        here = rows.at[line * 2 + t, 0:own]
        return exchange(here, here, (f, h, s), rows.at[line * 2 + s, 0:own])

    class Spread:
        def __init__(self, rows):
            self.rows = rows
            self.down = [hop(rows, h, 0, after, before), None]
            self.up = [None, hop(rows, h, 1, before, after)]
            self.down[1] = hop(rows, h, 1, after, before)
            self.up[0] = hop(rows, h, 0, before, after)
            self.near = [beside(rows, h)]

        def relay(self):
            self.down[0].arrived()
            self.far = [hop(self.rows, before, 0, after, across)]
            self.up[1].arrived()
            self.far.append(hop(self.rows, after, 1, before, across))

        def share(self):
            self.down[1].arrived()
            self.near.append(beside(self.rows, before))
            self.up[0].arrived()
            self.near.append(beside(self.rows, after))

        def close(self):
            for move in self.far:
                move.arrived()
            self.near.append(beside(self.rows, across))

        def blocks(self):
            lines = [h, before, after, across]
            return [(line * 2 + t, None) for line in lines] + [
                (line * 2 + s, move) for line, move in zip(lines, self.near)
            ]

        def sent(self):
            for move in self.down + self.up + self.far + self.near:
                move.sent()

    for b in range(images):
        unit, _ = normal_parts(image(tokens, b))
        normed[b * ROWS : (b + 1) * ROWS, :] = (unit * gain[0:1] + bias[0:1]).astype(BF16)

    for step in first:
        step.arrived()
    grad_spread = Spread(rows_grad)
    second = [
        exchange(*[wbuf.at[:, :, t, :, whole(f, 128)]] * 2, (fx[d], h, t),
                 wbuf.at[:, :, t, :, whole(fx[d], 128)])
        for d in range(1, 4)
    ]

    def mark_slots(b):
        for part in range(4):
            spot = lax.broadcasted_iota(jnp.int32, (CAP, own), 0) + CAP * part
            named = (prow[b, 0:1, 0:own] == spot) | (prow[b, 1:2, 0:own] == spot)
            big[b, part * CAP : (part + 1) * CAP, 0:own] = jnp.where(named, 1.0, 0.0).astype(BF16)

    pl.loop(0, H)(mark_slots)
    grad_spread.relay()
    pl.loop(H, 2 * H)(mark_slots)
    for step in second:
        step.arrived()
    third = exchange(*[wbuf.at[:, :, t]] * 2, (f, h, s), wbuf.at[:, :, s])

    expert_moves = []
    depth, span = win_hbm.shape[1], win_hbm.shape[2]
    mine = [
        kept(win_hbm.at[f * 2 + t], win.at[whole(f, depth), whole(t, span)]),
        kept(wback_hbm.at[f * 2 + t], wback.at[whole(t, span), whole(f, depth)]),
    ]
    for d in range(0, 4):
        for c in (t, s) if d else (s,):
            target = win.at[whole(f, depth), whole(t, span)]
            landing = win.at[whole(fx[d], depth), whole(c, span)]
            device = (fx[d], h, c)
            expert_moves.append(exchange(win_hbm.at[fx[d] * 2 + c], target, device, landing))
            target = wback.at[whole(t, span), whole(f, depth)]
            landing = wback.at[whole(c, span), whole(fx[d], depth)]
            expert_moves.append(exchange(wback_hbm.at[fx[d] * 2 + c], target, device, landing))

    grad_spread.share()
    third.arrived()

    for i in range(3):
        part = mm(normed[...], wbuf[i].reshape(width, width), NT)
        if i == 0:
            part = part * HEAD ** (-0.5)
        qkv[:, i * width : (i + 1) * width] = part.astype(BF16)
    lane = lax.broadcasted_iota(jnp.int32, (1, 128), 1)
    sides = [jnp.where(lane < HEAD, 1.0, 0.0).astype(BF16), jnp.where(lane < HEAD, 0.0, 1.0).astype(BF16)]
    key_index = lax.broadcasted_iota(jnp.int32, (1, ROWS), 1)

    def pair_of(index):
        b, pair = index // half, lax.rem(index, half)
        rows = whole(b, ROWS)
        cols = [whole(pair + i * half, 128) for i in range(3)]
        return rows, cols

    @pl.loop(0, images * half)
    def _(index):
        rows, cols = pair_of(index)
        query, key, value = (qkv[rows, col] for col in cols)
        total = jnp.zeros((ROWS, 128), F32)
        for side in range(2):
            score = mm(query * sides[side], key, NT)
            score = jnp.where(key_index < SEQ, score, -1e30)
            score = jnp.exp(score - jnp.max(score, axis=-1, keepdims=True))
            prob = score / jnp.sum(score, axis=-1, keepdims=True)
            probs[index * 2 + side] = prob
            total += mm(prob.astype(BF16), value * sides[side])
        mixed[rows, cols[0]] = total.astype(BF16)

    for b in range(images):
        rows = slice(b * ROWS, (b + 1) * ROWS)
        value = image(tokens, b) + mm(mixed[rows, :], wbuf[3].reshape(width, width))
        middle[rows, :] = value
        unit, _ = normal_parts(value)
        rows_norm[h * 2 + t, rows, :] = (unit * gain[1:2] + bias[1:2]).astype(BF16)

    norm_spread = Spread(rows_norm)
    grad_spread.close()

    def accumulate(rows, b, begin):
        for part in range(4):
            span_rows = slice(part * CAP, (part + 1) * CAP)
            value = mm(big[b, span_rows, 0:own], rows[b, 0:own])
            wide[span_rows, :] = value if begin else wide[span_rows, :] + value

    def accumulate_all(spread, begin, end):
        for place, (b, move) in list(enumerate(spread.blocks()))[begin:end]:
            if move is not None:
                move.arrived()
            accumulate(spread.rows, b, place == 0)

    def pack(send):
        for part in range(4):
            send[part] = wide[part * CAP : (part + 1) * CAP, :].astype(BF16)

    def dispatch(send, landing):
        moved = [
            exchange(send.at[fx[d]], landing.at[f], (fx[d], h, t), landing.at[fx[d]])
            for d in range(1, 4)
        ]
        return [kept(send.at[f], landing.at[f])] + moved

    accumulate_all(grad_spread, 0, 4)
    norm_spread.relay()
    accumulate_all(grad_spread, 4, 8)
    pack(gsend)
    norm_spread.share()
    accumulate_all(norm_spread, 0, 3)
    norm_spread.close()
    accumulate_all(norm_spread, 3, 8)
    pack(xsend)
    norm_moved = dispatch(xsend, xrows)

    expert = h * local_count + f * 2 + t
    router_lane = lax.broadcasted_iota(jnp.int32, (1, wr.shape[0]), 1)
    chosen = (router_lane == expert).astype(F32)
    chunk = 512
    chunks = win.shape[1] // chunk
    for move in mine + expert_moves:
        move.arrived()

    def forward(group):
        here = whole(group, CAP)
        rows = xrows[group]
        result = jnp.zeros((CAP, width), F32)
        for c in range(chunks):
            value, slope = gelu_parts(mm(rows, win[:, c * chunk : (c + 1) * chunk]))
            value = value.astype(BF16)
            big[c, here, :] = value
            big[4 + c, here, :] = slope.astype(BF16)
            result += mm(value, wback[c * chunk : (c + 1) * chunk, :])
        wide[whole(4 + group, CAP), :] = result

    grad_moved = []
    for d in range(4):
        norm_moved[d].arrived()
        if d == 1:
            grad_moved = dispatch(gsend, grows)
        forward(fx[d])

    for move in norm_moved:
        move.sent()

    def backward(group):
        here = whole(group, CAP)
        rows = xrows[group]
        result = wide[whole(4 + group, CAP), :]
        logits = mm(rows, wr[...], NT)
        odds = jnp.exp(logits - jnp.max(logits, axis=-1, keepdims=True))
        odds = odds / jnp.sum(odds, axis=-1, keepdims=True)
        gate = jnp.sum(odds * chosen, axis=-1, keepdims=True)
        row_grad = grows[group].astype(F32)
        gate_grad = jnp.sum(row_grad * result, axis=-1, keepdims=True)
        wide[whole(4 + group, CAP), :] = gate * result
        result_grad = (gate * row_grad).astype(BF16)
        grows[group] = result_grad
        logit = (gate_grad * gate * (chosen - odds)).astype(BF16)
        logit_grad[here, :] = logit
        total = mm(logit, wr[...])
        for c in range(chunks):
            grad = mm(result_grad, wback[c * chunk : (c + 1) * chunk, :], NT)
            grad = (grad * big[4 + c, here, :].astype(F32)).astype(BF16)
            big[4 + c, here, :] = grad
            total += mm(grad, win[:, c * chunk : (c + 1) * chunk], NT)
        xsend[group] = total.astype(BF16)

    back_moves = []
    for d in range(4):
        grad_moved[d].arrived()
        backward(fx[d])
        if d:
            back_moves.append(
                exchange(xsend.at[fx[d]], xback.at[f], (fx[d], h, t), xback.at[fx[d]])
            )
        else:
            back_moves.append(kept(xsend.at[f], xback.at[f]))

    grad_spread.sent()
    norm_spread.sent()
    flat_rows = xrows[...].reshape(4 * CAP, width)
    flat_grad = grows[...].reshape(4 * CAP, width)
    for c in range(chunks):
        rows_grad[c] = mm(flat_rows, big[4 + c], TN).astype(BF16)
        rows_norm[c] = mm(big[c], flat_grad, TN).astype(BF16)
    route = mm(logit_grad[...], flat_rows, TN)
    share_rows = wr.shape[0] // 8
    for j in range(8):
        route_out[j, 0:share_rows, :] = route[j * share_rows : (j + 1) * share_rows]

    for move in grad_moved:
        move.sent()
    for group in range(4):
        gsend[group] = wide[(4 + group) * CAP : (5 + group) * CAP, :].astype(BF16)
    for move in back_moves:
        move.arrived()
    out_moves = dispatch(gsend, gback)

    def to_owners():
        halves = chunks // 2
        for d in range(4):
            for c in (t, s):
                device = (fx[d], h, c)
                for part in range(halves):
                    span_part = slice(part * chunk, (part + 1) * chunk)
                    source_in = rows_grad.at[c * halves + part, whole(fx[d], depth), :]
                    source_back = rows_norm.at[c * halves + part, :, whole(fx[d], depth)]
                    target_in = gin_out.at[f * 2 + t, :, span_part]
                    target_back = gback_out.at[f * 2 + t, span_part]
                    if d == 0 and c is t:
                        kept(source_in, target_in)
                        kept(source_back, target_back)
                        continue
                    exchange(source_in, target_in, device, gin_out.at[fx[d] * 2 + c, :, span_part])
                    exchange(source_back, target_back, device, gback_out.at[fx[d] * 2 + c, span_part])

    plane_peers = [(d, c) for d in range(4) for c in ((t, s) if d else (s,))]
    route_kept = kept(route_out.at[f * 2 + t], route_in.at[f * 2 + t])
    route_moves = [
        exchange(route_out.at[fx[d] * 2 + c], route_in.at[f * 2 + t], (fx[d], h, c), route_in.at[fx[d] * 2 + c])
        for d, c in plane_peers
    ]

    def share(b, back):
        spots = jnp.transpose(prow[b])[0:own]
        slot = lax.broadcasted_iota(jnp.int32, (own, 4 * CAP), 1)
        named = (spots[:, 0:1] == slot) | (spots[:, 1:2] == slot)
        return mm(jnp.where(named, 1.0, 0.0).astype(BF16), back[...].reshape(4 * CAP, width))

    class Gather:
        def __init__(self, which, back, near_out, far_out):
            self.which, self.back = which, back
            self.near_out, self.far_out = near_out, far_out
            self.lines = [across, after, before, h]
            self.near = []

        def give(self, place):
            line = self.lines[place]
            self.near_out(place)[...] = share(line * 2 + s, self.back).astype(BF16)
            landing = sib_in.at[self.which, place]
            self.near.append(exchange(self.near_out(place), landing, (f, h, s), landing))

        def take(self, place):
            value = share(self.lines[place] * 2 + t, self.back)
            self.near[place].arrived()
            value = value + sib_in[self.which, place].astype(F32)
            if place == 3:
                own_sum[self.which] = value
            else:
                self.far_out(place)[...] = value.astype(BF16)

        def hop(self, place, part, to, slot):
            landing = z_in.at[self.which, slot, parts[part]]
            return exchange(self.far_out(place).at[parts[part]], landing, (f, to, t), landing)

        def start(self):
            self.first = [self.hop(0, 0, after, 0), self.hop(0, 1, before, 0)]

        def direct(self, place):
            part, to = ((1, after), (0, before))[place - 1]
            self.last = getattr(self, "last", []) + [self.hop(place, part, to, place)]

        def relay(self):
            for place, part, to in ((1, 0, after), (2, 1, before)):
                self.first[part].arrived()
                rows = self.far_out(place).at[parts[part]]
                passed = z_in[self.which, 0, parts[part], :].astype(F32)
                rows[...] = (rows[...].astype(F32) + passed).astype(BF16)
                self.last.append(self.hop(place, part, to, place))

        def total(self, rows):
            for move in self.last:
                move.arrived()
            total = own_sum[self.which, rows, :]
            for slot in (1, 2):
                total = total + z_in[self.which, slot, rows, :].astype(F32)
            return total

    norm_sums = Gather(0, xback, lambda place: sib_out.at[place], lambda place: z_out.at[place])
    norm_sums.give(0)
    norm_sums.give(1)
    norm_sums.take(0)
    norm_sums.start()
    norm_sums.give(2)
    norm_sums.take(1)
    norm_sums.direct(1)
    norm_sums.take(2)
    norm_sums.direct(2)
    norm_sums.give(3)
    norm_sums.take(3)
    to_owners()
    norm_sums.relay()

    route_kept.arrived()
    for move in route_moves:
        move.arrived()
    route = route_in[0, 0:share_rows, :]
    for j in range(1, 8):
        route = route + route_in[j, 0:share_rows, :]
    route_z[h, 0:share_rows, :] = route
    route_line = [
        exchange(route_z.at[h], route_z.at[h], (f, hz[d], t), route_z.at[hfrom[d]]) for d in range(1, H)
    ]

    for move in out_moves:
        move.arrived()
    out_sums = Gather(
        1, gback, lambda place: big.at[place, 0:own], lambda place: big.at[4 + place, 0:own]
    )
    for place in range(4):
        out_sums.give(place)
    for place in range(4):
        out_sums.take(place)

    for move in norm_sums.last:
        move.arrived()
    out_sums.start()
    out_sums.direct(1)
    out_sums.direct(2)
    small_c[t] = jnp.zeros(small_c.shape[1:], F32)
    for b in range(images):
        rows = slice(b * ROWS, (b + 1) * ROWS)
        grad = norm_sums.total(rows)
        unit, scale = normal_parts(middle[rows, :])
        small_c[t, 1:2] += jnp.sum(grad * unit, axis=0, keepdims=True)
        small_c[t, 3:4] += jnp.sum(grad, axis=0, keepdims=True)
        live = ((h * 2 + t) * images + b < counts[0]).astype(F32)
        grad = normal_pull(grad, unit, scale, gain[1:2]) + image(cot, b) * live
        grad_mid[rows, :] = grad

    for move in back_moves:
        move.sent()
    low = grad_mid[...].astype(BF16)
    count = H * 2 * 64
    wide[3 * count : 4 * count, :] = mm(mixed[...], low, TN)
    mixed[...] = mm(low, wbuf[3].reshape(width, width), NT).astype(BF16)

    @pl.loop(0, images * half)
    def _(index):
        rows, cols = pair_of(index)
        query, key, value = (qkv[rows, col] for col in cols)
        pulled = mixed[rows, cols[0]]
        grads = [jnp.zeros((ROWS, 128), F32) for _ in range(3)]
        for side in range(2):
            prob = probs[index * 2 + side]
            one = pulled * sides[side]
            prob_grad = mm(one, value, NT)
            grads[2] += mm(prob.astype(BF16), one, TN)
            inner = jnp.sum(prob * prob_grad, axis=-1, keepdims=True)
            score_grad = (prob * (prob_grad - inner)).astype(BF16)
            grads[0] += mm(score_grad, key * sides[side])
            grads[1] += mm(score_grad, query * sides[side], TN)
        grads[0] = grads[0] * HEAD ** (-0.5)
        for grad, col in zip(grads, cols):
            qkv[rows, col] = grad.astype(BF16)

    out_sums.relay()
    for i in range(3):
        wide[i * count : (i + 1) * count, :] = mm(
            qkv[:, i * width : (i + 1) * width], normed[...], TN
        )

    def wide_rows(i, other, core):
        return whole((i * H + other) * 2 + core, 64)

    for i in range(4):
        for other in range(H):
            xsend[i, other * 64 : (other + 1) * 64, :] = wide[wide_rows(i, other, s), :].astype(BF16)
    att_out = xsend.at[:, 0 : H * 64]
    att_near = exchange(att_out, att_in, (f, h, s), att_in)

    for b in range(images):
        rows = slice(b * ROWS, (b + 1) * ROWS)
        grad = jnp.zeros((ROWS, width), F32)
        for i in range(3):
            grad += mm(qkv[rows, i * width : (i + 1) * width], wbuf[i].reshape(width, width))
        unit, scale = normal_parts(image(tokens, b))
        small_c[t, 0:1] += jnp.sum(grad * unit, axis=0, keepdims=True)
        small_c[t, 2:3] += jnp.sum(grad, axis=0, keepdims=True)
        grad = normal_pull(grad, unit, scale, gain[0:1]) + grad_mid[rows, :]
        tgrad[b * SEQ : (b + 1) * SEQ, :] = grad[0:SEQ]
    small_near = exchange(small_c.at[t], small_c.at[t], (f, h, s), small_c.at[s])

    att_near.arrived()
    att_near.sent()
    for i in range(4):
        for other in range(H):
            here = wide_rows(i, other, t)
            here_low = slice(other * 64, (other + 1) * 64)
            value = wide[here, :] + att_in[i, here_low, :].astype(F32)
            wide[here, :] = value
            xsend[i, here_low, :] = value.astype(BF16)
    plane = [
        exchange(xsend.at[:, 0 : H * 64, whole(fx[d], 128)], plane_in.at[f], (fx[d], h, t), plane_in.at[fx[d]])
        for d in range(1, 4)
    ]
    small_near.arrived()
    small_p[f] = small_c[0] + small_c[1]
    small_plane = [
        exchange(small_p.at[f], small_p.at[f], (fx[d], h, t), small_p.at[fx[d]]) for d in range(1, 4)
    ]
    for move in route_line:
        move.arrived()
    route = route_z[0]
    for d in range(1, H):
        route = route + route_z[d]
    route_all[f * 2 + t] = route
    route_last = [
        exchange(route_all.at[f * 2 + t], route_all.at[f * 2 + t], (fx[d], h, c), route_all.at[fx[d] * 2 + c])
        for d, c in plane_peers
    ]

    for b in range(images):
        rows = slice(b * ROWS, (b + 1) * ROWS)
        value = middle[rows, :] + out_sums.total(rows)
        stage[b * SEQ : (b + 1) * SEQ, :] = value[0:SEQ]
    out[...] = stage[0 : images * SEQ, :].astype(BF16)

    for move in plane:
        move.arrived()
    for i in range(4):
        for other in range(H):
            value = wide[wide_rows(i, other, t), whole(f, 128)]
            for d in range(1, 4):
                value = value + plane_in[fx[d], i, other * 64 : (other + 1) * 64, :].astype(F32)
            wide[wide_rows(i, other, t), 0:128] = value
            line_out[other, i] = value.astype(BF16)
    line = [
        exchange(line_out.at[hz[d]], line_in.at[h], (f, hz[d], t), line_in.at[hfrom[d]])
        for d in range(1, H)
    ]
    for move in small_plane:
        move.arrived()
    small_z[h] = (small_p[0] + small_p[1]) + (small_p[2] + small_p[3])
    small_line = [
        exchange(small_z.at[h], small_z.at[h], (f, hz[d], t), small_z.at[hfrom[d]]) for d in range(1, H)
    ]
    for move in route_last:
        move.arrived()
    for j in range(8):
        wrg[j * share_rows : (j + 1) * share_rows, :] = route_all[j, 0:share_rows, :]

    for move in line:
        move.arrived()
    for i in range(4):
        value = wide[wide_rows(i, h, t), 0:128]
        for d in range(1, H):
            value = value + line_in[hfrom[d], i].astype(F32)
        if i < 3:
            wqg[i] = value
        else:
            wog[...] = value
    for move in small_line:
        move.arrived()
    total = small_z[0]
    for d in range(1, H):
        total = total + small_z[d]
    lng[...] = total[0:2]
    lnb[...] = total[2:4]

    for move in pending:
        move.finish()


def expert_specs(depth, span):
    return [
        pl.BlockSpec((1, depth, span), lambda step: (step, 0, 0)),
        pl.BlockSpec((1, span, depth), lambda step: (step, 0, 0)),
    ]


def finish_kernel(*refs):
    sources, targets = refs[:9], refs[9:]

    @pl.when(pl.program_id(0) == 0)
    def _():
        for i in range(7):
            targets[i][...] = sources[i][...]

    for i in (7, 8):
        targets[i][...] = sources[i][...].astype(F32)


def fast_device(
    tokens,
    cotangent,
    image_counts,
    w_qkv,
    w_out,
    ln_gain,
    ln_bias,
    w_router,
    w_in,
    w_back,
    expert_ids,
    slots,
):
    H = lax.axis_size("heads")
    own_rows, width = tokens.shape
    images = own_rows // SEQ
    own = images * ROWS
    local_count, depth, span = w_in.shape[1:]
    experts = w_router.shape[2]
    hidden = span * 2
    core = lax.axis_index("tensor")

    relative = expert_ids[0] - lax.axis_index("heads") * local_count
    wanted = (slots[0] >= 0) & (relative >= 0) & (relative < local_count) & (relative % 2 == core)
    places = jnp.where(wanted, (relative // 2) * CAP + slots[0], -1)
    places = jnp.transpose(places).reshape(2, 2 * H, images, SEQ)
    places = jnp.pad(places, ((0, 0), (0, 0), (0, 0), (0, ROWS - SEQ)), constant_values=-1)
    places = jnp.transpose(places.reshape(2, 2 * H, own), (1, 0, 2))
    places = jnp.pad(places, ((0, 0), (0, 6), (0, width - own)), constant_values=-1)

    vmem = pl.BlockSpec(memory_space=pltpu.VMEM)
    smem = pl.BlockSpec(memory_space=pltpu.SMEM)
    anywhere = pl.BlockSpec(memory_space=pl.ANY)
    shape = jax.ShapeDtypeStruct

    def low(*dims):
        return pltpu.VMEM(dims, BF16)

    def full(*dims):
        return pltpu.VMEM(dims, F32)

    outs = pl.pallas_call(
        lambda *refs: block_kernel(H, images, local_count, refs),
        out_shape=(
            shape((own_rows, width), BF16),
            shape((own_rows, width), F32),
            shape((3, 64, depth), F32),
            shape((64, depth), F32),
            shape((2, width), F32),
            shape((2, width), F32),
            shape((experts, width), F32),
            shape((local_count, depth, span), BF16),
            shape((local_count, span, depth), BF16),
        ),
        in_specs=[vmem, vmem, smem, vmem, vmem, vmem, vmem, vmem, anywhere, anywhere, vmem],
        out_specs=[vmem] * 7 + [anywhere] * 2,
        scratch_shapes=[
            full(images * SEQ + 16, width),
            low(4, H, 2, 64, width),
            low(width, hidden),
            low(hidden, width),
            low(2 * H, 512, width),
            low(2 * H, 512, width),
            low(8, 4 * CAP, 512),
            full(8 * CAP, width),
            low(4, CAP, width),
            low(4, CAP, width),
            low(4, CAP, width),
            low(4, CAP, width),
            low(4, CAP, width),
            low(4, CAP, width),
            low(own, width),
            low(own, 3 * width),
            full(images * width // HEAD, ROWS, ROWS),
            low(own, width),
            full(own, width),
            full(own, width),
            low(4 * CAP, experts),
            low(H, own, width),
            low(2, H, own, width),
            low(3, own, width),
            low(2, 3, own, width),
            full(2, own, width),
            low(4, H * 64, width),
            low(4, 4, H * 64, 128),
            low(H, 4, 64, 128),
            low(H, 4, 64, 128),
            full(2, 8, width),
            full(4, 8, width),
            full(H, 8, width),
            full(8, 8, width),
            full(8, 8, width),
            full(H, 8, width),
            full(8, 8, width),
            pltpu.SemaphoreType.DMA((192,)),
            pltpu.SemaphoreType.DMA((192,)),
            pltpu.SemaphoreType.DMA((16,)),
        ],
        compiler_params=pltpu.CompilerParams(
            collective_id=0, has_side_effects=True, vmem_limit_bytes=62 * 2**20
        ),
        name="block",
    )(
        tokens, cotangent, image_counts, jnp.transpose(w_qkv[0], (0, 2, 1)), w_out[0], ln_gain[0], ln_bias[0],
        jnp.transpose(w_router[0]),
        w_in[0], w_back[0], places,
    )
    small = [pl.BlockSpec(part.shape, lambda step, n=part.ndim: (0,) * n) for part in outs[:7]]
    outs = pl.pallas_call(
        finish_kernel,
        grid=(local_count,),
        out_shape=[shape(part.shape, F32 if i >= 7 else part.dtype) for i, part in enumerate(outs)],
        in_specs=small + expert_specs(depth, span),
        out_specs=small + expert_specs(depth, span),
        name="finish",
    )(*outs)
    block_out, token_grad, qkv_grad, out_grad, gains, shifts, router, in_grad, back_grad = outs
    return (
        block_out,
        token_grad,
        jnp.transpose(qkv_grad, (0, 2, 1))[None],
        out_grad[None],
        gains[None],
        shifts[None],
        jnp.transpose(router)[None],
        in_grad[None],
        back_grad[None],
    )


def solution(mesh):
    def program(*arrays):
        sizes = dict(mesh.shape)
        devices = sizes["fsdp"] * sizes["heads"] * sizes["tensor"]
        own_rows = arrays[0].shape[0] // devices
        one_expert = sizes["fsdp"] == 4 and sizes["tensor"] == 2 and arrays[8].shape[1] == devices
        one_expert = one_expert and sizes["heads"] == 4 and own_rows % (2 * SEQ) == 0
        return placed(mesh, fast_device if one_expert else on_device)(*arrays)

    return program


def placed(mesh, on_device):
    return jax.shard_map(
        on_device,
        mesh=mesh,
        in_specs=(
            P(("fsdp", "heads", "tensor"), None),
            P(("fsdp", "heads", "tensor"), None),
            P("fsdp"),
            P(None, None, "fsdp", ("heads", "tensor")),
            P(None, ("heads", "tensor"), "fsdp"),
            P(),
            P(),
            P(),
            P(None, "heads", "fsdp", "tensor"),
            P(None, "heads", "tensor", "fsdp"),
            P(None, "fsdp", None),
            P(None, "fsdp", None),
        ),
        out_specs=(
            P(("fsdp", "heads", "tensor"), None),
            P(("fsdp", "heads", "tensor"), None),
            P(None, None, "fsdp", ("heads", "tensor")),
            P(None, ("heads", "tensor"), "fsdp"),
            P(),
            P(),
            P(),
            P(None, "heads", "fsdp", "tensor"),
            P(None, "heads", "tensor", "fsdp"),
        ),
        check_vma=False,
    )
```

```python
import jax
import jax.numpy as jnp
from jax import lax
from jax.experimental import pallas as pl
from jax.experimental.pallas import tpu as pltpu
from jax.sharding import PartitionSpec as P

HEAD = 64
SEQ = 197
LAYERS = 1
CAP = 256


def layer_norm(value, ln_gains, ln_shift):
    centred = value - jnp.mean(value, axis=-1, keepdims=True)
    spread = jnp.mean(centred * centred, axis=-1, keepdims=True)
    return centred * lax.rsqrt(spread + 1e-06) * ln_gains + ln_shift


def gelu_exact(value):
    return jax.nn.gelu(value, approximate=False)


def with_zero_row(matrix):
    return jnp.concatenate([matrix, jnp.zeros((1,) + matrix.shape[1:], matrix.dtype)], axis=0)


def slot_tables(named_expert, slot_rows, first_expert, local_experts):
    group_rows = named_expert.shape[0]
    is_local = (
        (slot_rows >= 0)
        & (named_expert >= first_expert)
        & (named_expert < first_expert + local_experts)
    )
    places = jnp.where(
        is_local, (named_expert - first_expert) * CAP + slot_rows, local_experts * CAP
    )
    picked = jnp.full((local_experts * CAP + 1,), 2 * group_rows, jnp.int32)
    picked = picked.at[places.reshape(-1)].set(jnp.arange(2 * group_rows, dtype=jnp.int32))
    return (places, picked[: local_experts * CAP])


def joined_qkv(qkv_weight):
    head_cols = qkv_weight.shape[2]
    return jnp.transpose(qkv_weight, (1, 0, 2)).reshape(qkv_weight.shape[1], 3 * head_cols)


def forward_block(
    residual, weights, ln_gains, ln_shift, router_weight, named_expert, slot_rows, first_expert
):
    qkv_weight, out_weight, in_weight, back_weight = weights
    own_rows, widths = residual.shape
    group_rows = named_expert.shape[0]
    head_cols = qkv_weight.shape[2]
    local_experts = in_weight.shape[0]
    head_shape = (group_rows // SEQ, SEQ, head_cols // HEAD, HEAD)
    q_scale = HEAD ** (-0.5)
    flat_qkv = joined_qkv(qkv_weight)
    normed_rows = layer_norm(residual, ln_gains[0], ln_shift[0]).astype(jnp.bfloat16)
    normed = lax.all_gather(normed_rows, ("heads", "tensor"), axis=0, tiled=True)
    projected = jnp.dot(normed, flat_qkv, preferred_element_type=jnp.float32)
    queries = (projected[:, :head_cols] * q_scale).astype(jnp.bfloat16).reshape(head_shape)
    key_rows = projected[:, head_cols : 2 * head_cols].astype(jnp.bfloat16).reshape(head_shape)
    value_rows = projected[:, 2 * head_cols :].astype(jnp.bfloat16).reshape(head_shape)
    scores = jnp.einsum("bqhd,bkhd->bhqk", queries, key_rows, preferred_element_type=jnp.float32)
    log_total = jax.nn.logsumexp(scores, axis=-1)
    attn_probs = jax.nn.softmax(scores, axis=-1).astype(jnp.bfloat16)
    mixed_rows = jnp.einsum(
        "bhqk,bkhd->bqhd", attn_probs, value_rows, preferred_element_type=jnp.float32
    )
    mixed_rows = mixed_rows.reshape(group_rows, head_cols).astype(jnp.bfloat16)
    middle = residual + lax.psum_scatter(
        jnp.dot(mixed_rows, out_weight, preferred_element_type=jnp.float32),
        ("heads", "tensor"),
        scatter_dimension=0,
        tiled=True,
    )
    head_full = ()
    normed_two_rows = layer_norm(middle, ln_gains[1], ln_shift[1]).astype(jnp.bfloat16)
    normed_two = lax.all_gather(normed_two_rows, ("heads", "tensor"), axis=0, tiled=True)
    router = jax.nn.softmax(
        jnp.dot(normed_two, router_weight, preferred_element_type=jnp.float32), axis=-1
    )
    gate_values = jnp.take_along_axis(router, named_expert, axis=1) * (slot_rows >= 0)
    places, picked = slot_tables(named_expert, slot_rows, first_expert, local_experts)
    routed = with_zero_row(normed_two)[picked // 2].reshape(local_experts, CAP, widths)
    hidden = jnp.einsum("ecd,edf->ecf", routed, in_weight, preferred_element_type=jnp.float32)
    active = gelu_exact(hidden).astype(jnp.bfloat16)
    result = jnp.einsum("ecf,efd->ecd", active, back_weight, preferred_element_type=jnp.float32)
    flat_result = with_zero_row(result.reshape(local_experts * CAP, widths))
    block_out = middle + lax.psum_scatter(
        (
            flat_result[places[:, 0]] * gate_values[:, 0:1]
            + flat_result[places[:, 1]] * gate_values[:, 1:2]
        ).astype(jnp.bfloat16),
        ("heads", "tensor"),
        scatter_dimension=0,
        tiled=True,
    ).astype(jnp.float32)
    stored = (
        residual,
        middle,
        normed,
        queries,
        key_rows,
        value_rows,
        log_total,
        mixed_rows,
        normed_two_rows,
        router,
        gate_values,
        places,
        picked,
        routed,
        hidden,
        active,
        flat_result,
    )
    return (block_out, stored, head_full)


def backward_block(
    grad_rows, stored, weights, ln_gains, ln_shift, router_weight, named_expert, row_start
):
    qkv_weight, out_weight, in_weight, back_weight = weights
    (
        residual,
        middle,
        normed,
        queries,
        key_rows,
        value_rows,
        log_total,
        mixed_rows,
        normed_two_rows,
        router,
        gate_values,
        places,
        picked,
        routed,
        hidden,
        active,
        flat_result,
    ) = stored
    own_rows, widths = residual.shape
    group_rows = named_expert.shape[0]
    head_cols = qkv_weight.shape[2]
    local_experts = in_weight.shape[0]
    expert_count = router.shape[1]
    q_scale = HEAD ** (-0.5)
    flat_qkv = joined_qkv(qkv_weight)
    grad_moe = lax.all_gather(
        grad_rows.astype(jnp.bfloat16), ("heads", "tensor"), axis=0, tiled=True
    )
    back_rows = with_zero_row(grad_moe)[picked // 2].astype(jnp.float32)
    gate_slots = with_zero_row(gate_values.reshape(-1))[picked]
    gate_grad_slots = jnp.sum(back_rows * flat_result[:-1], axis=1)
    gate_grads = with_zero_row(gate_grad_slots)[places]
    expert_range = jnp.arange(expert_count, dtype=jnp.int32)
    router_part = jnp.sum(
        gate_grads[:, :, None]
        * (named_expert[:, :, None] == expert_range[None, None, :]).astype(jnp.float32),
        axis=1,
    )
    grad_result = (
        (gate_slots[:, None] * back_rows).astype(jnp.bfloat16).reshape(local_experts, CAP, widths)
    )
    grad_active = jnp.einsum(
        "ecd,efd->ecf", grad_result, back_weight, preferred_element_type=jnp.float32
    )
    gelu_value, gelu_pull = jax.vjp(gelu_exact, hidden)
    grad_hidden = gelu_pull(grad_active)[0].astype(jnp.bfloat16)
    back_grad = jnp.einsum("ecf,ecd->efd", active, grad_result, preferred_element_type=jnp.float32)
    in_grad = jnp.einsum("ecd,ecf->edf", routed, grad_hidden, preferred_element_type=jnp.float32)
    grad_routed = jnp.einsum(
        "ecf,edf->ecd", grad_hidden, in_weight, preferred_element_type=jnp.float32
    )
    grad_routed = with_zero_row(grad_routed.reshape(local_experts * CAP, widths))
    token_part = grad_routed[places[:, 0]] + grad_routed[places[:, 1]]
    grad_normed_two, router_rows = (
        lax.psum_scatter(token_part, ("heads", "tensor"), scatter_dimension=0, tiled=True),
        lax.psum_scatter(router_part, ("heads", "tensor"), scatter_dimension=0, tiled=True),
    )
    router_own = lax.dynamic_slice_in_dim(router, row_start, own_rows, 0)
    grad_logits = (
        router_own * (router_rows - jnp.sum(router_own * router_rows, axis=-1, keepdims=True))
    ).astype(jnp.bfloat16)
    router_grad = jnp.einsum(
        "td,te->de", normed_two_rows, grad_logits, preferred_element_type=jnp.float32
    )
    grad_normed_two = grad_normed_two + jnp.einsum(
        "te,de->td", grad_logits, router_weight, preferred_element_type=jnp.float32
    )
    norm_value, norm_pull = jax.vjp(layer_norm, middle, ln_gains[1], ln_shift[1])
    grad_middle, gain_two, shift_two = norm_pull(grad_normed_two)
    grad_middle = grad_middle + grad_rows
    grad_attn = lax.all_gather(
        grad_middle.astype(jnp.bfloat16), ("heads", "tensor"), axis=0, tiled=True
    )
    out_grad = jnp.einsum("tc,td->cd", mixed_rows, grad_attn, preferred_element_type=jnp.float32)
    grad_mixed = jnp.einsum("td,cd->tc", grad_attn, out_weight, preferred_element_type=jnp.float32)
    grad_mixed = grad_mixed.astype(jnp.bfloat16).reshape(queries.shape)
    scores = jnp.einsum("bqhd,bkhd->bhqk", queries, key_rows, preferred_element_type=jnp.float32)
    attn_probs = jnp.exp(scores - log_total[..., None])
    grad_values = jnp.einsum(
        "bhqk,bqhd->bkhd",
        attn_probs.astype(jnp.bfloat16),
        grad_mixed,
        preferred_element_type=jnp.float32,
    )
    grad_probs = jnp.einsum(
        "bqhd,bkhd->bhqk", grad_mixed, value_rows, preferred_element_type=jnp.float32
    )
    grad_scores = (
        attn_probs * (grad_probs - jnp.sum(attn_probs * grad_probs, axis=-1, keepdims=True))
    ).astype(jnp.bfloat16)
    grad_queries = jnp.einsum(
        "bhqk,bkhd->bqhd", grad_scores, key_rows, preferred_element_type=jnp.float32
    )
    grad_keys = jnp.einsum(
        "bhqk,bqhd->bkhd", grad_scores, queries, preferred_element_type=jnp.float32
    )
    grad_projected = jnp.concatenate(
        [
            grad_queries.reshape(group_rows, head_cols),
            grad_keys.reshape(group_rows, head_cols),
            grad_values.reshape(group_rows, head_cols),
        ],
        axis=1,
    ).astype(jnp.bfloat16)
    qkv_flat_grad = jnp.einsum(
        "td,tc->dc", normed, grad_projected, preferred_element_type=jnp.float32
    )
    column_scale = jnp.concatenate(
        [jnp.full((head_cols,), q_scale, jnp.float32), jnp.ones((2 * head_cols,), jnp.float32)]
    )
    qkv_grad = jnp.transpose(
        (qkv_flat_grad * column_scale).reshape(widths, 3, head_cols), (1, 0, 2)
    )
    query_term = (
        jnp.einsum(
            "tc,dc->td",
            grad_projected[:, :head_cols],
            flat_qkv[:, :head_cols],
            preferred_element_type=jnp.float32,
        )
        * q_scale
    )
    grad_normed = lax.psum_scatter(
        query_term
        + jnp.einsum(
            "tc,dc->td",
            grad_projected[:, head_cols:],
            flat_qkv[:, head_cols:],
            preferred_element_type=jnp.float32,
        ),
        ("heads", "tensor"),
        scatter_dimension=0,
        tiled=True,
    )
    first_value, first_pull = jax.vjp(layer_norm, residual, ln_gains[0], ln_shift[0])
    grad_input, gain_one, shift_one = first_pull(grad_normed)
    grad_input = grad_input + grad_middle
    matrix_grads = (qkv_grad, out_grad, in_grad, back_grad)
    small_grads = (jnp.stack([gain_one, gain_two]), jnp.stack([shift_one, shift_two]), router_grad)
    return (grad_input, matrix_grads, small_grads)


def on_device(
    tokens,
    cotangent,
    image_counts,
    w_qkv,
    w_out,
    ln_gain,
    ln_bias,
    w_router,
    w_in,
    w_back,
    expert_ids,
    slots,
):
    own_rows = tokens.shape[0]
    row_start = lax.axis_index(("heads", "tensor")) * own_rows
    first_expert = lax.axis_index("heads") * w_in.shape[1]
    residual = tokens.astype(jnp.float32)
    head_list = []
    block_index = 0
    weights = (
        lax.all_gather(w_qkv[block_index], "fsdp", axis=1, tiled=True),
        lax.all_gather(w_out[block_index], "fsdp", axis=1, tiled=True),
        lax.all_gather(w_in[block_index], "fsdp", axis=1, tiled=True),
        lax.all_gather(w_back[block_index], "fsdp", axis=2, tiled=True),
    )
    residual, stored, head_full = forward_block(
        residual,
        weights,
        ln_gain[block_index],
        ln_bias[block_index],
        w_router[block_index],
        expert_ids[block_index],
        slots[block_index],
        first_expert,
    )
    stored_list = [stored]
    head_list.append(head_full)
    image_index = (row_start + jnp.arange(own_rows, dtype=jnp.int32)) // SEQ
    live_rows = (image_index < image_counts[0]).astype(jnp.float32)
    grad_rows = cotangent.astype(jnp.float32) * live_rows[:, None]
    matrix_list = [None] * LAYERS
    small_list = [None] * LAYERS
    for block_index in reversed(range(LAYERS)):
        weights = (
            lax.all_gather(w_qkv[block_index], "fsdp", axis=1, tiled=True),
            lax.all_gather(w_out[block_index], "fsdp", axis=1, tiled=True),
            lax.all_gather(w_in[block_index], "fsdp", axis=1, tiled=True),
            lax.all_gather(w_back[block_index], "fsdp", axis=2, tiled=True),
        )
        grad_rows, matrix_grads, small_grads = backward_block(
            grad_rows,
            stored_list[block_index],
            weights,
            ln_gain[block_index],
            ln_bias[block_index],
            w_router[block_index],
            expert_ids[block_index],
            row_start,
        )
        matrix_list[block_index] = (
            lax.psum_scatter(matrix_grads[0], "fsdp", scatter_dimension=1, tiled=True),
            lax.psum_scatter(matrix_grads[1], "fsdp", scatter_dimension=1, tiled=True),
            lax.psum_scatter(matrix_grads[2], "fsdp", scatter_dimension=1, tiled=True),
            lax.psum_scatter(matrix_grads[3], "fsdp", scatter_dimension=2, tiled=True),
        )
        small_list[block_index] = small_grads
    gain_grads, shift_grads, router_grads = lax.psum(
        (
            jnp.stack([entry[0] for entry in small_list]),
            jnp.stack([entry[1] for entry in small_list]),
            jnp.stack([entry[2] for entry in small_list]),
        ),
        ("fsdp", "heads", "tensor"),
    )
    qkv_grads = jnp.stack([entry[0] for entry in matrix_list])
    out_grads = jnp.stack([entry[1] for entry in matrix_list])
    in_grads = jnp.stack([entry[2] for entry in matrix_list])
    back_grads = jnp.stack([entry[3] for entry in matrix_list])
    return (
        residual.astype(jnp.bfloat16),
        grad_rows,
        qkv_grads,
        out_grads,
        gain_grads,
        shift_grads,
        router_grads,
        in_grads,
        back_grads,
    )


ROWS = -(-SEQ // 16) * 16
MESH = pl.DeviceIdType.MESH
F32, BF16 = jnp.float32, jnp.bfloat16
NN, NT, TN = (((1,), (0,)), ((), ())), (((1,), (1,)), ((), ())), (((0,), (0,)), ((), ()))


def mm(left, right, dims=NN):
    return lax.dot_general(left, right, dims, preferred_element_type=F32)


def whole(index, size):
    return pl.ds(pl.multiple_of(index * size, size), size)


def normal_parts(value):
    centred = value - jnp.mean(value, axis=-1, keepdims=True)
    scale = lax.rsqrt(jnp.mean(centred * centred, axis=-1, keepdims=True) + 1e-06)
    return centred * scale, scale


def normal_pull(grad, unit, scale, gains):
    grad_unit = grad * gains
    mean_grad = jnp.mean(grad_unit, axis=-1, keepdims=True)
    mean_both = jnp.mean(grad_unit * unit, axis=-1, keepdims=True)
    return scale * (grad_unit - mean_grad - unit * mean_both)


def gelu_parts(value):
    size = jnp.abs(value)
    step = 1.0 / (1.0 + 0.3275911 * 2.0**-0.5 * size)
    bell = jnp.exp(-0.5 * (value * value))
    series = 1.061405429 * step - 1.453152027
    series = series * step + 1.421413741
    series = series * step - 0.284496736
    series = series * step + 0.254829592
    tail = 0.5 * series * step * bell
    share = jnp.where(value < 0, tail, 1.0 - tail)
    return value * share, share + value * (bell * 0.3989422804014327)


class Exchange:
    def __init__(self, source, target, device, landing, send, recv):
        self.out = pltpu.make_async_remote_copy(
            source, target, send, recv, device_id=device, device_id_type=MESH
        )
        self.into = pltpu.make_async_remote_copy(
            landing, landing, send, recv, device_id=device, device_id_type=MESH
        )

        self.open = [True, True]
        self.out.start()

    def arrived(self):
        if self.open[0]:
            self.into.wait_recv()
        self.open[0] = False

    def sent(self):
        if self.open[1]:
            self.out.wait_send()
        self.open[1] = False

    def finish(self):
        self.arrived()
        self.sent()


class Kept:
    def __init__(self, source, target, semaphore):
        self.copy = pltpu.make_async_copy(source, target, semaphore)
        self.open = True
        self.copy.start()

    def arrived(self):
        if self.open:
            self.copy.wait()
        self.open = False

    sent = finish = arrived


def block_kernel(depth_z, images, local_count, refs):
    H = depth_z
    (
        tokens, cot, counts, wq, wo, gain, bias, wr, win_hbm, wback_hbm, named_in, slots_in,
        out, tgrad, wqg, wog, lng, lnb, wrg, gin_out, gback_out,
        stage, prow, wbuf, win, wback, rows_grad, rows_norm, big, wide,
        xsend, gsend, xrows, grows, xback, gback,
        normed, qkv, probs, mixed, middle, grad_mid, logit_grad,
        sib_out, sib_in, z_out, z_in, own_sum,
        att_in, plane_in, line_out, line_in,
        small_c, small_p, small_z, route_out, route_in, route_z, route_all,
        send_sems, recv_sems, local_sems,
    ) = refs
    own = images * ROWS
    width = tokens.shape[1]
    half = width // 128
    f, h, t = (lax.axis_index(name) for name in ("fsdp", "heads", "tensor"))
    s = 1 - t
    fx = [f, f + 1 - 2 * lax.rem(f, 2), lax.rem(f + 2, 4), 3 - f]
    hz = [lax.rem(h + d, H) for d in range(H)]
    hfrom = [lax.rem(h + H - d, H) for d in range(H)]
    after, before, across = lax.rem(2 * h + 1, 5), lax.rem(3 * h + 2, 5), 3 - h
    counter = [0]
    pending = []

    def exchange(source, target, device, landing):
        index = counter[0]
        counter[0] += 1
        made = Exchange(
            source, target, device, landing, send_sems.at[index], recv_sems.at[index]
        )
        pending.append(made)
        return made

    local_counter = [0]

    def kept(source, target):
        made = Kept(source, target, local_sems.at[local_counter[0]])
        local_counter[0] += 1
        pending.append(made)
        return made

    barrier = pltpu.get_barrier_semaphore()
    peers = [(f, hz[d], t) for d in range(1, H)] + [(f, h, s)]
    peers += [(fx[d], h, c) for d in range(1, 4) for c in (t, s)]
    for peer in peers:
        pl.semaphore_signal(barrier, inc=1, device_id=peer, device_id_type=MESH)

    for i in range(3):
        wbuf[i, h, t, :, whole(f, 128)] = wq[i]
    wbuf[3, h, t, :, whole(f, 128)] = wo[...]
    pl.semaphore_wait(barrier, len(peers))

    first = [
        exchange(*[wbuf.at[:, h, t, :, whole(f, 128)]] * 2, (f, hz[d], t),
                 wbuf.at[:, hfrom[d], t, :, whole(f, 128)])
        for d in range(1, H)
    ]

    depth, span = win_hbm.shape[1], win_hbm.shape[2]

    def move_in(d, c):
        landing = win.at[whole(fx[d], depth), whole(c, span)]
        target = win.at[whole(f, depth), whole(t, span)]
        return exchange(win_hbm.at[fx[d] * 2 + c], target, (fx[d], h, c), landing)

    def move_back(d, c):
        landing = wback.at[whole(c, span), whole(fx[d], depth)]
        target = wback.at[whole(t, span), whole(f, depth)]
        return exchange(wback_hbm.at[fx[d] * 2 + c], target, (fx[d], h, c), landing)

    expert_moves = [move_in(1, t), move_in(2, t)]
    mine = [
        kept(win_hbm.at[f * 2 + t], win.at[whole(f, depth), whole(t, span)]),
        kept(wback_hbm.at[f * 2 + t], wback.at[whole(t, span), whole(f, depth)]),
    ]

    row_index = lax.broadcasted_iota(jnp.int32, (ROWS, 1), 0)

    def image(source, b):
        if b == 0:
            stage[0 : images * SEQ, :] = source[...].astype(F32)
        return jnp.where(row_index < SEQ, stage[b * SEQ : b * SEQ + ROWS, :], 0.0)

    for b in range(images):
        live = ((h * 2 + t) * images + b < counts[0]).astype(F32)
        rows_grad[h * 2 + t, b * ROWS : (b + 1) * ROWS, :] = (image(cot, b) * live).astype(BF16)

    parts = [slice(0, own // 2), slice(own // 2, own)]

    def hop(rows, line, part, to, source):
        here = rows.at[line * 2 + t, parts[part]]
        return exchange(here, here, (f, to, t), rows.at[source * 2 + t, parts[part]])

    def beside(rows, line):
        here = rows.at[line * 2 + t, 0:own]
        return exchange(here, here, (f, h, s), rows.at[line * 2 + s, 0:own])

    class Spread:
        def __init__(self, rows):
            self.rows = rows
            self.down = [hop(rows, h, 0, after, before), None]
            self.up = [None, hop(rows, h, 1, before, after)]
            self.down[1] = hop(rows, h, 1, after, before)
            self.up[0] = hop(rows, h, 0, before, after)
            self.near = [beside(rows, h)]

        def relay(self):
            self.down[0].arrived()
            self.far = [hop(self.rows, before, 0, after, across)]
            self.up[1].arrived()
            self.far.append(hop(self.rows, after, 1, before, across))

        def share(self):
            self.down[1].arrived()
            self.near.append(beside(self.rows, before))
            self.up[0].arrived()
            self.near.append(beside(self.rows, after))

        def close(self):
            for move in self.far:
                move.arrived()
            self.near.append(beside(self.rows, across))

        def blocks(self):
            lines = [h, before, after, across]
            moves = self.near + [None] * (4 - len(self.near))
            return [(line * 2 + t, None) for line in lines] + [
                (line * 2 + s, move) for line, move in zip(lines, moves)
            ]

        def sent(self):
            for move in self.down + self.up + self.far + self.near:
                move.sent()

    for b in range(images):
        unit, _ = normal_parts(image(tokens, b))
        normed[b * ROWS : (b + 1) * ROWS, :] = (unit * gain[0:1] + bias[0:1]).astype(BF16)

    for step in first:
        step.arrived()
    grad_spread = Spread(rows_grad)
    second = [
        exchange(*[wbuf.at[:, :, t, :, whole(f, 128)]] * 2, (fx[d], h, t),
                 wbuf.at[:, :, t, :, whole(fx[d], 128)])
        for d in range(1, 4)
    ]

    relative = named_in[...] - h * local_count
    wanted = (slots_in[...] >= 0) & (relative >= 0) & (relative < local_count)
    wanted = wanted & (lax.rem(relative + 2 * local_count, 2) == t)
    places = jnp.where(wanted, lax.div(relative, 2) * CAP + slots_in[...], -1)
    reach = -(-(images * ROWS) // 128) * 128 + 128
    tail = jnp.full((2, reach), -1, jnp.int32)
    places = jnp.concatenate([places, tail], axis=1)[:, 0 : places.shape[1] // 128 * 128 + reach]
    place_lane = lax.broadcasted_iota(jnp.int32, (2, reach), 1)
    for b in range(2 * H):
        rows = jnp.full((2, reach), -1, jnp.int32)
        for i in range(images):
            begin = (b * images + i) * SEQ - i * ROWS
            base = max(begin // 128, 0) * 128
            window = pltpu.roll(places[:, base : base + reach], (base - begin) % reach, 1)
            inside = (place_lane >= i * ROWS) & (place_lane < i * ROWS + SEQ)
            rows = jnp.where(inside, window, rows)
        prow[b, 0:2, :] = rows[:, 0 : prow.shape[2]]

    def mark_slots(b):
        for part in range(4):
            spot = lax.broadcasted_iota(jnp.int32, (CAP, own), 0) + CAP * part
            named = (prow[b, 0:1, 0:own] == spot) | (prow[b, 1:2, 0:own] == spot)
            big[b, part * CAP : (part + 1) * CAP, 0:own] = jnp.where(named, 1.0, 0.0).astype(BF16)

    pl.loop(0, H)(mark_slots)
    grad_spread.relay()
    pl.loop(H, 2 * H)(mark_slots)
    for step in second:
        step.arrived()
    third = exchange(*[wbuf.at[:, :, t]] * 2, (f, h, s), wbuf.at[:, :, s])

    for d, c in ((1, s), (2, s), (3, t), (3, s), (0, s)):
        expert_moves.append(move_in(d, c))
    for d, c in ((1, t), (2, t), (1, s), (2, s), (3, t), (3, s), (0, s)):
        expert_moves.append(move_back(d, c))

    grad_spread.share()
    third.arrived()

    for i in range(3):
        part = mm(normed[...], wbuf[i].reshape(width, width), NT)
        if i == 0:
            part = part * HEAD ** (-0.5)
        qkv[:, i * width : (i + 1) * width] = part.astype(BF16)
    lane = lax.broadcasted_iota(jnp.int32, (1, 128), 1)
    sides = [jnp.where(lane < HEAD, 1.0, 0.0).astype(BF16), jnp.where(lane < HEAD, 0.0, 1.0).astype(BF16)]
    key_index = lax.broadcasted_iota(jnp.int32, (1, ROWS), 1)

    def pair_of(index):
        b, pair = index // half, lax.rem(index, half)
        rows = whole(b, ROWS)
        cols = [whole(pair + i * half, 128) for i in range(3)]
        return rows, cols

    @pl.loop(0, images * half)
    def _(index):
        rows, cols = pair_of(index)
        query, key, value = (qkv[rows, col] for col in cols)
        total = jnp.zeros((ROWS, 128), F32)
        for side in range(2):
            score = mm(query * sides[side], key, NT)
            score = jnp.where(key_index < SEQ, score, -1e30)
            score = jnp.exp(score - jnp.max(score, axis=-1, keepdims=True))
            prob = score / jnp.sum(score, axis=-1, keepdims=True)
            probs[index * 2 + side] = prob
            total += mm(prob.astype(BF16), value * sides[side])
        mixed[rows, cols[0]] = total.astype(BF16)

    for b in range(images):
        rows = slice(b * ROWS, (b + 1) * ROWS)
        value = image(tokens, b) + mm(mixed[rows, :], wbuf[3].reshape(width, width))
        middle[rows, :] = value
        unit, _ = normal_parts(value)
        rows_norm[h * 2 + t, rows, :] = (unit * gain[1:2] + bias[1:2]).astype(BF16)

    norm_spread = Spread(rows_norm)
    grad_spread.close()

    def accumulate(rows, b, begin):
        for part in range(4):
            span_rows = slice(part * CAP, (part + 1) * CAP)
            value = mm(big[b, span_rows, 0:own], rows[b, 0:own])
            wide[span_rows, :] = value if begin else wide[span_rows, :] + value

    def accumulate_all(spread, order):
        blocks = spread.blocks()
        for place in order:
            b, move = blocks[place]
            if move is not None:
                move.arrived()
            accumulate(spread.rows, b, place == 0)

    def pack(send):
        for part in range(4):
            send[part] = wide[part * CAP : (part + 1) * CAP, :].astype(BF16)

    def dispatch(send, landing):
        moved = [
            exchange(send.at[fx[d]], landing.at[f], (fx[d], h, t), landing.at[fx[d]])
            for d in range(1, 4)
        ]
        return [kept(send.at[f], landing.at[f])] + moved

    accumulate_all(grad_spread, (0, 1, 2, 3))
    norm_spread.relay()
    accumulate_all(grad_spread, (4, 5, 6, 7))
    pack(gsend)
    grad_moved = dispatch(gsend, grows)
    norm_spread.share()
    accumulate_all(norm_spread, (0, 1, 2, 4, 5, 6))
    norm_spread.close()
    accumulate_all(norm_spread, (3, 7))
    pack(xsend)
    norm_moved = dispatch(xsend, xrows)

    expert = h * local_count + f * 2 + t
    router_lane = lax.broadcasted_iota(jnp.int32, (1, wr.shape[0]), 1)
    chosen = (router_lane == expert).astype(F32)
    chunk = 512
    chunks = win.shape[1] // chunk
    for move in mine + expert_moves:
        move.arrived()
    back_moves = []
    for d in range(4):
        group = fx[d]
        here = whole(group, CAP)
        norm_moved[d].arrived()
        rows = xrows[group]
        result = jnp.zeros((CAP, width), F32)
        for c in range(chunks):
            value, slope = gelu_parts(mm(rows, win[:, c * chunk : (c + 1) * chunk]))
            value = value.astype(BF16)
            big[c, here, :] = value
            wide[c * CAP : (c + 1) * CAP, :] = slope
            result += mm(value, wback[c * chunk : (c + 1) * chunk, :])
        logits = mm(rows, wr[...], NT)
        odds = jnp.exp(logits - jnp.max(logits, axis=-1, keepdims=True))
        odds = odds / jnp.sum(odds, axis=-1, keepdims=True)
        gate = jnp.sum(odds * chosen, axis=-1, keepdims=True)
        grad_moved[d].finish()
        norm_moved[d].sent()
        gsend[group] = (gate * result).astype(BF16)
        row_grad = grows[group].astype(F32)
        gate_grad = jnp.sum(row_grad * result, axis=-1, keepdims=True)
        result_grad = (gate * row_grad).astype(BF16)
        grows[group] = result_grad
        logit = (gate_grad * gate * (chosen - odds)).astype(BF16)
        logit_grad[here, :] = logit
        total = mm(logit, wr[...])
        for c in range(chunks):
            grad = mm(result_grad, wback[c * chunk : (c + 1) * chunk, :], NT)
            grad = (grad * wide[c * CAP : (c + 1) * CAP, :]).astype(BF16)
            big[4 + c, here, :] = grad
            total += mm(grad, win[:, c * chunk : (c + 1) * chunk], NT)
        xsend[group] = total.astype(BF16)
        if d:
            back_moves.append(exchange(xsend.at[group], xback.at[f], (group, h, t), xback.at[group]))
        else:
            back_moves.append(kept(xsend.at[f], xback.at[f]))

    grad_spread.sent()
    norm_spread.sent()
    flat_rows = xrows[...].reshape(4 * CAP, width)
    flat_grad = grows[...].reshape(4 * CAP, width)
    for c in range(chunks):
        rows_grad[c] = mm(flat_rows, big[4 + c], TN).astype(BF16)
        rows_norm[c] = mm(big[c], flat_grad, TN).astype(BF16)
    route = mm(logit_grad[...], flat_rows, TN)
    share_rows = wr.shape[0] // 8
    for j in range(8):
        route_out[j, 0:share_rows, :] = route[j * share_rows : (j + 1) * share_rows]

    for move in back_moves:
        move.arrived()
    out_moves = dispatch(gsend, gback)

    def to_owners():
        halves = chunks // 2
        for d in range(4):
            for c in (t, s):
                device = (fx[d], h, c)
                for part in range(halves):
                    span_part = slice(part * chunk, (part + 1) * chunk)
                    source_in = rows_grad.at[c * halves + part, whole(fx[d], depth), :]
                    source_back = rows_norm.at[c * halves + part, :, whole(fx[d], depth)]
                    target_in = gin_out.at[f * 2 + t, :, span_part]
                    target_back = gback_out.at[f * 2 + t, span_part]
                    if d == 0 and c is t:
                        kept(source_in, target_in)
                        kept(source_back, target_back)
                        continue
                    exchange(source_in, target_in, device, gin_out.at[fx[d] * 2 + c, :, span_part])
                    exchange(source_back, target_back, device, gback_out.at[fx[d] * 2 + c, span_part])

    plane_peers = [(d, c) for d in range(4) for c in ((t, s) if d else (s,))]
    route_kept = kept(route_out.at[f * 2 + t], route_in.at[f * 2 + t])
    route_moves = [
        exchange(route_out.at[fx[d] * 2 + c], route_in.at[f * 2 + t], (fx[d], h, c), route_in.at[fx[d] * 2 + c])
        for d, c in plane_peers
    ]

    def share(b, back):
        spots = jnp.transpose(prow[b])[0:own]
        slot = lax.broadcasted_iota(jnp.int32, (own, 4 * CAP), 1)
        named = (spots[:, 0:1] == slot) | (spots[:, 1:2] == slot)
        return mm(jnp.where(named, 1.0, 0.0).astype(BF16), back[...].reshape(4 * CAP, width))

    class Gather:
        def __init__(self, which, back, near_out, far_out):
            self.which, self.back = which, back
            self.near_out, self.far_out = near_out, far_out
            self.lines = [across, after, before, h]
            self.near = []

        def give(self, place):
            line = self.lines[place]
            self.near_out(place)[...] = share(line * 2 + s, self.back).astype(BF16)
            landing = sib_in.at[self.which, place]
            self.near.append(exchange(self.near_out(place), landing, (f, h, s), landing))

        def take(self, place):
            value = share(self.lines[place] * 2 + t, self.back)
            self.near[place].arrived()
            value = value + sib_in[self.which, place].astype(F32)
            if place == 3:
                own_sum[self.which] = value
            else:
                self.far_out(place)[...] = value.astype(BF16)

        def hop(self, place, part, to, slot):
            landing = z_in.at[self.which, slot, parts[part]]
            return exchange(self.far_out(place).at[parts[part]], landing, (f, to, t), landing)

        def start(self):
            self.first = [self.hop(0, 0, after, 0), self.hop(0, 1, before, 0)]

        def direct(self, place):
            part, to = ((1, after), (0, before))[place - 1]
            self.last = getattr(self, "last", []) + [self.hop(place, part, to, place)]

        def relay(self):
            for place, part, to in ((1, 0, after), (2, 1, before)):
                self.first[part].arrived()
                rows = self.far_out(place).at[parts[part]]
                passed = z_in[self.which, 0, parts[part], :].astype(F32)
                rows[...] = (rows[...].astype(F32) + passed).astype(BF16)
                self.last.append(self.hop(place, part, to, place))

        def total(self, rows):
            for move in self.last:
                move.arrived()
            total = own_sum[self.which, rows, :]
            for slot in (1, 2):
                total = total + z_in[self.which, slot, rows, :].astype(F32)
            return total

    norm_sums = Gather(0, xback, lambda place: sib_out.at[place], lambda place: z_out.at[place])
    norm_sums.give(0)
    norm_sums.take(0)
    norm_sums.start()
    to_owners()
    norm_sums.give(1)
    norm_sums.give(2)
    norm_sums.take(1)
    norm_sums.direct(1)
    norm_sums.take(2)
    norm_sums.direct(2)
    norm_sums.give(3)
    norm_sums.take(3)
    norm_sums.relay()

    route_kept.arrived()
    for move in route_moves:
        move.arrived()
    route = route_in[0, 0:share_rows, :]
    for j in range(1, 8):
        route = route + route_in[j, 0:share_rows, :]
    route_z[h, 0:share_rows, :] = route
    route_line = [
        exchange(route_z.at[h], route_z.at[h], (f, hz[d], t), route_z.at[hfrom[d]]) for d in range(1, H)
    ]

    for move in out_moves:
        move.arrived()
    out_sums = Gather(
        1, gback, lambda place: big.at[place, 0:own], lambda place: big.at[4 + place, 0:own]
    )
    for place in range(4):
        out_sums.give(place)
    for place in range(4):
        out_sums.take(place)

    for move in norm_sums.last:
        move.arrived()
    out_sums.start()
    out_sums.direct(1)
    out_sums.direct(2)
    small_c[t] = jnp.zeros(small_c.shape[1:], F32)
    for b in range(images):
        rows = slice(b * ROWS, (b + 1) * ROWS)
        grad = norm_sums.total(rows)
        unit, scale = normal_parts(middle[rows, :])
        small_c[t, 1:2] += jnp.sum(grad * unit, axis=0, keepdims=True)
        small_c[t, 3:4] += jnp.sum(grad, axis=0, keepdims=True)
        live = ((h * 2 + t) * images + b < counts[0]).astype(F32)
        grad = normal_pull(grad, unit, scale, gain[1:2]) + image(cot, b) * live
        grad_mid[rows, :] = grad

    for move in back_moves:
        move.sent()
    low = grad_mid[...].astype(BF16)
    count = H * 2 * 64
    wide[3 * count : 4 * count, :] = mm(mixed[...], low, TN)

    def wide_rows(i, other, core):
        return whole((i * H + other) * 2 + core, 64)

    def core_sums(span_i):
        for i in range(span_i.start, span_i.stop):
            for other in range(H):
                here_low = slice(other * 64, (other + 1) * 64)
                xsend[i, here_low, :] = wide[wide_rows(i, other, s), :].astype(BF16)
        landing = att_in.at[span_i]
        return exchange(xsend.at[span_i, 0 : H * 64], landing, (f, h, s), landing)

    def plane_sums(span_i, near):
        near.finish()
        for i in range(span_i.start, span_i.stop):
            for other in range(H):
                here = wide_rows(i, other, t)
                here_low = slice(other * 64, (other + 1) * 64)
                value = wide[here, :] + att_in[i, here_low, :].astype(F32)
                wide[here, :] = value
                xsend[i, here_low, :] = value.astype(BF16)
        return [
            exchange(
                xsend.at[span_i, 0 : H * 64, whole(fx[d], 128)], plane_in.at[f, span_i],
                (fx[d], h, t), plane_in.at[fx[d], span_i],
            )
            for d in range(1, 4)
        ]

    last_near = core_sums(slice(3, 4))
    mixed[...] = mm(low, wbuf[3].reshape(width, width), NT).astype(BF16)

    @pl.loop(0, images * half)
    def _(index):
        rows, cols = pair_of(index)
        query, key, value = (qkv[rows, col] for col in cols)
        pulled = mixed[rows, cols[0]]
        grads = [jnp.zeros((ROWS, 128), F32) for _ in range(3)]
        for side in range(2):
            prob = probs[index * 2 + side]
            one = pulled * sides[side]
            prob_grad = mm(one, value, NT)
            grads[2] += mm(prob.astype(BF16), one, TN)
            inner = jnp.sum(prob * prob_grad, axis=-1, keepdims=True)
            score_grad = (prob * (prob_grad - inner)).astype(BF16)
            grads[0] += mm(score_grad, key * sides[side])
            grads[1] += mm(score_grad, query * sides[side], TN)
        grads[0] = grads[0] * HEAD ** (-0.5)
        for grad, col in zip(grads, cols):
            qkv[rows, col] = grad.astype(BF16)

    out_sums.relay()
    for i in range(3):
        wide[i * count : (i + 1) * count, :] = mm(
            qkv[:, i * width : (i + 1) * width], normed[...], TN
        )

    plane = plane_sums(slice(3, 4), last_near)
    att_near = core_sums(slice(0, 3))

    for b in range(images):
        rows = slice(b * ROWS, (b + 1) * ROWS)
        grad = jnp.zeros((ROWS, width), F32)
        for i in range(3):
            grad += mm(qkv[rows, i * width : (i + 1) * width], wbuf[i].reshape(width, width))
        unit, scale = normal_parts(image(tokens, b))
        small_c[t, 0:1] += jnp.sum(grad * unit, axis=0, keepdims=True)
        small_c[t, 2:3] += jnp.sum(grad, axis=0, keepdims=True)
        grad = normal_pull(grad, unit, scale, gain[0:1]) + grad_mid[rows, :]
        tgrad[b * SEQ : (b + 1) * SEQ, :] = grad[0:SEQ]
    small_near = exchange(small_c.at[t], small_c.at[t], (f, h, s), small_c.at[s])

    plane += plane_sums(slice(0, 3), att_near)
    small_near.arrived()
    small_p[f] = small_c[0] + small_c[1]
    small_plane = [
        exchange(small_p.at[f], small_p.at[f], (fx[d], h, t), small_p.at[fx[d]]) for d in range(1, 4)
    ]
    for move in route_line:
        move.arrived()
    route = route_z[0]
    for d in range(1, H):
        route = route + route_z[d]
    route_all[f * 2 + t] = route
    route_last = [
        exchange(route_all.at[f * 2 + t], route_all.at[f * 2 + t], (fx[d], h, c), route_all.at[fx[d] * 2 + c])
        for d, c in plane_peers
    ]

    for b in range(images):
        rows = slice(b * ROWS, (b + 1) * ROWS)
        value = middle[rows, :] + out_sums.total(rows)
        stage[b * SEQ : (b + 1) * SEQ, :] = value[0:SEQ]
    out[...] = stage[0 : images * SEQ, :].astype(BF16)

    for move in plane:
        move.arrived()
    for i in range(4):
        for other in range(H):
            value = wide[wide_rows(i, other, t), whole(f, 128)]
            for d in range(1, 4):
                value = value + plane_in[fx[d], i, other * 64 : (other + 1) * 64, :].astype(F32)
            wide[wide_rows(i, other, t), 0:128] = value
            line_out[other, i] = value.astype(BF16)
    line = [
        exchange(line_out.at[hz[d]], line_in.at[h], (f, hz[d], t), line_in.at[hfrom[d]])
        for d in range(1, H)
    ]
    for move in small_plane:
        move.arrived()
    small_z[h] = (small_p[0] + small_p[1]) + (small_p[2] + small_p[3])
    small_line = [
        exchange(small_z.at[h], small_z.at[h], (f, hz[d], t), small_z.at[hfrom[d]]) for d in range(1, H)
    ]
    for move in route_last:
        move.arrived()
    for j in range(8):
        wrg[j * share_rows : (j + 1) * share_rows, :] = route_all[j, 0:share_rows, :]

    for move in line:
        move.arrived()
    for i in range(4):
        value = wide[wide_rows(i, h, t), 0:128]
        for d in range(1, H):
            value = value + line_in[hfrom[d], i].astype(F32)
        if i < 3:
            wqg[i] = value
        else:
            wog[...] = value
    for move in small_line:
        move.arrived()
    total = small_z[0]
    for d in range(1, H):
        total = total + small_z[d]
    lng[...] = total[0:2]
    lnb[...] = total[2:4]

    for move in pending:
        move.finish()


def finish_kernel(*refs):
    sources, targets = refs[:9], refs[9:18]
    held, wider = refs[18:27], refs[27:29]
    in_sems, out_sems = refs[29], refs[30]
    experts = sources[7].shape[0]
    inward, outward = [], []

    def begin(source, target, semaphores, index):
        copy = pltpu.make_async_copy(source, target, semaphores.at[index])
        copy.start()
        return copy

    for e in range(experts):
        for k in (7, 8):
            index = 7 + 2 * e + k - 7
            inward.append((e, k, index, begin(sources[k].at[e], held[k].at[e], in_sems, index)))
    small = [begin(sources[k], held[k], in_sems, k) for k in range(7)]
    for e, k, index, copy in inward:
        copy.wait()
        wider[k - 7][e] = held[k][e].astype(F32)
        outward.append(begin(wider[k - 7].at[e], targets[k].at[e], out_sems, index))
    for k, copy in enumerate(small):
        copy.wait()
        outward.append(begin(held[k], targets[k], out_sems, k))
    for copy in outward:
        copy.wait()


def fast_device(
    tokens,
    cotangent,
    image_counts,
    w_qkv,
    w_out,
    ln_gain,
    ln_bias,
    w_router,
    w_in,
    w_back,
    expert_ids,
    slots,
):
    H = lax.axis_size("heads")
    own_rows, width = tokens.shape
    images = own_rows // SEQ
    own = images * ROWS
    local_count, depth, span = w_in.shape[1:]
    experts = w_router.shape[2]
    hidden = span * 2
    vmem = pl.BlockSpec(memory_space=pltpu.VMEM)
    smem = pl.BlockSpec(memory_space=pltpu.SMEM)
    anywhere = pl.BlockSpec(memory_space=pl.ANY)
    shape = jax.ShapeDtypeStruct

    def low(*dims):
        return pltpu.VMEM(dims, BF16)

    def full(*dims):
        return pltpu.VMEM(dims, F32)

    outs = pl.pallas_call(
        lambda *refs: block_kernel(H, images, local_count, refs),
        out_shape=(
            shape((own_rows, width), BF16),
            shape((own_rows, width), F32),
            shape((3, 64, depth), F32),
            shape((64, depth), F32),
            shape((2, width), F32),
            shape((2, width), F32),
            shape((experts, width), F32),
            shape((local_count, depth, span), BF16),
            shape((local_count, span, depth), BF16),
        ),
        in_specs=[vmem, vmem, smem, vmem, vmem, vmem, vmem, vmem, anywhere, anywhere, vmem, vmem],
        out_specs=[vmem] * 7 + [anywhere] * 2,
        scratch_shapes=[
            full(images * SEQ + 16, width),
            pltpu.VMEM((2 * H, 8, -(-own // 128) * 128), jnp.int32),
            low(4, H, 2, 64, width),
            low(width, hidden),
            low(hidden, width),
            low(2 * H, 512, width),
            low(2 * H, 512, width),
            low(8, 4 * CAP, 512),
            full(8 * CAP, width),
            low(4, CAP, width),
            low(4, CAP, width),
            low(4, CAP, width),
            low(4, CAP, width),
            low(4, CAP, width),
            low(4, CAP, width),
            low(own, width),
            low(own, 3 * width),
            full(images * width // HEAD, ROWS, ROWS),
            low(own, width),
            full(own, width),
            full(own, width),
            low(4 * CAP, experts),
            low(H, own, width),
            low(2, H, own, width),
            low(3, own, width),
            low(2, 3, own, width),
            full(2, own, width),
            low(4, H * 64, width),
            low(4, 4, H * 64, 128),
            low(H, 4, 64, 128),
            low(H, 4, 64, 128),
            full(2, 8, width),
            full(4, 8, width),
            full(H, 8, width),
            full(8, 8, width),
            full(8, 8, width),
            full(H, 8, width),
            full(8, 8, width),
            pltpu.SemaphoreType.DMA((192,)),
            pltpu.SemaphoreType.DMA((192,)),
            pltpu.SemaphoreType.DMA((16,)),
        ],
        compiler_params=pltpu.CompilerParams(
            collective_id=0, has_side_effects=True, vmem_limit_bytes=62 * 2**20
        ),
        name="block",
    )(
        tokens, cotangent, image_counts, jnp.transpose(w_qkv[0], (0, 2, 1)), w_out[0], ln_gain[0], ln_bias[0],
        jnp.transpose(w_router[0]),
        w_in[0], w_back[0], jnp.transpose(expert_ids[0]), jnp.transpose(slots[0]),
    )
    sems = pltpu.SemaphoreType.DMA((7 + 2 * local_count,))
    outs = pl.pallas_call(
        finish_kernel,
        out_shape=[shape(part.shape, F32 if i >= 7 else part.dtype) for i, part in enumerate(outs)],
        in_specs=[anywhere] * 9,
        out_specs=[anywhere] * 9,
        scratch_shapes=[pltpu.VMEM(part.shape, part.dtype) for part in outs]
        + [full(*part.shape) for part in outs[7:]]
        + [sems, sems],
        compiler_params=pltpu.CompilerParams(vmem_limit_bytes=62 * 2**20),
        name="finish",
    )(*outs)
    block_out, token_grad, qkv_grad, out_grad, gains, shifts, router, in_grad, back_grad = outs
    return (
        block_out,
        token_grad,
        jnp.transpose(qkv_grad, (0, 2, 1))[None],
        out_grad[None],
        gains[None],
        shifts[None],
        jnp.transpose(router)[None],
        in_grad[None],
        back_grad[None],
    )


def solution(mesh):
    def program(*arrays):
        sizes = dict(mesh.shape)
        devices = sizes["fsdp"] * sizes["heads"] * sizes["tensor"]
        own_rows = arrays[0].shape[0] // devices
        one_expert = sizes["fsdp"] == 4 and sizes["tensor"] == 2 and arrays[8].shape[1] == devices
        one_expert = one_expert and sizes["heads"] == 4 and own_rows % (2 * SEQ) == 0
        return placed(mesh, fast_device if one_expert else on_device)(*arrays)

    return program


def placed(mesh, on_device):
    return jax.shard_map(
        on_device,
        mesh=mesh,
        in_specs=(
            P(("fsdp", "heads", "tensor"), None),
            P(("fsdp", "heads", "tensor"), None),
            P("fsdp"),
            P(None, None, "fsdp", ("heads", "tensor")),
            P(None, ("heads", "tensor"), "fsdp"),
            P(),
            P(),
            P(),
            P(None, "heads", "fsdp", "tensor"),
            P(None, "heads", "tensor", "fsdp"),
            P(None, "fsdp", None),
            P(None, "fsdp", None),
        ),
        out_specs=(
            P(("fsdp", "heads", "tensor"), None),
            P(("fsdp", "heads", "tensor"), None),
            P(None, None, "fsdp", ("heads", "tensor")),
            P(None, ("heads", "tensor"), "fsdp"),
            P(),
            P(),
            P(),
            P(None, "heads", "fsdp", "tensor"),
            P(None, "heads", "tensor", "fsdp"),
        ),
        check_vma=False,
    )
```

```python
import jax
import jax.numpy as jnp
from jax import lax
from jax.experimental import pallas as pl
from jax.experimental.pallas import tpu as pltpu
from jax.sharding import PartitionSpec as P

HEAD = 64
SEQ = 197
LAYERS = 1
CAP = 256


def layer_norm(value, ln_gains, ln_shift):
    centred = value - jnp.mean(value, axis=-1, keepdims=True)
    spread = jnp.mean(centred * centred, axis=-1, keepdims=True)
    return centred * lax.rsqrt(spread + 1e-06) * ln_gains + ln_shift


def gelu_exact(value):
    return jax.nn.gelu(value, approximate=False)


def with_zero_row(matrix):
    return jnp.concatenate([matrix, jnp.zeros((1,) + matrix.shape[1:], matrix.dtype)], axis=0)


def slot_tables(named_expert, slot_rows, first_expert, local_experts):
    group_rows = named_expert.shape[0]
    is_local = (
        (slot_rows >= 0)
        & (named_expert >= first_expert)
        & (named_expert < first_expert + local_experts)
    )
    places = jnp.where(
        is_local, (named_expert - first_expert) * CAP + slot_rows, local_experts * CAP
    )
    picked = jnp.full((local_experts * CAP + 1,), 2 * group_rows, jnp.int32)
    picked = picked.at[places.reshape(-1)].set(jnp.arange(2 * group_rows, dtype=jnp.int32))
    return (places, picked[: local_experts * CAP])


def joined_qkv(qkv_weight):
    head_cols = qkv_weight.shape[2]
    return jnp.transpose(qkv_weight, (1, 0, 2)).reshape(qkv_weight.shape[1], 3 * head_cols)


def forward_block(
    residual, weights, ln_gains, ln_shift, router_weight, named_expert, slot_rows, first_expert
):
    qkv_weight, out_weight, in_weight, back_weight = weights
    own_rows, widths = residual.shape
    group_rows = named_expert.shape[0]
    head_cols = qkv_weight.shape[2]
    local_experts = in_weight.shape[0]
    head_shape = (group_rows // SEQ, SEQ, head_cols // HEAD, HEAD)
    q_scale = HEAD ** (-0.5)
    flat_qkv = joined_qkv(qkv_weight)
    normed_rows = layer_norm(residual, ln_gains[0], ln_shift[0]).astype(jnp.bfloat16)
    normed = lax.all_gather(normed_rows, ("heads", "tensor"), axis=0, tiled=True)
    projected = jnp.dot(normed, flat_qkv, preferred_element_type=jnp.float32)
    queries = (projected[:, :head_cols] * q_scale).astype(jnp.bfloat16).reshape(head_shape)
    key_rows = projected[:, head_cols : 2 * head_cols].astype(jnp.bfloat16).reshape(head_shape)
    value_rows = projected[:, 2 * head_cols :].astype(jnp.bfloat16).reshape(head_shape)
    scores = jnp.einsum("bqhd,bkhd->bhqk", queries, key_rows, preferred_element_type=jnp.float32)
    log_total = jax.nn.logsumexp(scores, axis=-1)
    attn_probs = jax.nn.softmax(scores, axis=-1).astype(jnp.bfloat16)
    mixed_rows = jnp.einsum(
        "bhqk,bkhd->bqhd", attn_probs, value_rows, preferred_element_type=jnp.float32
    )
    mixed_rows = mixed_rows.reshape(group_rows, head_cols).astype(jnp.bfloat16)
    middle = residual + lax.psum_scatter(
        jnp.dot(mixed_rows, out_weight, preferred_element_type=jnp.float32),
        ("heads", "tensor"),
        scatter_dimension=0,
        tiled=True,
    )
    head_full = ()
    normed_two_rows = layer_norm(middle, ln_gains[1], ln_shift[1]).astype(jnp.bfloat16)
    normed_two = lax.all_gather(normed_two_rows, ("heads", "tensor"), axis=0, tiled=True)
    router = jax.nn.softmax(
        jnp.dot(normed_two, router_weight, preferred_element_type=jnp.float32), axis=-1
    )
    gate_values = jnp.take_along_axis(router, named_expert, axis=1) * (slot_rows >= 0)
    places, picked = slot_tables(named_expert, slot_rows, first_expert, local_experts)
    routed = with_zero_row(normed_two)[picked // 2].reshape(local_experts, CAP, widths)
    hidden = jnp.einsum("ecd,edf->ecf", routed, in_weight, preferred_element_type=jnp.float32)
    active = gelu_exact(hidden).astype(jnp.bfloat16)
    result = jnp.einsum("ecf,efd->ecd", active, back_weight, preferred_element_type=jnp.float32)
    flat_result = with_zero_row(result.reshape(local_experts * CAP, widths))
    block_out = middle + lax.psum_scatter(
        (
            flat_result[places[:, 0]] * gate_values[:, 0:1]
            + flat_result[places[:, 1]] * gate_values[:, 1:2]
        ).astype(jnp.bfloat16),
        ("heads", "tensor"),
        scatter_dimension=0,
        tiled=True,
    ).astype(jnp.float32)
    stored = (
        residual,
        middle,
        normed,
        queries,
        key_rows,
        value_rows,
        log_total,
        mixed_rows,
        normed_two_rows,
        router,
        gate_values,
        places,
        picked,
        routed,
        hidden,
        active,
        flat_result,
    )
    return (block_out, stored, head_full)


def backward_block(
    grad_rows, stored, weights, ln_gains, ln_shift, router_weight, named_expert, row_start
):
    qkv_weight, out_weight, in_weight, back_weight = weights
    (
        residual,
        middle,
        normed,
        queries,
        key_rows,
        value_rows,
        log_total,
        mixed_rows,
        normed_two_rows,
        router,
        gate_values,
        places,
        picked,
        routed,
        hidden,
        active,
        flat_result,
    ) = stored
    own_rows, widths = residual.shape
    group_rows = named_expert.shape[0]
    head_cols = qkv_weight.shape[2]
    local_experts = in_weight.shape[0]
    expert_count = router.shape[1]
    q_scale = HEAD ** (-0.5)
    flat_qkv = joined_qkv(qkv_weight)
    grad_moe = lax.all_gather(
        grad_rows.astype(jnp.bfloat16), ("heads", "tensor"), axis=0, tiled=True
    )
    back_rows = with_zero_row(grad_moe)[picked // 2].astype(jnp.float32)
    gate_slots = with_zero_row(gate_values.reshape(-1))[picked]
    gate_grad_slots = jnp.sum(back_rows * flat_result[:-1], axis=1)
    gate_grads = with_zero_row(gate_grad_slots)[places]
    expert_range = jnp.arange(expert_count, dtype=jnp.int32)
    router_part = jnp.sum(
        gate_grads[:, :, None]
        * (named_expert[:, :, None] == expert_range[None, None, :]).astype(jnp.float32),
        axis=1,
    )
    grad_result = (
        (gate_slots[:, None] * back_rows).astype(jnp.bfloat16).reshape(local_experts, CAP, widths)
    )
    grad_active = jnp.einsum(
        "ecd,efd->ecf", grad_result, back_weight, preferred_element_type=jnp.float32
    )
    gelu_value, gelu_pull = jax.vjp(gelu_exact, hidden)
    grad_hidden = gelu_pull(grad_active)[0].astype(jnp.bfloat16)
    back_grad = jnp.einsum("ecf,ecd->efd", active, grad_result, preferred_element_type=jnp.float32)
    in_grad = jnp.einsum("ecd,ecf->edf", routed, grad_hidden, preferred_element_type=jnp.float32)
    grad_routed = jnp.einsum(
        "ecf,edf->ecd", grad_hidden, in_weight, preferred_element_type=jnp.float32
    )
    grad_routed = with_zero_row(grad_routed.reshape(local_experts * CAP, widths))
    token_part = grad_routed[places[:, 0]] + grad_routed[places[:, 1]]
    grad_normed_two, router_rows = (
        lax.psum_scatter(token_part, ("heads", "tensor"), scatter_dimension=0, tiled=True),
        lax.psum_scatter(router_part, ("heads", "tensor"), scatter_dimension=0, tiled=True),
    )
    router_own = lax.dynamic_slice_in_dim(router, row_start, own_rows, 0)
    grad_logits = (
        router_own * (router_rows - jnp.sum(router_own * router_rows, axis=-1, keepdims=True))
    ).astype(jnp.bfloat16)
    router_grad = jnp.einsum(
        "td,te->de", normed_two_rows, grad_logits, preferred_element_type=jnp.float32
    )
    grad_normed_two = grad_normed_two + jnp.einsum(
        "te,de->td", grad_logits, router_weight, preferred_element_type=jnp.float32
    )
    norm_value, norm_pull = jax.vjp(layer_norm, middle, ln_gains[1], ln_shift[1])
    grad_middle, gain_two, shift_two = norm_pull(grad_normed_two)
    grad_middle = grad_middle + grad_rows
    grad_attn = lax.all_gather(
        grad_middle.astype(jnp.bfloat16), ("heads", "tensor"), axis=0, tiled=True
    )
    out_grad = jnp.einsum("tc,td->cd", mixed_rows, grad_attn, preferred_element_type=jnp.float32)
    grad_mixed = jnp.einsum("td,cd->tc", grad_attn, out_weight, preferred_element_type=jnp.float32)
    grad_mixed = grad_mixed.astype(jnp.bfloat16).reshape(queries.shape)
    scores = jnp.einsum("bqhd,bkhd->bhqk", queries, key_rows, preferred_element_type=jnp.float32)
    attn_probs = jnp.exp(scores - log_total[..., None])
    grad_values = jnp.einsum(
        "bhqk,bqhd->bkhd",
        attn_probs.astype(jnp.bfloat16),
        grad_mixed,
        preferred_element_type=jnp.float32,
    )
    grad_probs = jnp.einsum(
        "bqhd,bkhd->bhqk", grad_mixed, value_rows, preferred_element_type=jnp.float32
    )
    grad_scores = (
        attn_probs * (grad_probs - jnp.sum(attn_probs * grad_probs, axis=-1, keepdims=True))
    ).astype(jnp.bfloat16)
    grad_queries = jnp.einsum(
        "bhqk,bkhd->bqhd", grad_scores, key_rows, preferred_element_type=jnp.float32
    )
    grad_keys = jnp.einsum(
        "bhqk,bqhd->bkhd", grad_scores, queries, preferred_element_type=jnp.float32
    )
    grad_projected = jnp.concatenate(
        [
            grad_queries.reshape(group_rows, head_cols),
            grad_keys.reshape(group_rows, head_cols),
            grad_values.reshape(group_rows, head_cols),
        ],
        axis=1,
    ).astype(jnp.bfloat16)
    qkv_flat_grad = jnp.einsum(
        "td,tc->dc", normed, grad_projected, preferred_element_type=jnp.float32
    )
    column_scale = jnp.concatenate(
        [jnp.full((head_cols,), q_scale, jnp.float32), jnp.ones((2 * head_cols,), jnp.float32)]
    )
    qkv_grad = jnp.transpose(
        (qkv_flat_grad * column_scale).reshape(widths, 3, head_cols), (1, 0, 2)
    )
    query_term = (
        jnp.einsum(
            "tc,dc->td",
            grad_projected[:, :head_cols],
            flat_qkv[:, :head_cols],
            preferred_element_type=jnp.float32,
        )
        * q_scale
    )
    grad_normed = lax.psum_scatter(
        query_term
        + jnp.einsum(
            "tc,dc->td",
            grad_projected[:, head_cols:],
            flat_qkv[:, head_cols:],
            preferred_element_type=jnp.float32,
        ),
        ("heads", "tensor"),
        scatter_dimension=0,
        tiled=True,
    )
    first_value, first_pull = jax.vjp(layer_norm, residual, ln_gains[0], ln_shift[0])
    grad_input, gain_one, shift_one = first_pull(grad_normed)
    grad_input = grad_input + grad_middle
    matrix_grads = (qkv_grad, out_grad, in_grad, back_grad)
    small_grads = (jnp.stack([gain_one, gain_two]), jnp.stack([shift_one, shift_two]), router_grad)
    return (grad_input, matrix_grads, small_grads)


def on_device(
    tokens,
    cotangent,
    image_counts,
    w_qkv,
    w_out,
    ln_gain,
    ln_bias,
    w_router,
    w_in,
    w_back,
    expert_ids,
    slots,
):
    own_rows = tokens.shape[0]
    row_start = lax.axis_index(("heads", "tensor")) * own_rows
    first_expert = lax.axis_index("heads") * w_in.shape[1]
    residual = tokens.astype(jnp.float32)
    head_list = []
    block_index = 0
    weights = (
        lax.all_gather(w_qkv[block_index], "fsdp", axis=1, tiled=True),
        lax.all_gather(w_out[block_index], "fsdp", axis=1, tiled=True),
        lax.all_gather(w_in[block_index], "fsdp", axis=1, tiled=True),
        lax.all_gather(w_back[block_index], "fsdp", axis=2, tiled=True),
    )
    residual, stored, head_full = forward_block(
        residual,
        weights,
        ln_gain[block_index],
        ln_bias[block_index],
        w_router[block_index],
        expert_ids[block_index],
        slots[block_index],
        first_expert,
    )
    stored_list = [stored]
    head_list.append(head_full)
    image_index = (row_start + jnp.arange(own_rows, dtype=jnp.int32)) // SEQ
    live_rows = (image_index < image_counts[0]).astype(jnp.float32)
    grad_rows = cotangent.astype(jnp.float32) * live_rows[:, None]
    matrix_list = [None] * LAYERS
    small_list = [None] * LAYERS
    for block_index in reversed(range(LAYERS)):
        weights = (
            lax.all_gather(w_qkv[block_index], "fsdp", axis=1, tiled=True),
            lax.all_gather(w_out[block_index], "fsdp", axis=1, tiled=True),
            lax.all_gather(w_in[block_index], "fsdp", axis=1, tiled=True),
            lax.all_gather(w_back[block_index], "fsdp", axis=2, tiled=True),
        )
        grad_rows, matrix_grads, small_grads = backward_block(
            grad_rows,
            stored_list[block_index],
            weights,
            ln_gain[block_index],
            ln_bias[block_index],
            w_router[block_index],
            expert_ids[block_index],
            row_start,
        )
        matrix_list[block_index] = (
            lax.psum_scatter(matrix_grads[0], "fsdp", scatter_dimension=1, tiled=True),
            lax.psum_scatter(matrix_grads[1], "fsdp", scatter_dimension=1, tiled=True),
            lax.psum_scatter(matrix_grads[2], "fsdp", scatter_dimension=1, tiled=True),
            lax.psum_scatter(matrix_grads[3], "fsdp", scatter_dimension=2, tiled=True),
        )
        small_list[block_index] = small_grads
    gain_grads, shift_grads, router_grads = lax.psum(
        (
            jnp.stack([entry[0] for entry in small_list]),
            jnp.stack([entry[1] for entry in small_list]),
            jnp.stack([entry[2] for entry in small_list]),
        ),
        ("fsdp", "heads", "tensor"),
    )
    qkv_grads = jnp.stack([entry[0] for entry in matrix_list])
    out_grads = jnp.stack([entry[1] for entry in matrix_list])
    in_grads = jnp.stack([entry[2] for entry in matrix_list])
    back_grads = jnp.stack([entry[3] for entry in matrix_list])
    return (
        residual.astype(jnp.bfloat16),
        grad_rows,
        qkv_grads,
        out_grads,
        gain_grads,
        shift_grads,
        router_grads,
        in_grads,
        back_grads,
    )


ROWS = -(-SEQ // 16) * 16
MESH = pl.DeviceIdType.MESH
F32, BF16 = jnp.float32, jnp.bfloat16
NN, NT, TN = (((1,), (0,)), ((), ())), (((1,), (1,)), ((), ())), (((0,), (0,)), ((), ()))


def mm(left, right, dims=NN):
    return lax.dot_general(left, right, dims, preferred_element_type=F32)


def whole(index, size):
    return pl.ds(pl.multiple_of(index * size, size), size)


def normal_parts(value):
    centred = value - jnp.mean(value, axis=-1, keepdims=True)
    scale = lax.rsqrt(jnp.mean(centred * centred, axis=-1, keepdims=True) + 1e-06)
    return centred * scale, scale


def normal_pull(grad, unit, scale, gains):
    grad_unit = grad * gains
    mean_grad = jnp.mean(grad_unit, axis=-1, keepdims=True)
    mean_both = jnp.mean(grad_unit * unit, axis=-1, keepdims=True)
    return scale * (grad_unit - mean_grad - unit * mean_both)


def gelu_parts(value):
    size = jnp.abs(value)
    step = 1.0 / (1.0 + 0.3275911 * 2.0**-0.5 * size)
    bell = jnp.exp(-0.5 * (value * value))
    series = 1.061405429 * step - 1.453152027
    series = series * step + 1.421413741
    series = series * step - 0.284496736
    series = series * step + 0.254829592
    tail = 0.5 * series * step * bell
    share = jnp.where(value < 0, tail, 1.0 - tail)
    return value * share, share + value * (bell * 0.3989422804014327)


class Exchange:
    def __init__(self, source, target, device, landing, send, recv):
        self.out = pltpu.make_async_remote_copy(
            source, target, send, recv, device_id=device, device_id_type=MESH
        )
        self.into = pltpu.make_async_remote_copy(
            landing, landing, send, recv, device_id=device, device_id_type=MESH
        )

        self.open = [True, True]
        self.out.start()

    def arrived(self):
        if self.open[0]:
            self.into.wait_recv()
        self.open[0] = False

    def sent(self):
        if self.open[1]:
            self.out.wait_send()
        self.open[1] = False

    def finish(self):
        self.arrived()
        self.sent()


class Kept:
    def __init__(self, source, target, semaphore):
        self.copy = pltpu.make_async_copy(source, target, semaphore)
        self.open = True
        self.copy.start()

    def arrived(self):
        if self.open:
            self.copy.wait()
        self.open = False

    sent = finish = arrived


def block_kernel(depth_z, images, local_count, refs):
    H = depth_z
    (
        tokens, cot, counts, wq, wo, gain, bias, wr, win_hbm, wback_hbm, named_in, slots_in,
        out, tgrad, wqg, wog, lng, lnb, wrg, gin_out, gback_out,
        stage, prow, wbuf, win, wback, rows_grad, rows_norm, big, wide,
        xsend, gsend, xrows, grows, xback, gback,
        normed, qkv, probs, mixed, middle, grad_mid, logit_grad,
        sib_out, sib_in, z_out, z_in, own_sum,
        att_in, plane_in, line_out, line_in,
        small_c, small_p, small_z, route_out, route_in, route_z, route_all,
        send_sems, recv_sems, local_sems,
    ) = refs
    own = images * ROWS
    width = tokens.shape[1]
    half = width // 128
    f, h, t = (lax.axis_index(name) for name in ("fsdp", "heads", "tensor"))
    s = 1 - t
    fx = [f, f + 1 - 2 * lax.rem(f, 2), lax.rem(f + 2, 4), 3 - f]
    hz = [lax.rem(h + d, H) for d in range(H)]
    hfrom = [lax.rem(h + H - d, H) for d in range(H)]
    after, before, across = lax.rem(2 * h + 1, 5), lax.rem(3 * h + 2, 5), 3 - h
    counter = [0]
    pending = []

    def exchange(source, target, device, landing):
        index = counter[0]
        counter[0] += 1
        made = Exchange(
            source, target, device, landing, send_sems.at[index], recv_sems.at[index]
        )
        pending.append(made)
        return made

    local_counter = [0]

    def kept(source, target):
        made = Kept(source, target, local_sems.at[local_counter[0]])
        local_counter[0] += 1
        pending.append(made)
        return made

    barrier = pltpu.get_barrier_semaphore()
    peers = [(f, hz[d], t) for d in range(1, H)] + [(f, h, s)]
    peers += [(fx[d], h, c) for d in range(1, 4) for c in (t, s)]
    for peer in peers:
        pl.semaphore_signal(barrier, inc=1, device_id=peer, device_id_type=MESH)

    for i in range(3):
        wbuf[i, h, t, :, whole(f, 128)] = wq[i]
    wbuf[3, h, t, :, whole(f, 128)] = wo[...]
    pl.semaphore_wait(barrier, len(peers))

    first = [
        exchange(*[wbuf.at[:, h, t, :, whole(f, 128)]] * 2, (f, hz[d], t),
                 wbuf.at[:, hfrom[d], t, :, whole(f, 128)])
        for d in range(1, H)
    ]

    depth, span = win_hbm.shape[1], win_hbm.shape[2]

    def move_in(d, c):
        landing = win.at[whole(fx[d], depth), whole(c, span)]
        target = win.at[whole(f, depth), whole(t, span)]
        return exchange(win_hbm.at[fx[d] * 2 + c], target, (fx[d], h, c), landing)

    def move_back(d, c):
        landing = wback.at[whole(c, span), whole(fx[d], depth)]
        target = wback.at[whole(t, span), whole(f, depth)]
        return exchange(wback_hbm.at[fx[d] * 2 + c], target, (fx[d], h, c), landing)

    expert_moves = [move_in(d, c) for d, c in ((1, t), (2, t), (1, s), (2, s))]
    mine = [
        kept(win_hbm.at[f * 2 + t], win.at[whole(f, depth), whole(t, span)]),
        kept(wback_hbm.at[f * 2 + t], wback.at[whole(t, span), whole(f, depth)]),
    ]

    row_index = lax.broadcasted_iota(jnp.int32, (ROWS, 1), 0)

    def image(source, b):
        if b == 0:
            stage[0 : images * SEQ, :] = source[...].astype(F32)
        return jnp.where(row_index < SEQ, stage[b * SEQ : b * SEQ + ROWS, :], 0.0)

    for b in range(images):
        live = ((h * 2 + t) * images + b < counts[0]).astype(F32)
        rows_grad[h * 2 + t, b * ROWS : (b + 1) * ROWS, :] = (image(cot, b) * live).astype(BF16)

    parts = [slice(0, own // 2), slice(own // 2, own)]

    def hop(rows, line, part, to, source):
        here = rows.at[line * 2 + t, parts[part]]
        return exchange(here, here, (f, to, t), rows.at[source * 2 + t, parts[part]])

    def beside(rows, line):
        here = rows.at[line * 2 + t, 0:own]
        return exchange(here, here, (f, h, s), rows.at[line * 2 + s, 0:own])

    class Spread:
        def __init__(self, rows):
            self.rows = rows
            self.down = [hop(rows, h, 0, after, before), None]
            self.up = [None, hop(rows, h, 1, before, after)]
            self.near = [beside(rows, h)]

        def second(self):
            self.down[1] = hop(self.rows, h, 1, after, before)
            self.up[0] = hop(self.rows, h, 0, before, after)

        def relay(self):
            self.down[0].arrived()
            self.far = [hop(self.rows, before, 0, after, across)]
            self.up[1].arrived()
            self.far.append(hop(self.rows, after, 1, before, across))

        def share(self):
            self.down[1].arrived()
            self.near.append(beside(self.rows, before))
            self.up[0].arrived()
            self.near.append(beside(self.rows, after))

        def close(self):
            for move in self.far:
                move.arrived()
            self.near.append(beside(self.rows, across))

        def blocks(self):
            lines = [h, before, after, across]
            moves = self.near + [None] * (4 - len(self.near))
            return [(line * 2 + t, None) for line in lines] + [
                (line * 2 + s, move) for line, move in zip(lines, moves)
            ]

        def sent(self):
            for move in self.down + self.up + self.far + self.near:
                move.sent()

    for b in range(images):
        unit, _ = normal_parts(image(tokens, b))
        normed[b * ROWS : (b + 1) * ROWS, :] = (unit * gain[0:1] + bias[0:1]).astype(BF16)

    for step in first:
        step.arrived()
    grad_spread = Spread(rows_grad)
    second = [
        exchange(*[wbuf.at[:, :, t, :, whole(f, 128)]] * 2, (fx[d], h, t),
                 wbuf.at[:, :, t, :, whole(fx[d], 128)])
        for d in range(1, 4)
    ]

    relative = named_in[...] - h * local_count
    wanted = (slots_in[...] >= 0) & (relative >= 0) & (relative < local_count)
    wanted = wanted & (lax.rem(relative + 2 * local_count, 2) == t)
    places = jnp.where(wanted, lax.div(relative, 2) * CAP + slots_in[...], -1)
    reach = -(-(images * ROWS) // 128) * 128 + 128
    tail = jnp.full((2, reach), -1, jnp.int32)
    places = jnp.concatenate([places, tail], axis=1)[:, 0 : places.shape[1] // 128 * 128 + reach]
    place_lane = lax.broadcasted_iota(jnp.int32, (2, reach), 1)
    for b in range(2 * H):
        rows = jnp.full((2, reach), -1, jnp.int32)
        for i in range(images):
            begin = (b * images + i) * SEQ - i * ROWS
            base = max(begin // 128, 0) * 128
            window = pltpu.roll(places[:, base : base + reach], (base - begin) % reach, 1)
            inside = (place_lane >= i * ROWS) & (place_lane < i * ROWS + SEQ)
            rows = jnp.where(inside, window, rows)
        prow[b, 0:2, :] = rows[:, 0 : prow.shape[2]]

    def mark_slots(b):
        for part in range(4):
            spot = lax.broadcasted_iota(jnp.int32, (CAP, own), 0) + CAP * part
            named = (prow[b, 0:1, 0:own] == spot) | (prow[b, 1:2, 0:own] == spot)
            big[b, part * CAP : (part + 1) * CAP, 0:own] = jnp.where(named, 1.0, 0.0).astype(BF16)

    grad_spread.second()
    pl.loop(0, H)(mark_slots)
    grad_spread.relay()
    pl.loop(H, 2 * H)(mark_slots)
    for step in second:
        step.arrived()
    third = exchange(*[wbuf.at[:, :, t]] * 2, (f, h, s), wbuf.at[:, :, s])

    for d, c in ((3, t), (3, s), (0, s)):
        expert_moves.append(move_in(d, c))
    for d, c in ((1, t), (2, t), (1, s), (2, s), (3, t), (3, s), (0, s)):
        expert_moves.append(move_back(d, c))

    grad_spread.share()
    third.arrived()

    for i in range(3):
        part = mm(normed[...], wbuf[i].reshape(width, width), NT)
        if i == 0:
            part = part * HEAD ** (-0.5)
        qkv[:, i * width : (i + 1) * width] = part.astype(BF16)
    lane = lax.broadcasted_iota(jnp.int32, (1, 128), 1)
    sides = [jnp.where(lane < HEAD, 1.0, 0.0).astype(BF16), jnp.where(lane < HEAD, 0.0, 1.0).astype(BF16)]
    key_index = lax.broadcasted_iota(jnp.int32, (1, ROWS), 1)

    def pair_of(index):
        b, pair = index // half, lax.rem(index, half)
        rows = whole(b, ROWS)
        cols = [whole(pair + i * half, 128) for i in range(3)]
        return rows, cols

    @pl.loop(0, images * half)
    def _(index):
        rows, cols = pair_of(index)
        query, key, value = (qkv[rows, col] for col in cols)
        total = jnp.zeros((ROWS, 128), F32)
        for side in range(2):
            score = mm(query * sides[side], key, NT)
            score = jnp.where(key_index < SEQ, score, -1e30)
            score = jnp.exp(score - jnp.max(score, axis=-1, keepdims=True))
            prob = score / jnp.sum(score, axis=-1, keepdims=True)
            probs[index * 2 + side] = prob
            total += mm(prob.astype(BF16), value * sides[side])
        mixed[rows, cols[0]] = total.astype(BF16)

    for b in range(images):
        rows = slice(b * ROWS, (b + 1) * ROWS)
        value = image(tokens, b) + mm(mixed[rows, :], wbuf[3].reshape(width, width))
        middle[rows, :] = value
        unit, _ = normal_parts(value)
        rows_norm[h * 2 + t, rows, :] = (unit * gain[1:2] + bias[1:2]).astype(BF16)

    norm_spread = Spread(rows_norm)
    grad_spread.close()

    def accumulate(rows, b, begin):
        for part in range(4):
            span_rows = slice(part * CAP, (part + 1) * CAP)
            value = mm(big[b, span_rows, 0:own], rows[b, 0:own])
            wide[span_rows, :] = value if begin else wide[span_rows, :] + value

    def accumulate_all(spread, order):
        blocks = spread.blocks()
        for place in order:
            b, move = blocks[place]
            if move is not None:
                move.arrived()
            accumulate(spread.rows, b, place == 0)

    def pack(send):
        for part in range(4):
            send[part] = wide[part * CAP : (part + 1) * CAP, :].astype(BF16)

    def to_group(d, send, landing):
        return exchange(send.at[fx[d]], landing.at[f], (fx[d], h, t), landing.at[fx[d]])

    def dispatch(send, landing, last=4):
        landing[f] = send[f]
        return [None] + [to_group(d, send, landing) for d in range(1, last)]

    accumulate_all(grad_spread, (0, 1, 2, 3))
    norm_spread.second()
    accumulate_all(grad_spread, (4, 5, 6, 7))
    pack(gsend)
    norm_spread.relay()
    grad_moved = dispatch(gsend, grows)
    norm_spread.share()
    accumulate_all(norm_spread, (0, 1, 2, 4, 5, 6))
    norm_spread.close()
    accumulate_all(norm_spread, (3, 7))
    pack(xsend)
    norm_moved = dispatch(xsend, xrows, 3)

    expert = h * local_count + f * 2 + t
    router_lane = lax.broadcasted_iota(jnp.int32, (1, wr.shape[0]), 1)
    chosen = (router_lane == expert).astype(F32)
    chunk = 512
    chunks = win.shape[1] // chunk
    for move in mine + expert_moves:
        move.arrived()
    back_moves = []
    for d in range(4):
        group = fx[d]
        here = whole(group, CAP)
        if d:
            norm_moved[d].arrived()
        rows = xrows[group]
        result = jnp.zeros((CAP, width), F32)
        for c in range(chunks):
            value, slope = gelu_parts(mm(rows, win[:, c * chunk : (c + 1) * chunk]))
            value = value.astype(BF16)
            big[c, here, :] = value
            wide[c * CAP : (c + 1) * CAP, :] = slope
            result += mm(value, wback[c * chunk : (c + 1) * chunk, :])
        logits = mm(rows, wr[...], NT)
        odds = jnp.exp(logits - jnp.max(logits, axis=-1, keepdims=True))
        odds = odds / jnp.sum(odds, axis=-1, keepdims=True)
        gate = jnp.sum(odds * chosen, axis=-1, keepdims=True)
        if d:
            grad_moved[d].finish()
            norm_moved[d].sent()
        gsend[group] = (gate * result).astype(BF16)
        row_grad = grows[group].astype(F32)
        gate_grad = jnp.sum(row_grad * result, axis=-1, keepdims=True)
        result_grad = (gate * row_grad).astype(BF16)
        grows[group] = result_grad
        logit = (gate_grad * gate * (chosen - odds)).astype(BF16)
        logit_grad[here, :] = logit
        parts_grad = []
        for c in range(chunks):
            grad = mm(result_grad, wback[c * chunk : (c + 1) * chunk, :], NT)
            grad = (grad * wide[c * CAP : (c + 1) * CAP, :]).astype(BF16)
            big[4 + c, here, :] = grad
            parts_grad.append(grad)
        total = mm(logit, wr[...]) + mm(jnp.concatenate(parts_grad, axis=1), win[...], NT)
        if d:
            xsend[group] = total.astype(BF16)
            back_moves.append(to_group(d, xsend, xback))
        else:
            xback[f] = total.astype(BF16)
            norm_moved.append(to_group(3, xsend, xrows))

    grad_spread.sent()
    norm_spread.sent()
    flat_rows = xrows[...].reshape(4 * CAP, width)
    flat_grad = grows[...].reshape(4 * CAP, width)
    for c in range(chunks):
        rows_grad[c] = mm(flat_rows, big[4 + c], TN).astype(BF16)
        rows_norm[c] = mm(big[c], flat_grad, TN).astype(BF16)
    route = mm(logit_grad[...], flat_rows, TN)
    share_rows = wr.shape[0] // 8
    for j in range(8):
        route_out[j, 0:share_rows, :] = route[j * share_rows : (j + 1) * share_rows]

    for move in back_moves:
        move.arrived()
    out_moves = dispatch(gsend, gback)[1:]

    halves = chunks // 2

    def to_owner(d, c, part, back):
        device, one = (fx[d], h, c), d == 0 and c is t
        span_part = slice(part * chunk, (part + 1) * chunk)
        if back:
            source = rows_norm.at[c * halves + part, :, whole(fx[d], depth)]
            target = gback_out.at[f * 2 + t, span_part]
            landing = gback_out.at[fx[d] * 2 + c, span_part]
        else:
            source = rows_grad.at[c * halves + part, whole(fx[d], depth), :]
            target = gin_out.at[f * 2 + t, :, span_part]
            landing = gin_out.at[fx[d] * 2 + c, :, span_part]
        if one:
            kept(source, target)
        else:
            exchange(source, target, device, landing)

    def to_owners(part, back):
        for d in (1, 2, 3, 0):
            for c in (t, s):
                to_owner(d, c, part, back)

    plane_peers = [(d, c) for d in range(4) for c in ((t, s) if d else (s,))]
    route_in[f * 2 + t] = route_out[f * 2 + t]
    route_moves = [
        exchange(route_out.at[fx[d] * 2 + c], route_in.at[f * 2 + t], (fx[d], h, c), route_in.at[fx[d] * 2 + c])
        for d, c in plane_peers
    ]

    def share(b, back):
        spots = jnp.transpose(prow[b])[0:own]
        slot = lax.broadcasted_iota(jnp.int32, (own, 4 * CAP), 1)
        named = (spots[:, 0:1] == slot) | (spots[:, 1:2] == slot)
        return mm(jnp.where(named, 1.0, 0.0).astype(BF16), back[...].reshape(4 * CAP, width))

    class Gather:
        def __init__(self, which, back, near_out, far_out):
            self.which, self.back = which, back
            self.near_out, self.far_out = near_out, far_out
            self.lines = [across, after, before, h]
            self.near = []

        def give(self, place):
            line = self.lines[place]
            self.near_out(place)[...] = share(line * 2 + s, self.back).astype(BF16)
            landing = sib_in.at[self.which, place]
            self.near.append(exchange(self.near_out(place), landing, (f, h, s), landing))

        def take(self, place):
            value = share(self.lines[place] * 2 + t, self.back)
            self.near[place].arrived()
            value = value + sib_in[self.which, place].astype(F32)
            if place == 3:
                own_sum[self.which] = value
            else:
                self.far_out(place)[...] = value.astype(BF16)

        def hop(self, place, part, to, slot):
            landing = z_in.at[self.which, slot, parts[part]]
            return exchange(self.far_out(place).at[parts[part]], landing, (f, to, t), landing)

        def start(self):
            self.first = [self.hop(0, 0, after, 0), self.hop(0, 1, before, 0)]

        def direct(self, place):
            part, to = ((1, after), (0, before))[place - 1]
            self.last = getattr(self, "last", []) + [self.hop(place, part, to, place)]

        def relay(self):
            for place, part, to in ((1, 0, after), (2, 1, before)):
                self.first[part].arrived()
                rows = self.far_out(place).at[parts[part]]
                passed = z_in[self.which, 0, parts[part], :].astype(F32)
                rows[...] = (rows[...].astype(F32) + passed).astype(BF16)
                self.last.append(self.hop(place, part, to, place))

        def total(self, rows):
            for move in self.last:
                move.arrived()
            total = own_sum[self.which, rows, :]
            for slot in (1, 2):
                total = total + z_in[self.which, slot, rows, :].astype(F32)
            return total

    def to_owners_first():
        to_owners(0, True)
        to_owners(1, True)
        to_owners(0, False)

    norm_sums = Gather(0, xback, lambda place: sib_out.at[place], lambda place: z_out.at[place])
    norm_sums.give(0)
    norm_sums.take(0)
    norm_sums.start()
    norm_sums.give(1)
    norm_sums.give(2)
    norm_sums.take(1)
    norm_sums.direct(1)
    norm_sums.take(2)
    norm_sums.direct(2)
    norm_sums.give(3)
    norm_sums.take(3)
    for move in out_moves:
        move.arrived()
    to_owners_first()
    out_sums = Gather(
        1, gback, lambda place: big.at[place, 0:own], lambda place: big.at[4 + place, 0:own]
    )
    out_sums.give(0)
    out_sums.take(0)
    for place in range(1, 4):
        out_sums.give(place)
    norm_sums.relay()
    for place in range(1, 4):
        out_sums.take(place)

    for move in route_moves:
        move.arrived()
    route = route_in[0, 0:share_rows, :]
    for j in range(1, 8):
        route = route + route_in[j, 0:share_rows, :]
    route_z[h, 0:share_rows, :] = route
    route_line = [
        exchange(route_z.at[h], route_z.at[h], (f, hz[d], t), route_z.at[hfrom[d]]) for d in range(1, H)
    ]

    for move in norm_sums.last:
        move.arrived()
    out_sums.start()
    small_c[t] = jnp.zeros(small_c.shape[1:], F32)
    for b in range(images):
        rows = slice(b * ROWS, (b + 1) * ROWS)
        grad = norm_sums.total(rows)
        unit, scale = normal_parts(middle[rows, :])
        small_c[t, 1:2] += jnp.sum(grad * unit, axis=0, keepdims=True)
        small_c[t, 3:4] += jnp.sum(grad, axis=0, keepdims=True)
        live = ((h * 2 + t) * images + b < counts[0]).astype(F32)
        grad = normal_pull(grad, unit, scale, gain[1:2]) + image(cot, b) * live
        grad_mid[rows, :] = grad

    out_sums.direct(1)
    out_sums.direct(2)

    for move in back_moves:
        move.sent()
    low = grad_mid[...].astype(BF16)
    count = H * 2 * 64
    wide[3 * count : 4 * count, :] = mm(mixed[...], low, TN)

    def wide_rows(i, other, core):
        return whole((i * H + other) * 2 + core, 64)

    def core_sums(span_i, others):
        for i in span_i:
            for other in others:
                xsend[i, whole(other, 64), :] = wide[wide_rows(i, other, s), :].astype(BF16)
        here = (slice(span_i.start, span_i.stop), whole(others[0], 64))
        if len(others) > 1:
            here = (here[0], slice(0, H * 64))
        landing = att_in.at[here]
        return here, exchange(xsend.at[here], landing, (f, h, s), landing)

    def plane_sums(span_i, others, near):
        here, move = near
        move.finish()
        for i in span_i:
            for other in others:
                place, low_rows = wide_rows(i, other, t), whole(other, 64)
                value = wide[place, :] + att_in[i, low_rows, :].astype(F32)
                wide[place, :] = value
                xsend[i, low_rows, :] = value.astype(BF16)
        return [
            exchange(
                xsend.at[(*here, whole(fx[d], 128))], plane_in.at[(f, *here)],
                (fx[d], h, t), plane_in.at[(fx[d], *here)],
            )
            for d in range(1, 4)
        ]

    def own_columns(i, other):
        value = wide[wide_rows(i, other, t), whole(f, 128)]
        for d in range(1, 4):
            value = value + plane_in[fx[d], i, whole(other, 64), :].astype(F32)
        return value

    last_near = core_sums(range(3, 4), list(range(H)))
    mixed[...] = mm(low, wbuf[3].reshape(width, width), NT).astype(BF16)

    def attention_back(index):
        rows, cols = pair_of(index)
        query, key, value = (qkv[rows, col] for col in cols)
        pulled = mixed[rows, cols[0]]
        grads = [jnp.zeros((ROWS, 128), F32) for _ in range(3)]
        for side in range(2):
            prob = probs[index * 2 + side]
            one = pulled * sides[side]
            prob_grad = mm(one, value, NT)
            grads[2] += mm(prob.astype(BF16), one, TN)
            inner = jnp.sum(prob * prob_grad, axis=-1, keepdims=True)
            score_grad = (prob * (prob_grad - inner)).astype(BF16)
            grads[0] += mm(score_grad, key * sides[side])
            grads[1] += mm(score_grad, query * sides[side], TN)
        grads[0] = grads[0] * HEAD ** (-0.5)
        for grad, col in zip(grads, cols):
            qkv[rows, col] = grad.astype(BF16)

    order = [hz[1], hz[2], hz[3], hz[0]]
    nears, planes = [], []
    for turn, other in enumerate(order):
        pl.loop(0, images)(lambda b, other=other: attention_back(b * half + other))
        for i in range(3):
            rows = pl.ds(pl.multiple_of((i * H + other) * 128, 128), 128)
            wide[rows, :] = mm(qkv[:, whole(i * half + other, 128)], normed[...], TN)
        nears.append(core_sums(range(3), [other]))
        if turn == 0:
            last_plane = plane_sums(range(3, 4), list(range(H)), last_near)
        else:
            planes.append(plane_sums(range(3), [order[turn - 1]], nears[turn - 1]))
    out_sums.relay()

    for b in range(images):
        rows = slice(b * ROWS, (b + 1) * ROWS)
        grad = jnp.zeros((ROWS, width), F32)
        for i in range(3):
            grad += mm(qkv[rows, i * width : (i + 1) * width], wbuf[i].reshape(width, width))
        unit, scale = normal_parts(image(tokens, b))
        small_c[t, 0:1] += jnp.sum(grad * unit, axis=0, keepdims=True)
        small_c[t, 2:3] += jnp.sum(grad, axis=0, keepdims=True)
        grad = normal_pull(grad, unit, scale, gain[0:1]) + grad_mid[rows, :]
        tgrad[b * SEQ : (b + 1) * SEQ, :] = grad[0:SEQ]
    small_near = exchange(small_c.at[t], small_c.at[t], (f, h, s), small_c.at[s])

    planes.append(plane_sums(range(3), [order[3]], nears[3]))
    small_near.arrived()
    small_p[f] = small_c[0] + small_c[1]
    small_plane = [
        exchange(small_p.at[f], small_p.at[f], (fx[d], h, t), small_p.at[fx[d]]) for d in range(1, 4)
    ]
    for move in route_line:
        move.arrived()
    route = route_z[0]
    for d in range(1, H):
        route = route + route_z[d]
    route_all[f * 2 + t] = route
    route_last = [
        exchange(route_all.at[f * 2 + t], route_all.at[f * 2 + t], (fx[d], h, c), route_all.at[fx[d] * 2 + c])
        for d, c in plane_peers
    ]

    for move in last_plane:
        move.arrived()
    line = []
    for turn in range(3):
        for move in planes[turn]:
            move.arrived()
        other = order[turn]
        for i in range(4):
            line_out[other, i] = own_columns(i, other).astype(BF16)
        d = turn + 1
        line.append(
            exchange(line_out.at[other], line_in.at[h], (f, other, t), line_in.at[hfrom[d]])
        )
    for move in planes[3]:
        move.arrived()
    to_owners(1, False)
    for move in small_plane:
        move.arrived()
    small_z[h] = (small_p[0] + small_p[1]) + (small_p[2] + small_p[3])
    small_line = [
        exchange(small_z.at[h], small_z.at[h], (f, hz[d], t), small_z.at[hfrom[d]]) for d in range(1, H)
    ]
    for move in route_last:
        move.arrived()
    for j in range(8):
        wrg[j * share_rows : (j + 1) * share_rows, :] = route_all[j, 0:share_rows, :]

    for b in range(images):
        rows = slice(b * ROWS, (b + 1) * ROWS)
        value = middle[rows, :] + out_sums.total(rows)
        stage[b * SEQ : (b + 1) * SEQ, :] = value[0:SEQ]
    out[...] = stage[0 : images * SEQ, :].astype(BF16)

    for move in line:
        move.arrived()
    for i in range(4):
        value = own_columns(i, h)
        for d in range(1, H):
            value = value + line_in[hfrom[d], i].astype(F32)
        if i < 3:
            wqg[i] = value
        else:
            wog[...] = value
    for move in small_line:
        move.arrived()
    total = small_z[0]
    for d in range(1, H):
        total = total + small_z[d]
    lng[...] = total[0:2]
    lnb[...] = total[2:4]

    for move in pending:
        move.finish()


def finish_kernel(*refs):
    sources, targets = refs[:9], refs[9:18]
    held, wider = refs[18:27], refs[27:29]
    in_sems, out_sems = refs[29], refs[30]
    experts = sources[7].shape[0]
    inward, outward = [], []

    def begin(source, target, semaphores, index):
        copy = pltpu.make_async_copy(source, target, semaphores.at[index])
        copy.start()
        return copy

    for e in range(experts):
        for k in (7, 8):
            index = 7 + 2 * e + k - 7
            inward.append((e, k, index, begin(sources[k].at[e], held[k].at[e], in_sems, index)))
    small = [begin(sources[k], held[k], in_sems, k) for k in range(7)]
    for e, k, index, copy in inward:
        copy.wait()
        wider[k - 7][e] = held[k][e].astype(F32)
        outward.append(begin(wider[k - 7].at[e], targets[k].at[e], out_sems, index))
    for k, copy in enumerate(small):
        copy.wait()
        outward.append(begin(held[k], targets[k], out_sems, k))
    for copy in outward:
        copy.wait()


def fast_device(
    tokens,
    cotangent,
    image_counts,
    w_qkv,
    w_out,
    ln_gain,
    ln_bias,
    w_router,
    w_in,
    w_back,
    expert_ids,
    slots,
):
    H = lax.axis_size("heads")
    own_rows, width = tokens.shape
    images = own_rows // SEQ
    own = images * ROWS
    local_count, depth, span = w_in.shape[1:]
    experts = w_router.shape[2]
    hidden = span * 2
    vmem = pl.BlockSpec(memory_space=pltpu.VMEM)
    smem = pl.BlockSpec(memory_space=pltpu.SMEM)
    anywhere = pl.BlockSpec(memory_space=pl.ANY)
    shape = jax.ShapeDtypeStruct

    def low(*dims):
        return pltpu.VMEM(dims, BF16)

    def full(*dims):
        return pltpu.VMEM(dims, F32)

    outs = pl.pallas_call(
        lambda *refs: block_kernel(H, images, local_count, refs),
        out_shape=(
            shape((own_rows, width), BF16),
            shape((own_rows, width), F32),
            shape((3, 64, depth), F32),
            shape((64, depth), F32),
            shape((2, width), F32),
            shape((2, width), F32),
            shape((experts, width), F32),
            shape((local_count, depth, span), BF16),
            shape((local_count, span, depth), BF16),
        ),
        in_specs=[vmem, vmem, smem, vmem, vmem, vmem, vmem, vmem, anywhere, anywhere, vmem, vmem],
        out_specs=[vmem] * 7 + [anywhere] * 2,
        scratch_shapes=[
            full(images * SEQ + 16, width),
            pltpu.VMEM((2 * H, 8, -(-own // 128) * 128), jnp.int32),
            low(4, H, 2, 64, width),
            low(width, hidden),
            low(hidden, width),
            low(2 * H, 512, width),
            low(2 * H, 512, width),
            low(8, 4 * CAP, 512),
            full(8 * CAP, width),
            low(4, CAP, width),
            low(4, CAP, width),
            low(4, CAP, width),
            low(4, CAP, width),
            low(4, CAP, width),
            low(4, CAP, width),
            low(own, width),
            low(own, 3 * width),
            full(images * width // HEAD, ROWS, ROWS),
            low(own, width),
            full(own, width),
            full(own, width),
            low(4 * CAP, experts),
            low(H, own, width),
            low(2, H, own, width),
            low(3, own, width),
            low(2, 3, own, width),
            full(2, own, width),
            low(4, H * 64, width),
            low(4, 4, H * 64, 128),
            low(H, 4, 64, 128),
            low(H, 4, 64, 128),
            full(2, 8, width),
            full(4, 8, width),
            full(H, 8, width),
            full(8, 8, width),
            full(8, 8, width),
            full(H, 8, width),
            full(8, 8, width),
            pltpu.SemaphoreType.DMA((192,)),
            pltpu.SemaphoreType.DMA((192,)),
            pltpu.SemaphoreType.DMA((16,)),
        ],
        compiler_params=pltpu.CompilerParams(
            collective_id=0, has_side_effects=True, vmem_limit_bytes=62 * 2**20
        ),
        name="block",
    )(
        tokens, cotangent, image_counts, jnp.transpose(w_qkv[0], (0, 2, 1)), w_out[0], ln_gain[0], ln_bias[0],
        jnp.transpose(w_router[0]),
        w_in[0], w_back[0], jnp.transpose(expert_ids[0]), jnp.transpose(slots[0]),
    )
    sems = pltpu.SemaphoreType.DMA((7 + 2 * local_count,))
    outs = pl.pallas_call(
        finish_kernel,
        out_shape=[shape(part.shape, F32 if i >= 7 else part.dtype) for i, part in enumerate(outs)],
        in_specs=[anywhere] * 9,
        out_specs=[anywhere] * 9,
        scratch_shapes=[pltpu.VMEM(part.shape, part.dtype) for part in outs]
        + [full(*part.shape) for part in outs[7:]]
        + [sems, sems],
        compiler_params=pltpu.CompilerParams(vmem_limit_bytes=62 * 2**20),
        name="finish",
    )(*outs)
    block_out, token_grad, qkv_grad, out_grad, gains, shifts, router, in_grad, back_grad = outs
    return (
        block_out,
        token_grad,
        jnp.transpose(qkv_grad, (0, 2, 1))[None],
        out_grad[None],
        gains[None],
        shifts[None],
        jnp.transpose(router)[None],
        in_grad[None],
        back_grad[None],
    )


def solution(mesh):
    def program(*arrays):
        sizes = dict(mesh.shape)
        devices = sizes["fsdp"] * sizes["heads"] * sizes["tensor"]
        own_rows = arrays[0].shape[0] // devices
        one_expert = sizes["fsdp"] == 4 and sizes["tensor"] == 2 and arrays[8].shape[1] == devices
        one_expert = one_expert and sizes["heads"] == 4 and own_rows % (2 * SEQ) == 0
        return placed(mesh, fast_device if one_expert else on_device)(*arrays)

    return program


def placed(mesh, on_device):
    return jax.shard_map(
        on_device,
        mesh=mesh,
        in_specs=(
            P(("fsdp", "heads", "tensor"), None),
            P(("fsdp", "heads", "tensor"), None),
            P("fsdp"),
            P(None, None, "fsdp", ("heads", "tensor")),
            P(None, ("heads", "tensor"), "fsdp"),
            P(),
            P(),
            P(),
            P(None, "heads", "fsdp", "tensor"),
            P(None, "heads", "tensor", "fsdp"),
            P(None, "fsdp", None),
            P(None, "fsdp", None),
        ),
        out_specs=(
            P(("fsdp", "heads", "tensor"), None),
            P(("fsdp", "heads", "tensor"), None),
            P(None, None, "fsdp", ("heads", "tensor")),
            P(None, ("heads", "tensor"), "fsdp"),
            P(),
            P(),
            P(),
            P(None, "heads", "fsdp", "tensor"),
            P(None, "heads", "tensor", "fsdp"),
        ),
        check_vma=False,
    )
```

```python
import jax
import jax.numpy as jnp
from jax import lax
from jax.experimental import pallas as pl
from jax.experimental.pallas import tpu as pltpu
from jax.sharding import PartitionSpec as P

HEAD = 64
SEQ = 197
LAYERS = 1
CAP = 256


def layer_norm(value, ln_gains, ln_shift):
    centred = value - jnp.mean(value, axis=-1, keepdims=True)
    spread = jnp.mean(centred * centred, axis=-1, keepdims=True)
    return centred * lax.rsqrt(spread + 1e-06) * ln_gains + ln_shift


def gelu_exact(value):
    return jax.nn.gelu(value, approximate=False)


def with_zero_row(matrix):
    return jnp.concatenate([matrix, jnp.zeros((1,) + matrix.shape[1:], matrix.dtype)], axis=0)


def slot_tables(named_expert, slot_rows, first_expert, local_experts):
    group_rows = named_expert.shape[0]
    is_local = (
        (slot_rows >= 0)
        & (named_expert >= first_expert)
        & (named_expert < first_expert + local_experts)
    )
    places = jnp.where(
        is_local, (named_expert - first_expert) * CAP + slot_rows, local_experts * CAP
    )
    picked = jnp.full((local_experts * CAP + 1,), 2 * group_rows, jnp.int32)
    picked = picked.at[places.reshape(-1)].set(jnp.arange(2 * group_rows, dtype=jnp.int32))
    return (places, picked[: local_experts * CAP])


def joined_qkv(qkv_weight):
    head_cols = qkv_weight.shape[2]
    return jnp.transpose(qkv_weight, (1, 0, 2)).reshape(qkv_weight.shape[1], 3 * head_cols)


def forward_block(
    residual, weights, ln_gains, ln_shift, router_weight, named_expert, slot_rows, first_expert
):
    qkv_weight, out_weight, in_weight, back_weight = weights
    own_rows, widths = residual.shape
    group_rows = named_expert.shape[0]
    head_cols = qkv_weight.shape[2]
    local_experts = in_weight.shape[0]
    head_shape = (group_rows // SEQ, SEQ, head_cols // HEAD, HEAD)
    q_scale = HEAD ** (-0.5)
    flat_qkv = joined_qkv(qkv_weight)
    normed_rows = layer_norm(residual, ln_gains[0], ln_shift[0]).astype(jnp.bfloat16)
    normed = lax.all_gather(normed_rows, ("heads", "tensor"), axis=0, tiled=True)
    projected = jnp.dot(normed, flat_qkv, preferred_element_type=jnp.float32)
    queries = (projected[:, :head_cols] * q_scale).astype(jnp.bfloat16).reshape(head_shape)
    key_rows = projected[:, head_cols : 2 * head_cols].astype(jnp.bfloat16).reshape(head_shape)
    value_rows = projected[:, 2 * head_cols :].astype(jnp.bfloat16).reshape(head_shape)
    scores = jnp.einsum("bqhd,bkhd->bhqk", queries, key_rows, preferred_element_type=jnp.float32)
    log_total = jax.nn.logsumexp(scores, axis=-1)
    attn_probs = jax.nn.softmax(scores, axis=-1).astype(jnp.bfloat16)
    mixed_rows = jnp.einsum(
        "bhqk,bkhd->bqhd", attn_probs, value_rows, preferred_element_type=jnp.float32
    )
    mixed_rows = mixed_rows.reshape(group_rows, head_cols).astype(jnp.bfloat16)
    middle = residual + lax.psum_scatter(
        jnp.dot(mixed_rows, out_weight, preferred_element_type=jnp.float32),
        ("heads", "tensor"),
        scatter_dimension=0,
        tiled=True,
    )
    head_full = ()
    normed_two_rows = layer_norm(middle, ln_gains[1], ln_shift[1]).astype(jnp.bfloat16)
    normed_two = lax.all_gather(normed_two_rows, ("heads", "tensor"), axis=0, tiled=True)
    router = jax.nn.softmax(
        jnp.dot(normed_two, router_weight, preferred_element_type=jnp.float32), axis=-1
    )
    gate_values = jnp.take_along_axis(router, named_expert, axis=1) * (slot_rows >= 0)
    places, picked = slot_tables(named_expert, slot_rows, first_expert, local_experts)
    routed = with_zero_row(normed_two)[picked // 2].reshape(local_experts, CAP, widths)
    hidden = jnp.einsum("ecd,edf->ecf", routed, in_weight, preferred_element_type=jnp.float32)
    active = gelu_exact(hidden).astype(jnp.bfloat16)
    result = jnp.einsum("ecf,efd->ecd", active, back_weight, preferred_element_type=jnp.float32)
    flat_result = with_zero_row(result.reshape(local_experts * CAP, widths))
    block_out = middle + lax.psum_scatter(
        (
            flat_result[places[:, 0]] * gate_values[:, 0:1]
            + flat_result[places[:, 1]] * gate_values[:, 1:2]
        ).astype(jnp.bfloat16),
        ("heads", "tensor"),
        scatter_dimension=0,
        tiled=True,
    ).astype(jnp.float32)
    stored = (
        residual,
        middle,
        normed,
        queries,
        key_rows,
        value_rows,
        log_total,
        mixed_rows,
        normed_two_rows,
        router,
        gate_values,
        places,
        picked,
        routed,
        hidden,
        active,
        flat_result,
    )
    return (block_out, stored, head_full)


def backward_block(
    grad_rows, stored, weights, ln_gains, ln_shift, router_weight, named_expert, row_start
):
    qkv_weight, out_weight, in_weight, back_weight = weights
    (
        residual,
        middle,
        normed,
        queries,
        key_rows,
        value_rows,
        log_total,
        mixed_rows,
        normed_two_rows,
        router,
        gate_values,
        places,
        picked,
        routed,
        hidden,
        active,
        flat_result,
    ) = stored
    own_rows, widths = residual.shape
    group_rows = named_expert.shape[0]
    head_cols = qkv_weight.shape[2]
    local_experts = in_weight.shape[0]
    expert_count = router.shape[1]
    q_scale = HEAD ** (-0.5)
    flat_qkv = joined_qkv(qkv_weight)
    grad_moe = lax.all_gather(
        grad_rows.astype(jnp.bfloat16), ("heads", "tensor"), axis=0, tiled=True
    )
    back_rows = with_zero_row(grad_moe)[picked // 2].astype(jnp.float32)
    gate_slots = with_zero_row(gate_values.reshape(-1))[picked]
    gate_grad_slots = jnp.sum(back_rows * flat_result[:-1], axis=1)
    gate_grads = with_zero_row(gate_grad_slots)[places]
    expert_range = jnp.arange(expert_count, dtype=jnp.int32)
    router_part = jnp.sum(
        gate_grads[:, :, None]
        * (named_expert[:, :, None] == expert_range[None, None, :]).astype(jnp.float32),
        axis=1,
    )
    grad_result = (
        (gate_slots[:, None] * back_rows).astype(jnp.bfloat16).reshape(local_experts, CAP, widths)
    )
    grad_active = jnp.einsum(
        "ecd,efd->ecf", grad_result, back_weight, preferred_element_type=jnp.float32
    )
    gelu_value, gelu_pull = jax.vjp(gelu_exact, hidden)
    grad_hidden = gelu_pull(grad_active)[0].astype(jnp.bfloat16)
    back_grad = jnp.einsum("ecf,ecd->efd", active, grad_result, preferred_element_type=jnp.float32)
    in_grad = jnp.einsum("ecd,ecf->edf", routed, grad_hidden, preferred_element_type=jnp.float32)
    grad_routed = jnp.einsum(
        "ecf,edf->ecd", grad_hidden, in_weight, preferred_element_type=jnp.float32
    )
    grad_routed = with_zero_row(grad_routed.reshape(local_experts * CAP, widths))
    token_part = grad_routed[places[:, 0]] + grad_routed[places[:, 1]]
    grad_normed_two, router_rows = (
        lax.psum_scatter(token_part, ("heads", "tensor"), scatter_dimension=0, tiled=True),
        lax.psum_scatter(router_part, ("heads", "tensor"), scatter_dimension=0, tiled=True),
    )
    router_own = lax.dynamic_slice_in_dim(router, row_start, own_rows, 0)
    grad_logits = (
        router_own * (router_rows - jnp.sum(router_own * router_rows, axis=-1, keepdims=True))
    ).astype(jnp.bfloat16)
    router_grad = jnp.einsum(
        "td,te->de", normed_two_rows, grad_logits, preferred_element_type=jnp.float32
    )
    grad_normed_two = grad_normed_two + jnp.einsum(
        "te,de->td", grad_logits, router_weight, preferred_element_type=jnp.float32
    )
    norm_value, norm_pull = jax.vjp(layer_norm, middle, ln_gains[1], ln_shift[1])
    grad_middle, gain_two, shift_two = norm_pull(grad_normed_two)
    grad_middle = grad_middle + grad_rows
    grad_attn = lax.all_gather(
        grad_middle.astype(jnp.bfloat16), ("heads", "tensor"), axis=0, tiled=True
    )
    out_grad = jnp.einsum("tc,td->cd", mixed_rows, grad_attn, preferred_element_type=jnp.float32)
    grad_mixed = jnp.einsum("td,cd->tc", grad_attn, out_weight, preferred_element_type=jnp.float32)
    grad_mixed = grad_mixed.astype(jnp.bfloat16).reshape(queries.shape)
    scores = jnp.einsum("bqhd,bkhd->bhqk", queries, key_rows, preferred_element_type=jnp.float32)
    attn_probs = jnp.exp(scores - log_total[..., None])
    grad_values = jnp.einsum(
        "bhqk,bqhd->bkhd",
        attn_probs.astype(jnp.bfloat16),
        grad_mixed,
        preferred_element_type=jnp.float32,
    )
    grad_probs = jnp.einsum(
        "bqhd,bkhd->bhqk", grad_mixed, value_rows, preferred_element_type=jnp.float32
    )
    grad_scores = (
        attn_probs * (grad_probs - jnp.sum(attn_probs * grad_probs, axis=-1, keepdims=True))
    ).astype(jnp.bfloat16)
    grad_queries = jnp.einsum(
        "bhqk,bkhd->bqhd", grad_scores, key_rows, preferred_element_type=jnp.float32
    )
    grad_keys = jnp.einsum(
        "bhqk,bqhd->bkhd", grad_scores, queries, preferred_element_type=jnp.float32
    )
    grad_projected = jnp.concatenate(
        [
            grad_queries.reshape(group_rows, head_cols),
            grad_keys.reshape(group_rows, head_cols),
            grad_values.reshape(group_rows, head_cols),
        ],
        axis=1,
    ).astype(jnp.bfloat16)
    qkv_flat_grad = jnp.einsum(
        "td,tc->dc", normed, grad_projected, preferred_element_type=jnp.float32
    )
    column_scale = jnp.concatenate(
        [jnp.full((head_cols,), q_scale, jnp.float32), jnp.ones((2 * head_cols,), jnp.float32)]
    )
    qkv_grad = jnp.transpose(
        (qkv_flat_grad * column_scale).reshape(widths, 3, head_cols), (1, 0, 2)
    )
    query_term = (
        jnp.einsum(
            "tc,dc->td",
            grad_projected[:, :head_cols],
            flat_qkv[:, :head_cols],
            preferred_element_type=jnp.float32,
        )
        * q_scale
    )
    grad_normed = lax.psum_scatter(
        query_term
        + jnp.einsum(
            "tc,dc->td",
            grad_projected[:, head_cols:],
            flat_qkv[:, head_cols:],
            preferred_element_type=jnp.float32,
        ),
        ("heads", "tensor"),
        scatter_dimension=0,
        tiled=True,
    )
    first_value, first_pull = jax.vjp(layer_norm, residual, ln_gains[0], ln_shift[0])
    grad_input, gain_one, shift_one = first_pull(grad_normed)
    grad_input = grad_input + grad_middle
    matrix_grads = (qkv_grad, out_grad, in_grad, back_grad)
    small_grads = (jnp.stack([gain_one, gain_two]), jnp.stack([shift_one, shift_two]), router_grad)
    return (grad_input, matrix_grads, small_grads)


def on_device(
    tokens,
    cotangent,
    image_counts,
    w_qkv,
    w_out,
    ln_gain,
    ln_bias,
    w_router,
    w_in,
    w_back,
    expert_ids,
    slots,
):
    own_rows = tokens.shape[0]
    row_start = lax.axis_index(("heads", "tensor")) * own_rows
    first_expert = lax.axis_index("heads") * w_in.shape[1]
    residual = tokens.astype(jnp.float32)
    head_list = []
    block_index = 0
    weights = (
        lax.all_gather(w_qkv[block_index], "fsdp", axis=1, tiled=True),
        lax.all_gather(w_out[block_index], "fsdp", axis=1, tiled=True),
        lax.all_gather(w_in[block_index], "fsdp", axis=1, tiled=True),
        lax.all_gather(w_back[block_index], "fsdp", axis=2, tiled=True),
    )
    residual, stored, head_full = forward_block(
        residual,
        weights,
        ln_gain[block_index],
        ln_bias[block_index],
        w_router[block_index],
        expert_ids[block_index],
        slots[block_index],
        first_expert,
    )
    stored_list = [stored]
    head_list.append(head_full)
    image_index = (row_start + jnp.arange(own_rows, dtype=jnp.int32)) // SEQ
    live_rows = (image_index < image_counts[0]).astype(jnp.float32)
    grad_rows = cotangent.astype(jnp.float32) * live_rows[:, None]
    matrix_list = [None] * LAYERS
    small_list = [None] * LAYERS
    for block_index in reversed(range(LAYERS)):
        weights = (
            lax.all_gather(w_qkv[block_index], "fsdp", axis=1, tiled=True),
            lax.all_gather(w_out[block_index], "fsdp", axis=1, tiled=True),
            lax.all_gather(w_in[block_index], "fsdp", axis=1, tiled=True),
            lax.all_gather(w_back[block_index], "fsdp", axis=2, tiled=True),
        )
        grad_rows, matrix_grads, small_grads = backward_block(
            grad_rows,
            stored_list[block_index],
            weights,
            ln_gain[block_index],
            ln_bias[block_index],
            w_router[block_index],
            expert_ids[block_index],
            row_start,
        )
        matrix_list[block_index] = (
            lax.psum_scatter(matrix_grads[0], "fsdp", scatter_dimension=1, tiled=True),
            lax.psum_scatter(matrix_grads[1], "fsdp", scatter_dimension=1, tiled=True),
            lax.psum_scatter(matrix_grads[2], "fsdp", scatter_dimension=1, tiled=True),
            lax.psum_scatter(matrix_grads[3], "fsdp", scatter_dimension=2, tiled=True),
        )
        small_list[block_index] = small_grads
    gain_grads, shift_grads, router_grads = lax.psum(
        (
            jnp.stack([entry[0] for entry in small_list]),
            jnp.stack([entry[1] for entry in small_list]),
            jnp.stack([entry[2] for entry in small_list]),
        ),
        ("fsdp", "heads", "tensor"),
    )
    qkv_grads = jnp.stack([entry[0] for entry in matrix_list])
    out_grads = jnp.stack([entry[1] for entry in matrix_list])
    in_grads = jnp.stack([entry[2] for entry in matrix_list])
    back_grads = jnp.stack([entry[3] for entry in matrix_list])
    return (
        residual.astype(jnp.bfloat16),
        grad_rows,
        qkv_grads,
        out_grads,
        gain_grads,
        shift_grads,
        router_grads,
        in_grads,
        back_grads,
    )


ROWS = -(-SEQ // 16) * 16
MESH = pl.DeviceIdType.MESH
F32, BF16 = jnp.float32, jnp.bfloat16
NN, NT, TN = (((1,), (0,)), ((), ())), (((1,), (1,)), ((), ())), (((0,), (0,)), ((), ()))


def mm(left, right, dims=NN):
    return lax.dot_general(left, right, dims, preferred_element_type=F32)


def whole(index, size):
    return pl.ds(pl.multiple_of(index * size, size), size)


def normal_parts(value):
    centred = value - jnp.mean(value, axis=-1, keepdims=True)
    scale = lax.rsqrt(jnp.mean(centred * centred, axis=-1, keepdims=True) + 1e-06)
    return centred * scale, scale


def normal_pull(grad, unit, scale, gains):
    grad_unit = grad * gains
    mean_grad = jnp.mean(grad_unit, axis=-1, keepdims=True)
    mean_both = jnp.mean(grad_unit * unit, axis=-1, keepdims=True)
    return scale * (grad_unit - mean_grad - unit * mean_both)


def gelu_parts(value):
    size = jnp.abs(value)
    step = 1.0 / (1.0 + 0.3275911 * 2.0**-0.5 * size)
    bell = jnp.exp(-0.5 * (value * value))
    series = 1.061405429 * step - 1.453152027
    series = series * step + 1.421413741
    series = series * step - 0.284496736
    series = series * step + 0.254829592
    tail = 0.5 * series * step * bell
    share = jnp.where(value < 0, tail, 1.0 - tail)
    return value * share, share + value * (bell * 0.3989422804014327)


class Exchange:
    def __init__(self, source, target, device, landing, send, recv):
        self.out = pltpu.make_async_remote_copy(
            source, target, send, recv, device_id=device, device_id_type=MESH
        )
        self.into = pltpu.make_async_remote_copy(
            landing, landing, send, recv, device_id=device, device_id_type=MESH
        )

        self.open = [True, True]
        self.out.start()

    def arrived(self):
        if self.open[0]:
            self.into.wait_recv()
        self.open[0] = False

    def sent(self):
        if self.open[1]:
            self.out.wait_send()
        self.open[1] = False

    def finish(self):
        self.arrived()
        self.sent()


class Kept:
    def __init__(self, source, target, semaphore):
        self.copy = pltpu.make_async_copy(source, target, semaphore)
        self.open = True
        self.copy.start()

    def arrived(self):
        if self.open:
            self.copy.wait()
        self.open = False

    sent = finish = arrived


def block_kernel(depth_z, images, local_count, refs):
    H = depth_z
    (
        tokens, cot, counts, wq, wo, gain, bias, wr, win_hbm, wback_hbm, named_in, slots_in,
        out, tgrad, wqg, wog, lng, lnb, wrg, gin_out, gback_out,
        stage, prow, wbuf, win, wback, rows_grad, rows_norm, big, wide,
        xsend, gsend, xrows, grows, xback, gback,
        normed, qkv, probs, mixed, middle, grad_mid, logit_grad,
        sib_out, sib_in, z_out, z_in, own_sum,
        att_in, plane_in, line_out, line_in,
        small_c, small_p, small_z, route_out, route_in, route_z, route_all,
        send_sems, recv_sems, local_sems,
    ) = refs
    own_rows, width = tokens.shape
    flat = -(-own_rows // 16) * 16
    half = width // 128
    f, h, t = (lax.axis_index(name) for name in ("fsdp", "heads", "tensor"))
    s = 1 - t
    fx = [f, f + 1 - 2 * lax.rem(f, 2), lax.rem(f + 2, 4), 3 - f]
    hz = [lax.rem(h + d, H) for d in range(H)]
    hfrom = [lax.rem(h + H - d, H) for d in range(H)]
    after, before, across = lax.rem(2 * h + 1, 5), lax.rem(3 * h + 2, 5), 3 - h
    counter = [0]
    pending = []

    def exchange(source, target, device, landing):
        index = counter[0]
        counter[0] += 1
        made = Exchange(
            source, target, device, landing, send_sems.at[index], recv_sems.at[index]
        )
        pending.append(made)
        return made

    local_counter = [0]

    def kept(source, target):
        made = Kept(source, target, local_sems.at[local_counter[0]])
        local_counter[0] += 1
        pending.append(made)
        return made

    barrier = pltpu.get_barrier_semaphore()
    peers = [(f, hz[d], t) for d in range(1, H)] + [(f, h, s)]
    peers += [(fx[d], h, c) for d in range(1, 4) for c in (t, s)]
    for peer in peers:
        pl.semaphore_signal(barrier, inc=1, device_id=peer, device_id_type=MESH)

    for i in range(3):
        wbuf[i, h, t, :, whole(f, 128)] = wq[i]
    wbuf[3, h, t, :, whole(f, 128)] = wo[...]
    pl.semaphore_wait(barrier, len(peers))

    first = [
        exchange(*[wbuf.at[:, h, t, :, whole(f, 128)]] * 2, (f, hz[d], t),
                 wbuf.at[:, hfrom[d], t, :, whole(f, 128)])
        for d in range(1, H)
    ]

    depth, span = win_hbm.shape[1], win_hbm.shape[2]

    def move_in(d, c):
        landing = win.at[whole(fx[d], depth), whole(c, span)]
        target = win.at[whole(f, depth), whole(t, span)]
        return exchange(win_hbm.at[fx[d] * 2 + c], target, (fx[d], h, c), landing)

    def move_back(d, c):
        landing = wback.at[whole(c, span), whole(fx[d], depth)]
        target = wback.at[whole(t, span), whole(f, depth)]
        return exchange(wback_hbm.at[fx[d] * 2 + c], target, (fx[d], h, c), landing)

    expert_moves = [move_in(d, c) for d, c in ((1, t), (2, t), (1, s), (2, s))]
    mine = [
        kept(win_hbm.at[f * 2 + t], win.at[whole(f, depth), whole(t, span)]),
        kept(wback_hbm.at[f * 2 + t], wback.at[whole(t, span), whole(f, depth)]),
    ]

    row_index = lax.broadcasted_iota(jnp.int32, (ROWS, 1), 0)

    def image(source, b):
        if b == 0:
            stage[0 : images * SEQ, :] = source[...].astype(F32)
        return jnp.where(row_index < SEQ, stage[b * SEQ : b * SEQ + ROWS, :], 0.0)

    flat_index = lax.broadcasted_iota(jnp.int32, (flat, 1), 0)
    flat_image = sum((flat_index >= b * SEQ).astype(jnp.int32) for b in range(1, images))
    living = (flat_index < own_rows) & ((h * 2 + t) * images + flat_image < counts[0])
    stage[0:own_rows, :] = cot[...].astype(F32)
    rows_grad[h * 2 + t, 0:flat, :] = jnp.where(living, stage[0:flat, :], 0.0).astype(BF16)

    cut = -(-flat // 32) * 16
    parts = [slice(0, cut), slice(cut, flat)]

    def hop(rows, line, part, to, source):
        here = rows.at[line * 2 + t, parts[part]]
        return exchange(here, here, (f, to, t), rows.at[source * 2 + t, parts[part]])

    def beside(rows, line):
        here = rows.at[line * 2 + t, 0:flat]
        return exchange(here, here, (f, h, s), rows.at[line * 2 + s, 0:flat])

    class Spread:
        def __init__(self, rows):
            self.rows = rows
            self.down = [hop(rows, h, 0, after, before), None]
            self.up = [None, hop(rows, h, 1, before, after)]
            self.near = [beside(rows, h)]

        def second(self):
            self.down[1] = hop(self.rows, h, 1, after, before)
            self.up[0] = hop(self.rows, h, 0, before, after)

        def relay(self):
            self.down[0].arrived()
            self.far = [hop(self.rows, before, 0, after, across)]
            self.up[1].arrived()
            self.far.append(hop(self.rows, after, 1, before, across))

        def share(self):
            self.down[1].arrived()
            self.near.append(beside(self.rows, before))
            self.up[0].arrived()
            self.near.append(beside(self.rows, after))

        def close(self):
            for move in self.far:
                move.arrived()
            self.near.append(beside(self.rows, across))

        def blocks(self):
            lines = [h, before, after, across]
            moves = self.near + [None] * (4 - len(self.near))
            return [(line * 2 + t, None) for line in lines] + [
                (line * 2 + s, move) for line, move in zip(lines, moves)
            ]

        def sent(self):
            for move in self.down + self.up + self.far + self.near:
                move.sent()

    grad_spread = Spread(rows_grad)

    for b in range(images):
        unit, _ = normal_parts(image(tokens, b))
        normed[b * ROWS : (b + 1) * ROWS, :] = (unit * gain[0:1] + bias[0:1]).astype(BF16)

    for step in first:
        step.arrived()

    def across_plane(span_i, source, to, landing):
        here = wbuf.at[span_i, :, t, :, whole(source, 128)]
        return exchange(here, here, (to, h, t), wbuf.at[span_i, :, t, :, whole(landing, 128)])

    both = [slice(0, 2), slice(2, 4)]
    second = [across_plane(slice(0, 4), f, fx[d], fx[d]) for d in (1, 2)]

    relative = named_in[...] - h * local_count
    wanted = (slots_in[...] >= 0) & (relative >= 0) & (relative < local_count)
    wanted = wanted & (lax.rem(relative + 2 * local_count, 2) == t)
    places = jnp.where(wanted, lax.div(relative, 2) * CAP + slots_in[...], -1)
    reach = -(-flat // 128) * 128 + 128
    tail = jnp.full((2, reach), -1, jnp.int32)
    places = jnp.concatenate([places, tail], axis=1)[:, 0 : places.shape[1] // 128 * 128 + reach]
    place_lane = lax.broadcasted_iota(jnp.int32, (2, reach), 1)
    for b in range(2 * H):
        begin = b * own_rows
        base = begin // 128 * 128
        window = pltpu.roll(places[:, base : base + reach], (base - begin) % reach, 1)
        rows = jnp.where(place_lane < own_rows, window, -1)
        prow[b, 0:2, :] = rows[:, 0 : prow.shape[2]]

    def mark_slots(b):
        for part in range(4):
            spot = lax.broadcasted_iota(jnp.int32, (CAP, flat), 0) + CAP * part
            named = (prow[b, 0:1, 0:flat] == spot) | (prow[b, 1:2, 0:flat] == spot)
            big[b, part * CAP : (part + 1) * CAP, 0:flat] = jnp.where(named, 1.0, 0.0).astype(BF16)

    grad_spread.second()
    pl.loop(0, 2 * H)(mark_slots)
    for d in (1, 2):
        second[d - 1].arrived()
        second.append(across_plane(both[d - 1], fx[d], fx[3 - d], fx[3]))
    grad_spread.relay()
    for step in second[2:]:
        step.arrived()
    third = exchange(*[wbuf.at[:, :, t]] * 2, (f, h, s), wbuf.at[:, :, s])

    for d, c in ((3, t), (3, s), (0, s)):
        expert_moves.append(move_in(d, c))
    for d, c in ((1, t), (2, t), (1, s), (2, s), (3, t), (3, s), (0, s)):
        expert_moves.append(move_back(d, c))

    grad_spread.share()
    third.arrived()

    for i in range(3):
        part = mm(normed[...], wbuf[i].reshape(width, width), NT)
        if i == 0:
            part = part * HEAD ** (-0.5)
        qkv[:, i * width : (i + 1) * width] = part.astype(BF16)
    lane = lax.broadcasted_iota(jnp.int32, (1, 128), 1)
    sides = [jnp.where(lane < HEAD, 1.0, 0.0).astype(BF16), jnp.where(lane < HEAD, 0.0, 1.0).astype(BF16)]
    key_index = lax.broadcasted_iota(jnp.int32, (1, ROWS), 1)

    def pair_of(index):
        b, pair = index // half, lax.rem(index, half)
        rows = whole(b, ROWS)
        cols = [whole(pair + i * half, 128) for i in range(3)]
        return rows, cols

    @pl.loop(0, images * half)
    def _(index):
        rows, cols = pair_of(index)
        query, key, value = (qkv[rows, col] for col in cols)
        total = jnp.zeros((ROWS, 128), F32)
        for side in range(2):
            score = mm(query * sides[side], key, NT)
            score = jnp.where(key_index < SEQ, score, -1e30)
            score = jnp.exp(score - jnp.max(score, axis=-1, keepdims=True))
            prob = score / jnp.sum(score, axis=-1, keepdims=True)
            probs[index * 2 + side] = prob
            total += mm(prob.astype(BF16), value * sides[side])
        mixed[rows, cols[0]] = total.astype(BF16)

    for b in range(images):
        rows = slice(b * ROWS, (b + 1) * ROWS)
        value = image(tokens, b) + mm(mixed[rows, :], wbuf[3].reshape(width, width))
        middle[rows, :] = value
        unit, _ = normal_parts(value)
        own_sum[0, b * SEQ : (b + 1) * SEQ, :] = (unit * gain[1:2] + bias[1:2])[0:SEQ]
    own_flat = jnp.where(flat_index < own_rows, own_sum[0, 0:flat, :], 0.0)
    rows_norm[h * 2 + t, 0:flat, :] = own_flat.astype(BF16)

    norm_spread = Spread(rows_norm)
    grad_spread.close()

    def accumulate(rows, b, begin):
        for part in range(4):
            span_rows = slice(part * CAP, (part + 1) * CAP)
            value = mm(big[b, span_rows, 0:flat], rows[b, 0:flat])
            wide[span_rows, :] = value if begin else wide[span_rows, :] + value

    def accumulate_all(spread, order):
        blocks = spread.blocks()
        for place in order:
            b, move = blocks[place]
            if move is not None:
                move.arrived()
            accumulate(spread.rows, b, place == 0)

    def pack(send):
        for part in range(4):
            send[part] = wide[part * CAP : (part + 1) * CAP, :].astype(BF16)

    def to_group(d, send, landing):
        return exchange(send.at[fx[d]], landing.at[f], (fx[d], h, t), landing.at[fx[d]])

    def dispatch(send, landing, last=4):
        landing[f] = send[f]
        return [None] + [to_group(d, send, landing) for d in range(1, last)]

    accumulate_all(grad_spread, (0, 1, 2, 3))
    norm_spread.second()
    accumulate_all(grad_spread, (4, 5, 6, 7))
    pack(gsend)
    norm_spread.relay()
    grad_moved = dispatch(gsend, grows)
    norm_spread.share()
    accumulate_all(norm_spread, (0, 1, 2, 4, 5, 6))
    norm_spread.close()
    accumulate_all(norm_spread, (3, 7))
    pack(xsend)
    norm_moved = dispatch(xsend, xrows, 3)

    expert = h * local_count + f * 2 + t
    router_lane = lax.broadcasted_iota(jnp.int32, (1, wr.shape[0]), 1)
    chosen = (router_lane == expert).astype(F32)
    chunk = 512
    chunks = win.shape[1] // chunk
    for move in mine + expert_moves:
        move.arrived()
    back_moves = []
    for d in range(4):
        group = fx[d]
        here = whole(group, CAP)
        if d:
            norm_moved[d].arrived()
        rows = xrows[group]
        piece = 256
        ahead = mm(rows, win[:, 0:piece])
        result, held = None, None
        for c in range(win.shape[1] // piece):
            here_in = slice(c * piece % chunk, c * piece % chunk + piece)
            hidden = ahead
            if c + 1 < win.shape[1] // piece:
                ahead = mm(rows, win[:, (c + 1) * piece : (c + 2) * piece])
            value, slope = gelu_parts(hidden)
            value = value.astype(BF16)
            big[c * piece // chunk, here, here_in] = value
            wide[c * piece // chunk * CAP : (c * piece // chunk + 1) * CAP, here_in] = slope
            if c:
                term = mm(held, wback[(c - 1) * piece : c * piece, :])
                result = term if c == 1 else result + term
            held = value
        result = result + mm(held, wback[win.shape[1] - piece :, :])
        logits = mm(rows, wr[...], NT)
        odds = jnp.exp(logits - jnp.max(logits, axis=-1, keepdims=True))
        odds = odds / jnp.sum(odds, axis=-1, keepdims=True)
        gate = jnp.sum(odds * chosen, axis=-1, keepdims=True)
        if d:
            grad_moved[d].finish()
            norm_moved[d].sent()
        gsend[group] = (gate * result).astype(BF16)
        row_grad = grows[group].astype(F32)
        gate_grad = jnp.sum(row_grad * result, axis=-1, keepdims=True)
        result_grad = (gate * row_grad).astype(BF16)
        grows[group] = result_grad
        logit = (gate_grad * gate * (chosen - odds)).astype(BF16)
        logit_grad[here, :] = logit
        parts_grad = []
        for c in range(chunks):
            grad = mm(result_grad, wback[c * chunk : (c + 1) * chunk, :], NT)
            grad = (grad * wide[c * CAP : (c + 1) * CAP, :]).astype(BF16)
            big[4 + c, here, :] = grad
            parts_grad.append(grad)
        total = mm(logit, wr[...]) + mm(jnp.concatenate(parts_grad, axis=1), win[...], NT)
        if d:
            xsend[group] = total.astype(BF16)
            back_moves.append(to_group(d, xsend, xback))
        else:
            xback[f] = total.astype(BF16)
            norm_moved.append(to_group(3, xsend, xrows))

    grad_spread.sent()
    norm_spread.sent()
    flat_rows = xrows[...].reshape(4 * CAP, width)
    route = mm(logit_grad[...], flat_rows, TN)
    share_rows = wr.shape[0] // 8
    for j in range(8):
        for part in range(2):
            route_out[j, part * share_rows : (part + 1) * share_rows, :] = route[
                j * share_rows : (j + 1) * share_rows, part * (width // 2) : (part + 1) * (width // 2)
            ]
    route_in[f * 2 + t] = route_out[f * 2 + t]
    plane_peers = [(d, c) for d in range(4) for c in ((t, s) if d else (s,))]
    route_moves = [
        exchange(route_out.at[fx[d] * 2 + c], route_in.at[f * 2 + t], (fx[d], h, c), route_in.at[fx[d] * 2 + c])
        for d, c in plane_peers
    ]
    flat_grad = grows[...].reshape(4 * CAP, width)
    for c in range(chunks):
        rows_grad[c] = mm(flat_rows, big[4 + c], TN).astype(BF16)
        rows_norm[c] = mm(big[c], flat_grad, TN).astype(BF16)
    for move in route_moves:
        move.arrived()
    route = route_in[0]
    for j in range(1, 8):
        route = route + route_in[j]
    route_z[h] = route
    route_line = [
        exchange(route_z.at[h], route_z.at[h], (f, hz[d], t), route_z.at[hfrom[d]]) for d in range(1, H)
    ]

    for move in back_moves:
        move.arrived()
    out_moves = dispatch(gsend, gback)[1:]

    halves = chunks // 2

    def to_owner(d, c, part, back):
        device, one = (fx[d], h, c), d == 0 and c is t
        span_part = slice(part * chunk, (part + 1) * chunk)
        if back:
            source = rows_norm.at[c * halves + part, :, whole(fx[d], depth)]
            target = gback_out.at[f * 2 + t, span_part]
            landing = gback_out.at[fx[d] * 2 + c, span_part]
        else:
            source = rows_grad.at[c * halves + part, whole(fx[d], depth), :]
            target = gin_out.at[f * 2 + t, :, span_part]
            landing = gin_out.at[fx[d] * 2 + c, :, span_part]
        if one:
            kept(source, target)
        else:
            exchange(source, target, device, landing)

    def to_owners(part, back):
        for d in (1, 2, 3, 0):
            for c in (t, s):
                to_owner(d, c, part, back)

    def share(b, back):
        spots = jnp.transpose(prow[b])[0:flat]
        slot = lax.broadcasted_iota(jnp.int32, (flat, 4 * CAP), 1)
        named = (spots[:, 0:1] == slot) | (spots[:, 1:2] == slot)
        return mm(jnp.where(named, 1.0, 0.0).astype(BF16), back[...].reshape(4 * CAP, width))

    class Gather:
        def __init__(self, which, back, near_out, far_out):
            self.which, self.back = which, back
            self.near_out, self.far_out = near_out, far_out
            self.lines = [across, after, before, h]
            self.near = []

        def give(self, place):
            line = self.lines[place]
            self.near_out(place)[...] = share(line * 2 + s, self.back).astype(BF16)
            landing = sib_in.at[self.which, place]
            self.near.append(exchange(self.near_out(place), landing, (f, h, s), landing))

        def take(self, place):
            value = share(self.lines[place] * 2 + t, self.back)
            self.near[place].arrived()
            value = value + sib_in[self.which, place].astype(F32)
            if place == 3:
                own_sum[self.which, 0:flat, :] = value
            else:
                self.far_out(place)[...] = value.astype(BF16)

        def hop(self, place, part, to, slot):
            landing = z_in.at[self.which, slot, parts[part]]
            return exchange(self.far_out(place).at[parts[part]], landing, (f, to, t), landing)

        def start(self):
            self.first = [self.hop(0, 0, after, 0), self.hop(0, 1, before, 0)]

        def direct(self, place):
            part, to = ((1, after), (0, before))[place - 1]
            self.last = getattr(self, "last", []) + [self.hop(place, part, to, place)]

        def relay(self):
            for place, part, to in ((1, 0, after), (2, 1, before)):
                self.first[part].arrived()
                rows = self.far_out(place).at[parts[part]]
                passed = z_in[self.which, 0, parts[part], :].astype(F32)
                rows[...] = (rows[...].astype(F32) + passed).astype(BF16)
                self.last.append(self.hop(place, part, to, place))

        def total(self):
            for move in self.last:
                move.arrived()
            total = own_sum[self.which, 0:flat, :]
            for slot in (1, 2):
                total = total + z_in[self.which, slot].astype(F32)
            own_sum[self.which, 0:flat, :] = total

    norm_sums = Gather(0, xback, lambda place: sib_out.at[place], lambda place: z_out.at[place])
    norm_sums.give(0)
    norm_sums.take(0)
    norm_sums.start()
    norm_sums.give(1)
    norm_sums.give(2)
    norm_sums.take(1)
    norm_sums.direct(1)
    norm_sums.take(2)
    norm_sums.direct(2)
    norm_sums.give(3)
    norm_sums.take(3)
    for move in out_moves:
        move.arrived()
    to_owners(0, True)
    to_owners(1, True)
    to_owners(0, False)
    out_sums = Gather(
        1, gback, lambda place: big.at[place, 0:flat], lambda place: big.at[4 + place, 0:flat]
    )
    out_sums.give(0)
    out_sums.take(0)
    for place in range(1, 4):
        out_sums.give(place)
    norm_sums.relay()
    for place in range(1, 4):
        out_sums.take(place)


    norm_sums.total()
    out_sums.start()
    small_c[t] = jnp.zeros(small_c.shape[1:], F32)
    for b in range(images):
        rows = slice(b * ROWS, (b + 1) * ROWS)
        grad = jnp.where(row_index < SEQ, own_sum[0, b * SEQ : b * SEQ + ROWS, :], 0.0)
        unit, scale = normal_parts(middle[rows, :])
        small_c[t, 1:2] += jnp.sum(grad * unit, axis=0, keepdims=True)
        small_c[t, 3:4] += jnp.sum(grad, axis=0, keepdims=True)
        live = ((h * 2 + t) * images + b < counts[0]).astype(F32)
        grad = normal_pull(grad, unit, scale, gain[1:2]) + image(cot, b) * live
        grad_mid[rows, :] = grad

    out_sums.direct(1)
    out_sums.direct(2)

    for move in back_moves:
        move.sent()
    low = grad_mid[...].astype(BF16)
    count = H * 2 * 64
    wide[3 * count : 4 * count, :] = mm(mixed[...], low, TN)

    def wide_rows(i, other, core):
        return whole((i * H + other) * 2 + core, 64)

    def core_sums(span_i, others):
        for i in span_i:
            for other in others:
                xsend[i, whole(other, 64), :] = wide[wide_rows(i, other, s), :].astype(BF16)
        here = (slice(span_i.start, span_i.stop), whole(others[0], 64))
        if len(others) > 1:
            here = (here[0], slice(0, H * 64))
        landing = att_in.at[here]
        return here, exchange(xsend.at[here], landing, (f, h, s), landing)

    def plane_sums(span_i, others, near):
        here, move = near
        move.finish()
        for i in span_i:
            for other in others:
                place, low_rows = wide_rows(i, other, t), whole(other, 64)
                value = wide[place, :] + att_in[i, low_rows, :].astype(F32)
                wide[place, :] = value
                xsend[i, low_rows, :] = value.astype(BF16)
        return [
            exchange(
                xsend.at[(*here, whole(fx[d], 128))], plane_in.at[(f, *here)],
                (fx[d], h, t), plane_in.at[(fx[d], *here)],
            )
            for d in range(1, 4)
        ]

    def own_columns(i, other):
        value = wide[wide_rows(i, other, t), whole(f, 128)]
        for d in range(1, 4):
            value = value + plane_in[fx[d], i, whole(other, 64), :].astype(F32)
        return value

    last_near = core_sums(range(3, 4), list(range(H)))
    mixed[...] = mm(low, wbuf[3].reshape(width, width), NT).astype(BF16)

    def attention_back(index):
        rows, cols = pair_of(index)
        query, key, value = (qkv[rows, col] for col in cols)
        pulled = mixed[rows, cols[0]]
        grads = [jnp.zeros((ROWS, 128), F32) for _ in range(3)]
        for side in range(2):
            prob = probs[index * 2 + side]
            one = pulled * sides[side]
            prob_grad = mm(one, value, NT)
            grads[2] += mm(prob.astype(BF16), one, TN)
            inner = jnp.sum(prob * prob_grad, axis=-1, keepdims=True)
            score_grad = (prob * (prob_grad - inner)).astype(BF16)
            grads[0] += mm(score_grad, key * sides[side])
            grads[1] += mm(score_grad, query * sides[side], TN)
        grads[0] = grads[0] * HEAD ** (-0.5)
        for grad, col in zip(grads, cols):
            qkv[rows, col] = grad.astype(BF16)

    order = [hz[1], hz[2], hz[3], hz[0]]
    nears, planes = [], []
    for turn, other in enumerate(order):
        pl.loop(0, images)(lambda b, other=other: attention_back(b * half + other))
        for i in range(3):
            rows = pl.ds(pl.multiple_of((i * H + other) * 128, 128), 128)
            wide[rows, :] = mm(qkv[:, whole(i * half + other, 128)], normed[...], TN)
        nears.append(core_sums(range(3), [other]))
        if turn == 0:
            last_plane = plane_sums(range(3, 4), list(range(H)), last_near)
        else:
            planes.append(plane_sums(range(3), [order[turn - 1]], nears[turn - 1]))
    out_sums.relay()

    for b in range(images):
        rows = slice(b * ROWS, (b + 1) * ROWS)
        grad = jnp.zeros((ROWS, width), F32)
        for i in range(3):
            grad += mm(qkv[rows, i * width : (i + 1) * width], wbuf[i].reshape(width, width))
        unit, scale = normal_parts(image(tokens, b))
        small_c[t, 0:1] += jnp.sum(grad * unit, axis=0, keepdims=True)
        small_c[t, 2:3] += jnp.sum(grad, axis=0, keepdims=True)
        grad = normal_pull(grad, unit, scale, gain[0:1]) + grad_mid[rows, :]
        tgrad[b * SEQ : (b + 1) * SEQ, :] = grad[0:SEQ]
    small_near = exchange(small_c.at[t], small_c.at[t], (f, h, s), small_c.at[s])

    planes.append(plane_sums(range(3), [order[3]], nears[3]))
    small_near.arrived()
    small_p[f] = small_c[0] + small_c[1]
    small_plane = [
        exchange(small_p.at[f], small_p.at[f], (fx[d], h, t), small_p.at[fx[d]]) for d in range(1, 4)
    ]
    for move in route_line:
        move.arrived()
    route = route_z[0]
    for d in range(1, H):
        route = route + route_z[d]
    route_all[f * 2 + t] = route
    route_last = [
        exchange(route_all.at[f * 2 + t], route_all.at[f * 2 + t], (fx[d], h, c), route_all.at[fx[d] * 2 + c])
        for d, c in plane_peers
    ]

    for move in last_plane:
        move.arrived()
    line = []
    for turn in range(3):
        for move in planes[turn]:
            move.arrived()
        other = order[turn]
        for i in range(4):
            line_out[other, i] = own_columns(i, other).astype(BF16)
        d = turn + 1
        line.append(
            exchange(line_out.at[other], line_in.at[h], (f, other, t), line_in.at[hfrom[d]])
        )
    for move in planes[3]:
        move.arrived()
    to_owners(1, False)
    for move in small_plane:
        move.arrived()
    small_z[h] = (small_p[0] + small_p[1]) + (small_p[2] + small_p[3])
    small_line = [
        exchange(small_z.at[h], small_z.at[h], (f, hz[d], t), small_z.at[hfrom[d]]) for d in range(1, H)
    ]
    for move in route_last:
        move.arrived()
    for j in range(8):
        for part in range(2):
            wrg[j * share_rows : (j + 1) * share_rows, part * (width // 2) : (part + 1) * (width // 2)] = (
                route_all[j, part * share_rows : (part + 1) * share_rows, :]
            )

    out_sums.total()
    for b in range(images):
        stage[b * SEQ : (b + 1) * SEQ, :] = middle[b * ROWS : b * ROWS + SEQ, :]
    out[...] = (stage[0:own_rows, :] + own_sum[1, 0:own_rows, :]).astype(BF16)

    for move in line:
        move.arrived()
    for i in range(4):
        value = own_columns(i, h)
        for d in range(1, H):
            value = value + line_in[hfrom[d], i].astype(F32)
        if i < 3:
            wqg[i] = value
        else:
            wog[...] = value
    for move in small_line:
        move.arrived()
    total = small_z[0]
    for d in range(1, H):
        total = total + small_z[d]
    lng[...] = total[0:2]
    lnb[...] = total[2:4]

    for move in pending:
        move.finish()


def finish_kernel(*refs):
    sources, targets = refs[:9], refs[9:18]
    held, wider = refs[18:27], refs[27:29]
    in_sems, out_sems = refs[29], refs[30]
    experts = sources[7].shape[0]
    inward, outward = [], []

    def begin(source, target, semaphores, index):
        copy = pltpu.make_async_copy(source, target, semaphores.at[index])
        copy.start()
        return copy

    for e in range(experts):
        for k in (7, 8):
            index = 7 + 2 * e + k - 7
            inward.append((e, k, index, begin(sources[k].at[e], held[k].at[e], in_sems, index)))
    small = [begin(sources[k], held[k], in_sems, k) for k in range(7)]
    for e, k, index, copy in inward:
        copy.wait()
        wider[k - 7][e] = held[k][e].astype(F32)
        outward.append(begin(wider[k - 7].at[e], targets[k].at[e], out_sems, index))
    for k, copy in enumerate(small):
        copy.wait()
        outward.append(begin(held[k], targets[k], out_sems, k))
    for copy in outward:
        copy.wait()


def fast_device(
    tokens,
    cotangent,
    image_counts,
    w_qkv,
    w_out,
    ln_gain,
    ln_bias,
    w_router,
    w_in,
    w_back,
    expert_ids,
    slots,
):
    H = lax.axis_size("heads")
    own_rows, width = tokens.shape
    images = own_rows // SEQ
    own = images * ROWS
    flat = -(-own_rows // 16) * 16
    local_count, depth, span = w_in.shape[1:]
    experts = w_router.shape[2]
    hidden = span * 2
    vmem = pl.BlockSpec(memory_space=pltpu.VMEM)
    smem = pl.BlockSpec(memory_space=pltpu.SMEM)
    anywhere = pl.BlockSpec(memory_space=pl.ANY)
    shape = jax.ShapeDtypeStruct

    def low(*dims):
        return pltpu.VMEM(dims, BF16)

    def full(*dims):
        return pltpu.VMEM(dims, F32)

    outs = pl.pallas_call(
        lambda *refs: block_kernel(H, images, local_count, refs),
        out_shape=(
            shape((own_rows, width), BF16),
            shape((own_rows, width), F32),
            shape((3, 64, depth), F32),
            shape((64, depth), F32),
            shape((2, width), F32),
            shape((2, width), F32),
            shape((experts, width), F32),
            shape((local_count, depth, span), BF16),
            shape((local_count, span, depth), BF16),
        ),
        in_specs=[vmem, vmem, smem, vmem, vmem, vmem, vmem, vmem, anywhere, anywhere, vmem, vmem],
        out_specs=[vmem] * 7 + [anywhere] * 2,
        scratch_shapes=[
            full(images * SEQ + 16, width),
            pltpu.VMEM((2 * H, 8, -(-flat // 128) * 128), jnp.int32),
            low(4, H, 2, 64, width),
            low(width, hidden),
            low(hidden, width),
            low(2 * H, 512, width),
            low(2 * H, 512, width),
            low(8, 4 * CAP, 512),
            full(8 * CAP, width),
            low(4, CAP, width),
            low(4, CAP, width),
            low(4, CAP, width),
            low(4, CAP, width),
            low(4, CAP, width),
            low(4, CAP, width),
            low(own, width),
            low(own, 3 * width),
            full(images * width // HEAD, ROWS, ROWS),
            low(own, width),
            full(own, width),
            full(own, width),
            low(4 * CAP, experts),
            low(H, flat, width),
            low(2, H, flat, width),
            low(3, flat, width),
            low(2, 3, flat, width),
            full(2, own, width),
            low(4, H * 64, width),
            low(4, 4, H * 64, 128),
            low(H, 4, 64, 128),
            low(H, 4, 64, 128),
            full(2, 8, width),
            full(4, 8, width),
            full(H, 8, width),
            full(8, experts // 4, width // 2),
            full(8, experts // 4, width // 2),
            full(H, experts // 4, width // 2),
            full(8, experts // 4, width // 2),
            pltpu.SemaphoreType.DMA((192,)),
            pltpu.SemaphoreType.DMA((192,)),
            pltpu.SemaphoreType.DMA((16,)),
        ],
        compiler_params=pltpu.CompilerParams(
            collective_id=0, has_side_effects=True, vmem_limit_bytes=62 * 2**20
        ),
        name="block",
    )(
        tokens, cotangent, image_counts, jnp.transpose(w_qkv[0], (0, 2, 1)), w_out[0], ln_gain[0], ln_bias[0],
        jnp.transpose(w_router[0]),
        w_in[0], w_back[0], jnp.transpose(expert_ids[0]), jnp.transpose(slots[0]),
    )
    sems = pltpu.SemaphoreType.DMA((7 + 2 * local_count,))
    outs = pl.pallas_call(
        finish_kernel,
        out_shape=[shape(part.shape, F32 if i >= 7 else part.dtype) for i, part in enumerate(outs)],
        in_specs=[anywhere] * 9,
        out_specs=[anywhere] * 9,
        scratch_shapes=[pltpu.VMEM(part.shape, part.dtype) for part in outs]
        + [full(*part.shape) for part in outs[7:]]
        + [sems, sems],
        compiler_params=pltpu.CompilerParams(vmem_limit_bytes=62 * 2**20),
        name="finish",
    )(*outs)
    block_out, token_grad, qkv_grad, out_grad, gains, shifts, router, in_grad, back_grad = outs
    return (
        block_out,
        token_grad,
        jnp.transpose(qkv_grad, (0, 2, 1))[None],
        out_grad[None],
        gains[None],
        shifts[None],
        jnp.transpose(router)[None],
        in_grad[None],
        back_grad[None],
    )


def solution(mesh):
    def program(*arrays):
        sizes = dict(mesh.shape)
        devices = sizes["fsdp"] * sizes["heads"] * sizes["tensor"]
        own_rows = arrays[0].shape[0] // devices
        one_expert = sizes["fsdp"] == 4 and sizes["tensor"] == 2 and arrays[8].shape[1] == devices
        one_expert = one_expert and sizes["heads"] == 4 and own_rows % (2 * SEQ) == 0
        return placed(mesh, fast_device if one_expert else on_device)(*arrays)

    return program


def placed(mesh, on_device):
    return jax.shard_map(
        on_device,
        mesh=mesh,
        in_specs=(
            P(("fsdp", "heads", "tensor"), None),
            P(("fsdp", "heads", "tensor"), None),
            P("fsdp"),
            P(None, None, "fsdp", ("heads", "tensor")),
            P(None, ("heads", "tensor"), "fsdp"),
            P(),
            P(),
            P(),
            P(None, "heads", "fsdp", "tensor"),
            P(None, "heads", "tensor", "fsdp"),
            P(None, "fsdp", None),
            P(None, "fsdp", None),
        ),
        out_specs=(
            P(("fsdp", "heads", "tensor"), None),
            P(("fsdp", "heads", "tensor"), None),
            P(None, None, "fsdp", ("heads", "tensor")),
            P(None, ("heads", "tensor"), "fsdp"),
            P(),
            P(),
            P(),
            P(None, "heads", "fsdp", "tensor"),
            P(None, "heads", "tensor", "fsdp"),
        ),
        check_vma=False,
    )
```

```python
import jax
import jax.numpy as jnp
from jax import lax
from jax.experimental import pallas as pl
from jax.experimental.pallas import tpu as pltpu
from jax.sharding import PartitionSpec as P

HEAD = 64
SEQ = 197
LAYERS = 1
CAP = 256


def layer_norm(value, ln_gains, ln_shift):
    centred = value - jnp.mean(value, axis=-1, keepdims=True)
    spread = jnp.mean(centred * centred, axis=-1, keepdims=True)
    return centred * lax.rsqrt(spread + 1e-06) * ln_gains + ln_shift


def gelu_exact(value):
    return jax.nn.gelu(value, approximate=False)


def with_zero_row(matrix):
    return jnp.concatenate([matrix, jnp.zeros((1,) + matrix.shape[1:], matrix.dtype)], axis=0)


def slot_tables(named_expert, slot_rows, first_expert, local_experts):
    group_rows = named_expert.shape[0]
    is_local = (
        (slot_rows >= 0)
        & (named_expert >= first_expert)
        & (named_expert < first_expert + local_experts)
    )
    places = jnp.where(
        is_local, (named_expert - first_expert) * CAP + slot_rows, local_experts * CAP
    )
    picked = jnp.full((local_experts * CAP + 1,), 2 * group_rows, jnp.int32)
    picked = picked.at[places.reshape(-1)].set(jnp.arange(2 * group_rows, dtype=jnp.int32))
    return (places, picked[: local_experts * CAP])


def joined_qkv(qkv_weight):
    head_cols = qkv_weight.shape[2]
    return jnp.transpose(qkv_weight, (1, 0, 2)).reshape(qkv_weight.shape[1], 3 * head_cols)


def forward_block(
    residual, weights, ln_gains, ln_shift, router_weight, named_expert, slot_rows, first_expert
):
    qkv_weight, out_weight, in_weight, back_weight = weights
    own_rows, widths = residual.shape
    group_rows = named_expert.shape[0]
    head_cols = qkv_weight.shape[2]
    local_experts = in_weight.shape[0]
    head_shape = (group_rows // SEQ, SEQ, head_cols // HEAD, HEAD)
    q_scale = HEAD ** (-0.5)
    flat_qkv = joined_qkv(qkv_weight)
    normed_rows = layer_norm(residual, ln_gains[0], ln_shift[0]).astype(jnp.bfloat16)
    normed = lax.all_gather(normed_rows, ("heads", "tensor"), axis=0, tiled=True)
    projected = jnp.dot(normed, flat_qkv, preferred_element_type=jnp.float32)
    queries = (projected[:, :head_cols] * q_scale).astype(jnp.bfloat16).reshape(head_shape)
    key_rows = projected[:, head_cols : 2 * head_cols].astype(jnp.bfloat16).reshape(head_shape)
    value_rows = projected[:, 2 * head_cols :].astype(jnp.bfloat16).reshape(head_shape)
    scores = jnp.einsum("bqhd,bkhd->bhqk", queries, key_rows, preferred_element_type=jnp.float32)
    log_total = jax.nn.logsumexp(scores, axis=-1)
    attn_probs = jax.nn.softmax(scores, axis=-1).astype(jnp.bfloat16)
    mixed_rows = jnp.einsum(
        "bhqk,bkhd->bqhd", attn_probs, value_rows, preferred_element_type=jnp.float32
    )
    mixed_rows = mixed_rows.reshape(group_rows, head_cols).astype(jnp.bfloat16)
    middle = residual + lax.psum_scatter(
        jnp.dot(mixed_rows, out_weight, preferred_element_type=jnp.float32),
        ("heads", "tensor"),
        scatter_dimension=0,
        tiled=True,
    )
    head_full = ()
    normed_two_rows = layer_norm(middle, ln_gains[1], ln_shift[1]).astype(jnp.bfloat16)
    normed_two = lax.all_gather(normed_two_rows, ("heads", "tensor"), axis=0, tiled=True)
    router = jax.nn.softmax(
        jnp.dot(normed_two, router_weight, preferred_element_type=jnp.float32), axis=-1
    )
    gate_values = jnp.take_along_axis(router, named_expert, axis=1) * (slot_rows >= 0)
    places, picked = slot_tables(named_expert, slot_rows, first_expert, local_experts)
    routed = with_zero_row(normed_two)[picked // 2].reshape(local_experts, CAP, widths)
    hidden = jnp.einsum("ecd,edf->ecf", routed, in_weight, preferred_element_type=jnp.float32)
    active = gelu_exact(hidden).astype(jnp.bfloat16)
    result = jnp.einsum("ecf,efd->ecd", active, back_weight, preferred_element_type=jnp.float32)
    flat_result = with_zero_row(result.reshape(local_experts * CAP, widths))
    block_out = middle + lax.psum_scatter(
        (
            flat_result[places[:, 0]] * gate_values[:, 0:1]
            + flat_result[places[:, 1]] * gate_values[:, 1:2]
        ).astype(jnp.bfloat16),
        ("heads", "tensor"),
        scatter_dimension=0,
        tiled=True,
    ).astype(jnp.float32)
    stored = (
        residual,
        middle,
        normed,
        queries,
        key_rows,
        value_rows,
        log_total,
        mixed_rows,
        normed_two_rows,
        router,
        gate_values,
        places,
        picked,
        routed,
        hidden,
        active,
        flat_result,
    )
    return (block_out, stored, head_full)


def backward_block(
    grad_rows, stored, weights, ln_gains, ln_shift, router_weight, named_expert, row_start
):
    qkv_weight, out_weight, in_weight, back_weight = weights
    (
        residual,
        middle,
        normed,
        queries,
        key_rows,
        value_rows,
        log_total,
        mixed_rows,
        normed_two_rows,
        router,
        gate_values,
        places,
        picked,
        routed,
        hidden,
        active,
        flat_result,
    ) = stored
    own_rows, widths = residual.shape
    group_rows = named_expert.shape[0]
    head_cols = qkv_weight.shape[2]
    local_experts = in_weight.shape[0]
    expert_count = router.shape[1]
    q_scale = HEAD ** (-0.5)
    flat_qkv = joined_qkv(qkv_weight)
    grad_moe = lax.all_gather(
        grad_rows.astype(jnp.bfloat16), ("heads", "tensor"), axis=0, tiled=True
    )
    back_rows = with_zero_row(grad_moe)[picked // 2].astype(jnp.float32)
    gate_slots = with_zero_row(gate_values.reshape(-1))[picked]
    gate_grad_slots = jnp.sum(back_rows * flat_result[:-1], axis=1)
    gate_grads = with_zero_row(gate_grad_slots)[places]
    expert_range = jnp.arange(expert_count, dtype=jnp.int32)
    router_part = jnp.sum(
        gate_grads[:, :, None]
        * (named_expert[:, :, None] == expert_range[None, None, :]).astype(jnp.float32),
        axis=1,
    )
    grad_result = (
        (gate_slots[:, None] * back_rows).astype(jnp.bfloat16).reshape(local_experts, CAP, widths)
    )
    grad_active = jnp.einsum(
        "ecd,efd->ecf", grad_result, back_weight, preferred_element_type=jnp.float32
    )
    gelu_value, gelu_pull = jax.vjp(gelu_exact, hidden)
    grad_hidden = gelu_pull(grad_active)[0].astype(jnp.bfloat16)
    back_grad = jnp.einsum("ecf,ecd->efd", active, grad_result, preferred_element_type=jnp.float32)
    in_grad = jnp.einsum("ecd,ecf->edf", routed, grad_hidden, preferred_element_type=jnp.float32)
    grad_routed = jnp.einsum(
        "ecf,edf->ecd", grad_hidden, in_weight, preferred_element_type=jnp.float32
    )
    grad_routed = with_zero_row(grad_routed.reshape(local_experts * CAP, widths))
    token_part = grad_routed[places[:, 0]] + grad_routed[places[:, 1]]
    grad_normed_two, router_rows = (
        lax.psum_scatter(token_part, ("heads", "tensor"), scatter_dimension=0, tiled=True),
        lax.psum_scatter(router_part, ("heads", "tensor"), scatter_dimension=0, tiled=True),
    )
    router_own = lax.dynamic_slice_in_dim(router, row_start, own_rows, 0)
    grad_logits = (
        router_own * (router_rows - jnp.sum(router_own * router_rows, axis=-1, keepdims=True))
    ).astype(jnp.bfloat16)
    router_grad = jnp.einsum(
        "td,te->de", normed_two_rows, grad_logits, preferred_element_type=jnp.float32
    )
    grad_normed_two = grad_normed_two + jnp.einsum(
        "te,de->td", grad_logits, router_weight, preferred_element_type=jnp.float32
    )
    norm_value, norm_pull = jax.vjp(layer_norm, middle, ln_gains[1], ln_shift[1])
    grad_middle, gain_two, shift_two = norm_pull(grad_normed_two)
    grad_middle = grad_middle + grad_rows
    grad_attn = lax.all_gather(
        grad_middle.astype(jnp.bfloat16), ("heads", "tensor"), axis=0, tiled=True
    )
    out_grad = jnp.einsum("tc,td->cd", mixed_rows, grad_attn, preferred_element_type=jnp.float32)
    grad_mixed = jnp.einsum("td,cd->tc", grad_attn, out_weight, preferred_element_type=jnp.float32)
    grad_mixed = grad_mixed.astype(jnp.bfloat16).reshape(queries.shape)
    scores = jnp.einsum("bqhd,bkhd->bhqk", queries, key_rows, preferred_element_type=jnp.float32)
    attn_probs = jnp.exp(scores - log_total[..., None])
    grad_values = jnp.einsum(
        "bhqk,bqhd->bkhd",
        attn_probs.astype(jnp.bfloat16),
        grad_mixed,
        preferred_element_type=jnp.float32,
    )
    grad_probs = jnp.einsum(
        "bqhd,bkhd->bhqk", grad_mixed, value_rows, preferred_element_type=jnp.float32
    )
    grad_scores = (
        attn_probs * (grad_probs - jnp.sum(attn_probs * grad_probs, axis=-1, keepdims=True))
    ).astype(jnp.bfloat16)
    grad_queries = jnp.einsum(
        "bhqk,bkhd->bqhd", grad_scores, key_rows, preferred_element_type=jnp.float32
    )
    grad_keys = jnp.einsum(
        "bhqk,bqhd->bkhd", grad_scores, queries, preferred_element_type=jnp.float32
    )
    grad_projected = jnp.concatenate(
        [
            grad_queries.reshape(group_rows, head_cols),
            grad_keys.reshape(group_rows, head_cols),
            grad_values.reshape(group_rows, head_cols),
        ],
        axis=1,
    ).astype(jnp.bfloat16)
    qkv_flat_grad = jnp.einsum(
        "td,tc->dc", normed, grad_projected, preferred_element_type=jnp.float32
    )
    column_scale = jnp.concatenate(
        [jnp.full((head_cols,), q_scale, jnp.float32), jnp.ones((2 * head_cols,), jnp.float32)]
    )
    qkv_grad = jnp.transpose(
        (qkv_flat_grad * column_scale).reshape(widths, 3, head_cols), (1, 0, 2)
    )
    query_term = (
        jnp.einsum(
            "tc,dc->td",
            grad_projected[:, :head_cols],
            flat_qkv[:, :head_cols],
            preferred_element_type=jnp.float32,
        )
        * q_scale
    )
    grad_normed = lax.psum_scatter(
        query_term
        + jnp.einsum(
            "tc,dc->td",
            grad_projected[:, head_cols:],
            flat_qkv[:, head_cols:],
            preferred_element_type=jnp.float32,
        ),
        ("heads", "tensor"),
        scatter_dimension=0,
        tiled=True,
    )
    first_value, first_pull = jax.vjp(layer_norm, residual, ln_gains[0], ln_shift[0])
    grad_input, gain_one, shift_one = first_pull(grad_normed)
    grad_input = grad_input + grad_middle
    matrix_grads = (qkv_grad, out_grad, in_grad, back_grad)
    small_grads = (jnp.stack([gain_one, gain_two]), jnp.stack([shift_one, shift_two]), router_grad)
    return (grad_input, matrix_grads, small_grads)


def on_device(
    tokens,
    cotangent,
    image_counts,
    w_qkv,
    w_out,
    ln_gain,
    ln_bias,
    w_router,
    w_in,
    w_back,
    expert_ids,
    slots,
):
    own_rows = tokens.shape[0]
    row_start = lax.axis_index(("heads", "tensor")) * own_rows
    first_expert = lax.axis_index("heads") * w_in.shape[1]
    residual = tokens.astype(jnp.float32)
    head_list = []
    block_index = 0
    weights = (
        lax.all_gather(w_qkv[block_index], "fsdp", axis=1, tiled=True),
        lax.all_gather(w_out[block_index], "fsdp", axis=1, tiled=True),
        lax.all_gather(w_in[block_index], "fsdp", axis=1, tiled=True),
        lax.all_gather(w_back[block_index], "fsdp", axis=2, tiled=True),
    )
    residual, stored, head_full = forward_block(
        residual,
        weights,
        ln_gain[block_index],
        ln_bias[block_index],
        w_router[block_index],
        expert_ids[block_index],
        slots[block_index],
        first_expert,
    )
    stored_list = [stored]
    head_list.append(head_full)
    image_index = (row_start + jnp.arange(own_rows, dtype=jnp.int32)) // SEQ
    live_rows = (image_index < image_counts[0]).astype(jnp.float32)
    grad_rows = cotangent.astype(jnp.float32) * live_rows[:, None]
    matrix_list = [None] * LAYERS
    small_list = [None] * LAYERS
    for block_index in reversed(range(LAYERS)):
        weights = (
            lax.all_gather(w_qkv[block_index], "fsdp", axis=1, tiled=True),
            lax.all_gather(w_out[block_index], "fsdp", axis=1, tiled=True),
            lax.all_gather(w_in[block_index], "fsdp", axis=1, tiled=True),
            lax.all_gather(w_back[block_index], "fsdp", axis=2, tiled=True),
        )
        grad_rows, matrix_grads, small_grads = backward_block(
            grad_rows,
            stored_list[block_index],
            weights,
            ln_gain[block_index],
            ln_bias[block_index],
            w_router[block_index],
            expert_ids[block_index],
            row_start,
        )
        matrix_list[block_index] = (
            lax.psum_scatter(matrix_grads[0], "fsdp", scatter_dimension=1, tiled=True),
            lax.psum_scatter(matrix_grads[1], "fsdp", scatter_dimension=1, tiled=True),
            lax.psum_scatter(matrix_grads[2], "fsdp", scatter_dimension=1, tiled=True),
            lax.psum_scatter(matrix_grads[3], "fsdp", scatter_dimension=2, tiled=True),
        )
        small_list[block_index] = small_grads
    gain_grads, shift_grads, router_grads = lax.psum(
        (
            jnp.stack([entry[0] for entry in small_list]),
            jnp.stack([entry[1] for entry in small_list]),
            jnp.stack([entry[2] for entry in small_list]),
        ),
        ("fsdp", "heads", "tensor"),
    )
    qkv_grads = jnp.stack([entry[0] for entry in matrix_list])
    out_grads = jnp.stack([entry[1] for entry in matrix_list])
    in_grads = jnp.stack([entry[2] for entry in matrix_list])
    back_grads = jnp.stack([entry[3] for entry in matrix_list])
    return (
        residual.astype(jnp.bfloat16),
        grad_rows,
        qkv_grads,
        out_grads,
        gain_grads,
        shift_grads,
        router_grads,
        in_grads,
        back_grads,
    )


ROWS = -(-SEQ // 16) * 16
MESH = pl.DeviceIdType.MESH
F32, BF16 = jnp.float32, jnp.bfloat16
NN, NT, TN = (((1,), (0,)), ((), ())), (((1,), (1,)), ((), ())), (((0,), (0,)), ((), ()))


def mm(left, right, dims=NN):
    return lax.dot_general(left, right, dims, preferred_element_type=F32)


def whole(index, size):
    return pl.ds(pl.multiple_of(index * size, size), size)


def normal_parts(value):
    centred = value - jnp.mean(value, axis=-1, keepdims=True)
    scale = lax.rsqrt(jnp.mean(centred * centred, axis=-1, keepdims=True) + 1e-06)
    return centred * scale, scale


def normal_pull(grad, unit, scale, gains):
    grad_unit = grad * gains
    mean_grad = jnp.mean(grad_unit, axis=-1, keepdims=True)
    mean_both = jnp.mean(grad_unit * unit, axis=-1, keepdims=True)
    return scale * (grad_unit - mean_grad - unit * mean_both)


def gelu_parts(value):
    size = jnp.abs(value)
    step = 1.0 / (1.0 + 0.3275911 * 2.0**-0.5 * size)
    bell = jnp.exp(-0.5 * (value * value))
    series = 1.061405429 * step - 1.453152027
    series = series * step + 1.421413741
    series = series * step - 0.284496736
    series = series * step + 0.254829592
    tail = 0.5 * series * step * bell
    share = jnp.where(value < 0, tail, 1.0 - tail)
    return value * share, share + value * (bell * 0.3989422804014327)


class Exchange:
    def __init__(self, source, target, device, landing, send, recv):
        self.out = pltpu.make_async_remote_copy(
            source, target, send, recv, device_id=device, device_id_type=MESH
        )
        self.into = pltpu.make_async_remote_copy(
            landing, landing, send, recv, device_id=device, device_id_type=MESH
        )

        self.open = [True, True]
        self.out.start()

    def arrived(self):
        if self.open[0]:
            self.into.wait_recv()
        self.open[0] = False

    def sent(self):
        if self.open[1]:
            self.out.wait_send()
        self.open[1] = False

    def finish(self):
        self.arrived()
        self.sent()


class Kept:
    def __init__(self, source, target, semaphore):
        self.copy = pltpu.make_async_copy(source, target, semaphore)
        self.open = True
        self.copy.start()

    def arrived(self):
        if self.open:
            self.copy.wait()
        self.open = False

    sent = finish = arrived


def block_kernel(depth_z, images, local_count, refs):
    H = depth_z
    (
        tokens, cot, counts, wq, wo, gain, bias, wr, win_hbm, wback_hbm, named_in, slots_in,
        out, tgrad, wqg, wog, lng, lnb, wrg, gin_out, gback_out,
        tgrad_held, stage, prow, wbuf, win, wback, rows_grad, rows_norm, big, wide,
        xsend, gsend, xrows, grows, xback, gback,
        normed, qkv, probs, mixed, middle, grad_mid, logit_grad,
        sib_out, sib_in, z_out, z_in, own_sum,
        att_in, plane_in, line_out, line_in,
        small_c, small_p, small_z, route_out, route_in, route_z, route_all,
        send_sems, recv_sems, local_sems,
    ) = refs
    own_rows, width = tokens.shape
    flat = -(-own_rows // 16) * 16
    half = width // 128
    f, h, t = (lax.axis_index(name) for name in ("fsdp", "heads", "tensor"))
    s = 1 - t
    fx = [f, f + 1 - 2 * lax.rem(f, 2), lax.rem(f + 2, 4), 3 - f]
    hz = [lax.rem(h + d, H) for d in range(H)]
    hfrom = [lax.rem(h + H - d, H) for d in range(H)]
    after, before, across = lax.rem(2 * h + 1, 5), lax.rem(3 * h + 2, 5), 3 - h
    counter = [0]
    pending = []

    def exchange(source, target, device, landing):
        index = counter[0]
        counter[0] += 1
        made = Exchange(
            source, target, device, landing, send_sems.at[index], recv_sems.at[index]
        )
        pending.append(made)
        return made

    local_counter = [0]

    def kept(source, target):
        made = Kept(source, target, local_sems.at[local_counter[0]])
        local_counter[0] += 1
        pending.append(made)
        return made

    barrier = pltpu.get_barrier_semaphore()
    peers = [(f, hz[d], t) for d in range(1, H)] + [(f, h, s)]
    peers += [(fx[d], h, c) for d in range(1, 4) for c in (t, s)]
    for peer in peers:
        pl.semaphore_signal(barrier, inc=1, device_id=peer, device_id_type=MESH)

    for i in range(3):
        wbuf[i, h, t, :, whole(f, 128)] = wq[i]
    wbuf[3, h, t, :, whole(f, 128)] = wo[...]
    pl.semaphore_wait(barrier, len(peers))

    first = [
        exchange(*[wbuf.at[:, h, t, :, whole(f, 128)]] * 2, (f, hz[d], t),
                 wbuf.at[:, hfrom[d], t, :, whole(f, 128)])
        for d in range(1, H)
    ]

    depth, span = win_hbm.shape[1], win_hbm.shape[2]

    def move_in(d, c):
        landing = win.at[whole(fx[d], depth), whole(c, span)]
        target = win.at[whole(f, depth), whole(t, span)]
        return exchange(win_hbm.at[fx[d] * 2 + c], target, (fx[d], h, c), landing)

    def move_back(d, c):
        landing = wback.at[whole(c, span), whole(fx[d], depth)]
        target = wback.at[whole(t, span), whole(f, depth)]
        return exchange(wback_hbm.at[fx[d] * 2 + c], target, (fx[d], h, c), landing)

    expert_moves = [move_in(d, c) for d, c in ((1, t), (2, t), (1, s), (2, s))]
    mine = [
        kept(win_hbm.at[f * 2 + t], win.at[whole(f, depth), whole(t, span)]),
        kept(wback_hbm.at[f * 2 + t], wback.at[whole(t, span), whole(f, depth)]),
    ]

    row_index = lax.broadcasted_iota(jnp.int32, (ROWS, 1), 0)

    def image(source, b):
        if b == 0:
            stage[0 : images * SEQ, :] = source[...].astype(F32)
        return jnp.where(row_index < SEQ, stage[b * SEQ : b * SEQ + ROWS, :], 0.0)

    flat_index = lax.broadcasted_iota(jnp.int32, (flat, 1), 0)
    flat_image = sum((flat_index >= b * SEQ).astype(jnp.int32) for b in range(1, images))
    living = (flat_index < own_rows) & ((h * 2 + t) * images + flat_image < counts[0])
    stage[0:own_rows, :] = cot[...].astype(F32)
    rows_grad[h * 2 + t, 0:flat, :] = jnp.where(living, stage[0:flat, :], 0.0).astype(BF16)

    cut = -(-flat // 32) * 16
    parts = [slice(0, cut), slice(cut, flat)]

    def hop(rows, line, part, to, source):
        here = rows.at[line * 2 + t, parts[part]]
        return exchange(here, here, (f, to, t), rows.at[source * 2 + t, parts[part]])

    def beside(rows, line):
        here = rows.at[line * 2 + t, 0:flat]
        return exchange(here, here, (f, h, s), rows.at[line * 2 + s, 0:flat])

    class Spread:
        def __init__(self, rows):
            self.rows = rows
            self.down = [hop(rows, h, 0, after, before), None]
            self.up = [None, hop(rows, h, 1, before, after)]
            self.near = [beside(rows, h)]

        def second(self):
            self.down[1] = hop(self.rows, h, 1, after, before)
            self.up[0] = hop(self.rows, h, 0, before, after)

        def relay(self):
            self.down[0].arrived()
            self.far = [hop(self.rows, before, 0, after, across)]
            self.up[1].arrived()
            self.far.append(hop(self.rows, after, 1, before, across))

        def share(self):
            self.down[1].arrived()
            self.near.append(beside(self.rows, before))
            self.up[0].arrived()
            self.near.append(beside(self.rows, after))

        def close(self):
            for move in self.far:
                move.arrived()
            self.near.append(beside(self.rows, across))

        def blocks(self):
            lines = [h, before, after, across]
            moves = self.near + [None] * (4 - len(self.near))
            return [(line * 2 + t, None) for line in lines] + [
                (line * 2 + s, move) for line, move in zip(lines, moves)
            ]

        def sent(self):
            for move in self.down + self.up + self.far + self.near:
                move.sent()

    grad_spread = Spread(rows_grad)

    for b in range(images):
        unit, _ = normal_parts(image(tokens, b))
        normed[b * ROWS : (b + 1) * ROWS, :] = (unit * gain[0:1] + bias[0:1]).astype(BF16)

    for step in first:
        step.arrived()

    def across_plane(span_i, source, to, landing):
        here = wbuf.at[span_i, :, t, :, whole(source, 128)]
        return exchange(here, here, (to, h, t), wbuf.at[span_i, :, t, :, whole(landing, 128)])

    both = [slice(0, 2), slice(2, 4)]
    second = [across_plane(slice(0, 4), f, fx[d], fx[d]) for d in (1, 2)]

    relative = named_in[...] - h * local_count
    wanted = (slots_in[...] >= 0) & (relative >= 0) & (relative < local_count)
    wanted = wanted & (lax.rem(relative + 2 * local_count, 2) == t)
    places = jnp.where(wanted, lax.div(relative, 2) * CAP + slots_in[...], -1)
    reach = -(-flat // 128) * 128 + 128
    tail = jnp.full((2, reach), -1, jnp.int32)
    places = jnp.concatenate([places, tail], axis=1)[:, 0 : places.shape[1] // 128 * 128 + reach]
    place_lane = lax.broadcasted_iota(jnp.int32, (2, reach), 1)
    for b in range(2 * H):
        begin = b * own_rows
        base = begin // 128 * 128
        window = pltpu.roll(places[:, base : base + reach], (base - begin) % reach, 1)
        rows = jnp.where(place_lane < own_rows, window, -1)
        prow[b, 0:2, :] = rows[:, 0 : prow.shape[2]]

    def mark_slots(b):
        for part in range(4):
            spot = lax.broadcasted_iota(jnp.int32, (CAP, flat), 0) + CAP * part
            named = (prow[b, 0:1, 0:flat] == spot) | (prow[b, 1:2, 0:flat] == spot)
            big[b, part * CAP : (part + 1) * CAP, 0:flat] = jnp.where(named, 1.0, 0.0).astype(BF16)

    grad_spread.second()
    pl.loop(0, 2 * H)(mark_slots)
    for d in (1, 2):
        second[d - 1].arrived()
        second.append(across_plane(both[d - 1], fx[d], fx[3 - d], fx[3]))
    grad_spread.relay()
    for step in second[2:]:
        step.arrived()
    third = exchange(*[wbuf.at[:, :, t]] * 2, (f, h, s), wbuf.at[:, :, s])

    for d, c in ((3, t), (3, s), (0, s)):
        expert_moves.append(move_in(d, c))
    for d, c in ((1, t), (2, t), (1, s), (2, s), (3, t), (3, s), (0, s)):
        expert_moves.append(move_back(d, c))

    grad_spread.share()
    third.arrived()

    for i in range(3):
        part = mm(normed[...], wbuf[i].reshape(width, width), NT)
        if i == 0:
            part = part * HEAD ** (-0.5)
        qkv[:, i * width : (i + 1) * width] = part.astype(BF16)
    lane = lax.broadcasted_iota(jnp.int32, (1, 128), 1)
    sides = [jnp.where(lane < HEAD, 1.0, 0.0).astype(BF16), jnp.where(lane < HEAD, 0.0, 1.0).astype(BF16)]
    key_index = lax.broadcasted_iota(jnp.int32, (1, ROWS), 1)

    def pair_of(index):
        b, pair = index // half, lax.rem(index, half)
        rows = whole(b, ROWS)
        cols = [whole(pair + i * half, 128) for i in range(3)]
        return rows, cols

    @pl.loop(0, images * half)
    def _(index):
        rows, cols = pair_of(index)
        query, key, value = (qkv[rows, col] for col in cols)
        total = jnp.zeros((ROWS, 128), F32)
        for side in range(2):
            score = mm(query * sides[side], key, NT)
            score = jnp.where(key_index < SEQ, score, -1e30)
            score = jnp.exp(score - jnp.max(score, axis=-1, keepdims=True))
            prob = score / jnp.sum(score, axis=-1, keepdims=True)
            probs[index * 2 + side] = prob
            total += mm(prob.astype(BF16), value * sides[side])
        mixed[rows, cols[0]] = total.astype(BF16)

    for b in range(images):
        rows = slice(b * ROWS, (b + 1) * ROWS)
        value = image(tokens, b) + mm(mixed[rows, :], wbuf[3].reshape(width, width))
        middle[rows, :] = value
        unit, _ = normal_parts(value)
        own_sum[0, b * SEQ : (b + 1) * SEQ, :] = (unit * gain[1:2] + bias[1:2])[0:SEQ]
    own_flat = jnp.where(flat_index < own_rows, own_sum[0, 0:flat, :], 0.0)
    rows_norm[h * 2 + t, 0:flat, :] = own_flat.astype(BF16)

    norm_spread = Spread(rows_norm)
    grad_spread.close()

    def accumulate(rows, b, begin):
        for part in range(4):
            span_rows = slice(part * CAP, (part + 1) * CAP)
            value = mm(big[b, span_rows, 0:flat], rows[b, 0:flat])
            wide[span_rows, :] = value if begin else wide[span_rows, :] + value

    def accumulate_all(spread, order):
        blocks = spread.blocks()
        for place in order:
            b, move = blocks[place]
            if move is not None:
                move.arrived()
            accumulate(spread.rows, b, place == 0)

    def pack(send):
        for part in range(4):
            send[part] = wide[part * CAP : (part + 1) * CAP, :].astype(BF16)

    def to_group(d, send, landing):
        return exchange(send.at[fx[d]], landing.at[f], (fx[d], h, t), landing.at[fx[d]])

    def dispatch(send, landing, last=4):
        landing[f] = send[f]
        return [None] + [to_group(d, send, landing) for d in range(1, last)]

    accumulate_all(grad_spread, (0, 1, 2, 3))
    norm_spread.second()
    accumulate_all(grad_spread, (4, 5, 6, 7))
    pack(gsend)
    norm_spread.relay()
    grad_moved = dispatch(gsend, grows)
    norm_spread.share()
    accumulate_all(norm_spread, (0, 1, 2, 4, 5, 6))
    norm_spread.close()
    accumulate_all(norm_spread, (3, 7))
    pack(xsend)
    norm_moved = dispatch(xsend, xrows, 3)

    expert = h * local_count + f * 2 + t
    router_lane = lax.broadcasted_iota(jnp.int32, (1, wr.shape[0]), 1)
    chosen = (router_lane == expert).astype(F32)
    chunk = 512
    chunks = win.shape[1] // chunk
    for move in mine + expert_moves:
        move.arrived()
    back_moves = []
    for d in range(4):
        group = fx[d]
        here = whole(group, CAP)
        if d:
            norm_moved[d].arrived()
        rows = xrows[group]
        piece = 256
        ahead = mm(rows, win[:, 0:piece])
        result, held = None, None
        for c in range(win.shape[1] // piece):
            here_in = slice(c * piece % chunk, c * piece % chunk + piece)
            hidden = ahead
            if c + 1 < win.shape[1] // piece:
                ahead = mm(rows, win[:, (c + 1) * piece : (c + 2) * piece])
            value, slope = gelu_parts(hidden)
            value = value.astype(BF16)
            big[c * piece // chunk, here, here_in] = value
            wide[c * piece // chunk * CAP : (c * piece // chunk + 1) * CAP, here_in] = slope
            if c:
                term = mm(held, wback[(c - 1) * piece : c * piece, :])
                result = term if c == 1 else result + term
            held = value
        result = result + mm(held, wback[win.shape[1] - piece :, :])
        logits = mm(rows, wr[...], NT)
        odds = jnp.exp(logits - jnp.max(logits, axis=-1, keepdims=True))
        odds = odds / jnp.sum(odds, axis=-1, keepdims=True)
        gate = jnp.sum(odds * chosen, axis=-1, keepdims=True)
        if d:
            grad_moved[d].finish()
            norm_moved[d].sent()
        gsend[group] = (gate * result).astype(BF16)
        row_grad = grows[group].astype(F32)
        gate_grad = jnp.sum(row_grad * result, axis=-1, keepdims=True)
        result_grad = (gate * row_grad).astype(BF16)
        grows[group] = result_grad
        logit = (gate_grad * gate * (chosen - odds)).astype(BF16)
        logit_grad[here, :] = logit
        parts_grad = []
        for c in range(chunks):
            grad = mm(result_grad, wback[c * chunk : (c + 1) * chunk, :], NT)
            grad = (grad * wide[c * CAP : (c + 1) * CAP, :]).astype(BF16)
            big[4 + c, here, :] = grad
            parts_grad.append(grad)
        total = mm(logit, wr[...]) + mm(jnp.concatenate(parts_grad, axis=1), win[...], NT)
        if d:
            xsend[group] = total.astype(BF16)
            back_moves.append(to_group(d, xsend, xback))
        else:
            xback[f] = total.astype(BF16)
        if d == 0:
            norm_moved.append(to_group(3, xsend, xrows))

    grad_spread.sent()
    norm_spread.sent()
    flat_rows = xrows[...].reshape(4 * CAP, width)
    route = mm(logit_grad[...], flat_rows, TN)
    share_rows = wr.shape[0] // 8
    for j in range(8):
        for part in range(2):
            route_out[j, part * share_rows : (part + 1) * share_rows, :] = route[
                j * share_rows : (j + 1) * share_rows, part * (width // 2) : (part + 1) * (width // 2)
            ]
    route_in[f * 2 + t] = route_out[f * 2 + t]
    plane_peers = [(d, c) for d in range(4) for c in ((t, s) if d else (s,))]
    route_moves = [
        exchange(route_out.at[fx[d] * 2 + c], route_in.at[f * 2 + t], (fx[d], h, c), route_in.at[fx[d] * 2 + c])
        for d, c in plane_peers
    ]
    flat_grad = grows[...].reshape(4 * CAP, width)
    for c in range(chunks):
        rows_grad[c] = mm(flat_rows, big[4 + c], TN).astype(BF16)
        rows_norm[c] = mm(big[c], flat_grad, TN).astype(BF16)
    for move in route_moves:
        move.arrived()
    route = route_in[0]
    for j in range(1, 8):
        route = route + route_in[j]
    route_z[h] = route
    route_line = [
        exchange(route_z.at[h], route_z.at[h], (f, hz[d], t), route_z.at[hfrom[d]]) for d in range(1, H)
    ]

    for move in back_moves:
        move.arrived()
    out_moves = dispatch(gsend, gback)[1:]

    halves = chunks // 2

    def to_owner(d, c, part, back):
        device, one = (fx[d], h, c), d == 0 and c is t
        span_part = slice(part * chunk, (part + 1) * chunk)
        if back:
            source = rows_norm.at[c * halves + part, :, whole(fx[d], depth)]
            target = gback_out.at[f * 2 + t, span_part]
            landing = gback_out.at[fx[d] * 2 + c, span_part]
        else:
            source = rows_grad.at[c * halves + part, whole(fx[d], depth), :]
            target = gin_out.at[f * 2 + t, :, span_part]
            landing = gin_out.at[fx[d] * 2 + c, :, span_part]
        if one:
            kept(source, target)
        else:
            exchange(source, target, device, landing)

    def to_owners(part, back):
        for d in (1, 2, 3, 0):
            for c in (t, s):
                to_owner(d, c, part, back)

    def share(b, back):
        spots = jnp.transpose(prow[b])[0:flat]
        slot = lax.broadcasted_iota(jnp.int32, (flat, 4 * CAP), 1)
        named = (spots[:, 0:1] == slot) | (spots[:, 1:2] == slot)
        return mm(jnp.where(named, 1.0, 0.0).astype(BF16), back[...].reshape(4 * CAP, width))

    class Gather:
        def __init__(self, which, back, near_out, far_out):
            self.which, self.back = which, back
            self.near_out, self.far_out = near_out, far_out
            self.lines = [across, after, before, h]
            self.near = []

        def give(self, place):
            line = self.lines[place]
            self.near_out(place)[...] = share(line * 2 + s, self.back).astype(BF16)
            landing = sib_in.at[self.which, place]
            self.near.append(exchange(self.near_out(place), landing, (f, h, s), landing))

        def take(self, place):
            value = share(self.lines[place] * 2 + t, self.back)
            self.near[place].arrived()
            value = value + sib_in[self.which, place].astype(F32)
            if place == 3:
                own_sum[self.which, 0:flat, :] = value
            else:
                self.far_out(place)[...] = value.astype(BF16)

        def hop(self, place, part, to, slot):
            landing = z_in.at[self.which, slot, parts[part]]
            return exchange(self.far_out(place).at[parts[part]], landing, (f, to, t), landing)

        def start(self):
            self.first = [self.hop(0, 0, after, 0), self.hop(0, 1, before, 0)]

        def direct(self, place):
            part, to = ((1, after), (0, before))[place - 1]
            self.last = getattr(self, "last", []) + [self.hop(place, part, to, place)]

        def relay(self):
            for place, part, to in ((1, 0, after), (2, 1, before)):
                self.first[part].arrived()
                rows = self.far_out(place).at[parts[part]]
                passed = z_in[self.which, 0, parts[part], :].astype(F32)
                rows[...] = (rows[...].astype(F32) + passed).astype(BF16)
                self.last.append(self.hop(place, part, to, place))

        def total(self):
            for move in self.last:
                move.arrived()
            total = own_sum[self.which, 0:flat, :]
            for slot in (1, 2):
                total = total + z_in[self.which, slot].astype(F32)
            own_sum[self.which, 0:flat, :] = total

    norm_sums = Gather(0, xback, lambda place: sib_out.at[place], lambda place: z_out.at[place])
    norm_sums.give(0)
    norm_sums.take(0)
    norm_sums.start()
    to_owners(0, True)
    norm_sums.give(1)
    norm_sums.give(2)
    norm_sums.take(1)
    norm_sums.direct(1)
    norm_sums.take(2)
    norm_sums.direct(2)
    norm_sums.give(3)
    norm_sums.take(3)
    for move in out_moves:
        move.arrived()
    to_owners(1, True)
    to_owners(0, False)
    out_sums = Gather(
        1, gback, lambda place: big.at[place, 0:flat], lambda place: big.at[4 + place, 0:flat]
    )
    out_sums.give(0)
    out_sums.take(0)
    for place in range(1, 4):
        out_sums.give(place)
    norm_sums.relay()
    for place in range(1, 4):
        out_sums.take(place)


    norm_sums.total()
    out_sums.start()
    small_c[t] = jnp.zeros(small_c.shape[1:], F32)
    for b in range(images):
        rows = slice(b * ROWS, (b + 1) * ROWS)
        grad = jnp.where(row_index < SEQ, own_sum[0, b * SEQ : b * SEQ + ROWS, :], 0.0)
        unit, scale = normal_parts(middle[rows, :])
        small_c[t, 1:2] += jnp.sum(grad * unit, axis=0, keepdims=True)
        small_c[t, 3:4] += jnp.sum(grad, axis=0, keepdims=True)
        live = ((h * 2 + t) * images + b < counts[0]).astype(F32)
        grad = normal_pull(grad, unit, scale, gain[1:2]) + image(cot, b) * live
        grad_mid[rows, :] = grad

    out_sums.direct(1)
    out_sums.direct(2)

    for move in back_moves:
        move.sent()
    low = grad_mid[...].astype(BF16)
    count = H * 2 * 64
    wide[3 * count : 4 * count, :] = mm(mixed[...], low, TN)

    def wide_rows(i, other, core):
        return whole((i * H + other) * 2 + core, 64)

    def core_sums(span_i, others):
        for i in span_i:
            for other in others:
                xsend[i, whole(other, 64), :] = wide[wide_rows(i, other, s), :].astype(BF16)
        here = (slice(span_i.start, span_i.stop), whole(others[0], 64))
        if len(others) > 1:
            here = (here[0], slice(0, H * 64))
        landing = att_in.at[here]
        return here, exchange(xsend.at[here], landing, (f, h, s), landing)

    def plane_sums(span_i, others, near):
        here, move = near
        move.finish()
        for i in span_i:
            for other in others:
                place, low_rows = wide_rows(i, other, t), whole(other, 64)
                value = wide[place, :] + att_in[i, low_rows, :].astype(F32)
                wide[place, :] = value
                xsend[i, low_rows, :] = value.astype(BF16)
        return [
            exchange(
                xsend.at[(*here, whole(fx[d], 128))], plane_in.at[(f, *here)],
                (fx[d], h, t), plane_in.at[(fx[d], *here)],
            )
            for d in range(1, 4)
        ]

    def own_columns(i, other):
        value = wide[wide_rows(i, other, t), whole(f, 128)]
        for d in range(1, 4):
            value = value + plane_in[fx[d], i, whole(other, 64), :].astype(F32)
        return value

    last_near = core_sums(range(3, 4), list(range(H)))
    mixed[...] = mm(low, wbuf[3].reshape(width, width), NT).astype(BF16)

    def attention_back(index):
        rows, cols = pair_of(index)
        query, key, value = (qkv[rows, col] for col in cols)
        pulled = mixed[rows, cols[0]]
        grads = [jnp.zeros((ROWS, 128), F32) for _ in range(3)]
        for side in range(2):
            prob = probs[index * 2 + side]
            one = pulled * sides[side]
            prob_grad = mm(one, value, NT)
            grads[2] += mm(prob.astype(BF16), one, TN)
            inner = jnp.sum(prob * prob_grad, axis=-1, keepdims=True)
            score_grad = (prob * (prob_grad - inner)).astype(BF16)
            grads[0] += mm(score_grad, key * sides[side])
            grads[1] += mm(score_grad, query * sides[side], TN)
        grads[0] = grads[0] * HEAD ** (-0.5)
        for grad, col in zip(grads, cols):
            qkv[rows, col] = grad.astype(BF16)

    order = [hz[1], hz[2], hz[3], hz[0]]
    nears, planes = [], []
    for turn, other in enumerate(order):
        pl.loop(0, images)(lambda b, other=other: attention_back(b * half + other))
        for i in range(3):
            rows = pl.ds(pl.multiple_of((i * H + other) * 128, 128), 128)
            wide[rows, :] = mm(qkv[:, whole(i * half + other, 128)], normed[...], TN)
        nears.append(core_sums(range(3), [other]))
        if turn == 0:
            last_plane = plane_sums(range(3, 4), list(range(H)), last_near)
        else:
            planes.append(plane_sums(range(3), [order[turn - 1]], nears[turn - 1]))
    out_sums.relay()

    for b in range(images):
        rows = slice(b * ROWS, (b + 1) * ROWS)
        grad = jnp.zeros((ROWS, width), F32)
        for i in range(3):
            grad += mm(qkv[rows, i * width : (i + 1) * width], wbuf[i].reshape(width, width))
        unit, scale = normal_parts(image(tokens, b))
        small_c[t, 0:1] += jnp.sum(grad * unit, axis=0, keepdims=True)
        small_c[t, 2:3] += jnp.sum(grad, axis=0, keepdims=True)
        grad = normal_pull(grad, unit, scale, gain[0:1]) + grad_mid[rows, :]
        tgrad_held[b * SEQ : (b + 1) * SEQ, :] = grad[0:SEQ]
    kept(tgrad_held, tgrad)
    small_near = exchange(small_c.at[t], small_c.at[t], (f, h, s), small_c.at[s])

    planes.append(plane_sums(range(3), [order[3]], nears[3]))
    small_near.arrived()
    small_p[f] = small_c[0] + small_c[1]
    small_plane = [
        exchange(small_p.at[f], small_p.at[f], (fx[d], h, t), small_p.at[fx[d]]) for d in range(1, 4)
    ]
    for move in route_line:
        move.arrived()
    route = route_z[0]
    for d in range(1, H):
        route = route + route_z[d]
    route_all[f * 2 + t] = route
    route_last = [
        exchange(route_all.at[f * 2 + t], route_all.at[f * 2 + t], (fx[d], h, c), route_all.at[fx[d] * 2 + c])
        for d, c in plane_peers
    ]

    for move in last_plane:
        move.arrived()
    to_owners(1, False)
    line = []
    for turn in range(3):
        for move in planes[turn]:
            move.arrived()
        other = order[turn]
        for i in range(4):
            line_out[other, i] = own_columns(i, other).astype(BF16)
        d = turn + 1
        line.append(
            exchange(line_out.at[other], line_in.at[h], (f, other, t), line_in.at[hfrom[d]])
        )
    for move in planes[3]:
        move.arrived()
    for move in small_plane:
        move.arrived()
    small_z[h] = (small_p[0] + small_p[1]) + (small_p[2] + small_p[3])
    small_line = [
        exchange(small_z.at[h], small_z.at[h], (f, hz[d], t), small_z.at[hfrom[d]]) for d in range(1, H)
    ]
    for move in route_last:
        move.arrived()
    for j in range(8):
        for part in range(2):
            wrg[j * share_rows : (j + 1) * share_rows, part * (width // 2) : (part + 1) * (width // 2)] = (
                route_all[j, part * share_rows : (part + 1) * share_rows, :]
            )

    out_sums.total()
    for b in range(images):
        stage[b * SEQ : (b + 1) * SEQ, :] = middle[b * ROWS : b * ROWS + SEQ, :]
    out[...] = (stage[0:own_rows, :] + own_sum[1, 0:own_rows, :]).astype(BF16)

    for move in line:
        move.arrived()
    for i in range(4):
        value = own_columns(i, h)
        for d in range(1, H):
            value = value + line_in[hfrom[d], i].astype(F32)
        if i < 3:
            wqg[i] = value
        else:
            wog[...] = value
    for move in small_line:
        move.arrived()
    total = small_z[0]
    for d in range(1, H):
        total = total + small_z[d]
    lng[...] = total[0:2]
    lnb[...] = total[2:4]

    for move in pending:
        move.finish()


def finish_kernel(*refs):
    sources, targets = refs[:9], refs[9:18]
    held, wider = refs[18:27], refs[27:29]
    in_sems, out_sems = refs[29], refs[30]
    experts = sources[7].shape[0]
    inward, outward = [], []

    def begin(source, target, semaphores, index):
        copy = pltpu.make_async_copy(source, target, semaphores.at[index])
        copy.start()
        return copy

    for e in range(experts):
        for k in (7, 8):
            index = 7 + 2 * e + k - 7
            inward.append((e, k, index, begin(sources[k].at[e], held[k].at[e], in_sems, index)))
    small = [begin(sources[k], held[k], in_sems, k) for k in range(7)]
    for e, k, index, copy in inward:
        copy.wait()
        wider[k - 7][e] = held[k][e].astype(F32)
        outward.append(begin(wider[k - 7].at[e], targets[k].at[e], out_sems, index))
    for k, copy in enumerate(small):
        copy.wait()
        outward.append(begin(held[k], targets[k], out_sems, k))
    for copy in outward:
        copy.wait()


def fast_device(
    tokens,
    cotangent,
    image_counts,
    w_qkv,
    w_out,
    ln_gain,
    ln_bias,
    w_router,
    w_in,
    w_back,
    expert_ids,
    slots,
):
    H = lax.axis_size("heads")
    own_rows, width = tokens.shape
    images = own_rows // SEQ
    own = images * ROWS
    flat = -(-own_rows // 16) * 16
    local_count, depth, span = w_in.shape[1:]
    experts = w_router.shape[2]
    hidden = span * 2
    vmem = pl.BlockSpec(memory_space=pltpu.VMEM)
    smem = pl.BlockSpec(memory_space=pltpu.SMEM)
    anywhere = pl.BlockSpec(memory_space=pl.ANY)
    shape = jax.ShapeDtypeStruct

    def low(*dims):
        return pltpu.VMEM(dims, BF16)

    def full(*dims):
        return pltpu.VMEM(dims, F32)

    outs = pl.pallas_call(
        lambda *refs: block_kernel(H, images, local_count, refs),
        out_shape=(
            shape((own_rows, width), BF16),
            shape((own_rows, width), F32),
            shape((3, 64, depth), F32),
            shape((64, depth), F32),
            shape((2, width), F32),
            shape((2, width), F32),
            shape((experts, width), F32),
            shape((local_count, depth, span), BF16),
            shape((local_count, span, depth), BF16),
        ),
        in_specs=[vmem, vmem, smem, vmem, vmem, vmem, vmem, vmem, anywhere, anywhere, vmem, vmem],
        out_specs=[vmem, anywhere] + [vmem] * 5 + [anywhere] * 2,
        scratch_shapes=[
            full(own_rows, width),
            full(images * SEQ + 16, width),
            pltpu.VMEM((2 * H, 8, -(-flat // 128) * 128), jnp.int32),
            low(4, H, 2, 64, width),
            low(width, hidden),
            low(hidden, width),
            low(2 * H, 512, width),
            low(2 * H, 512, width),
            low(8, 4 * CAP, 512),
            full(8 * CAP, width),
            low(4, CAP, width),
            low(4, CAP, width),
            low(4, CAP, width),
            low(4, CAP, width),
            low(4, CAP, width),
            low(4, CAP, width),
            low(own, width),
            low(own, 3 * width),
            full(images * width // HEAD, ROWS, ROWS),
            low(own, width),
            full(own, width),
            full(own, width),
            low(4 * CAP, experts),
            low(H, flat, width),
            low(2, H, flat, width),
            low(3, flat, width),
            low(2, 3, flat, width),
            full(2, own, width),
            low(4, H * 64, width),
            low(4, 4, H * 64, 128),
            low(H, 4, 64, 128),
            low(H, 4, 64, 128),
            full(2, 8, width),
            full(4, 8, width),
            full(H, 8, width),
            full(8, experts // 4, width // 2),
            full(8, experts // 4, width // 2),
            full(H, experts // 4, width // 2),
            full(8, experts // 4, width // 2),
            pltpu.SemaphoreType.DMA((192,)),
            pltpu.SemaphoreType.DMA((192,)),
            pltpu.SemaphoreType.DMA((16,)),
        ],
        compiler_params=pltpu.CompilerParams(
            collective_id=0, has_side_effects=True, vmem_limit_bytes=62 * 2**20
        ),
        name="block",
    )(
        tokens, cotangent, image_counts, jnp.transpose(w_qkv[0], (0, 2, 1)), w_out[0], ln_gain[0], ln_bias[0],
        jnp.transpose(w_router[0]),
        w_in[0], w_back[0], jnp.transpose(expert_ids[0]), jnp.transpose(slots[0]),
    )
    sems = pltpu.SemaphoreType.DMA((7 + 2 * local_count,))
    outs = pl.pallas_call(
        finish_kernel,
        out_shape=[shape(part.shape, F32 if i >= 7 else part.dtype) for i, part in enumerate(outs)],
        in_specs=[anywhere] * 9,
        out_specs=[anywhere] * 9,
        scratch_shapes=[pltpu.VMEM(part.shape, part.dtype) for part in outs]
        + [full(*part.shape) for part in outs[7:]]
        + [sems, sems],
        compiler_params=pltpu.CompilerParams(vmem_limit_bytes=62 * 2**20),
        name="finish",
    )(*outs)
    block_out, token_grad, qkv_grad, out_grad, gains, shifts, router, in_grad, back_grad = outs
    return (
        block_out,
        token_grad,
        jnp.transpose(qkv_grad, (0, 2, 1))[None],
        out_grad[None],
        gains[None],
        shifts[None],
        jnp.transpose(router)[None],
        in_grad[None],
        back_grad[None],
    )


def solution(mesh):
    def program(*arrays):
        sizes = dict(mesh.shape)
        devices = sizes["fsdp"] * sizes["heads"] * sizes["tensor"]
        own_rows = arrays[0].shape[0] // devices
        one_expert = sizes["fsdp"] == 4 and sizes["tensor"] == 2 and arrays[8].shape[1] == devices
        one_expert = one_expert and sizes["heads"] == 4 and own_rows % (2 * SEQ) == 0
        return placed(mesh, fast_device if one_expert else on_device)(*arrays)

    return program


def placed(mesh, on_device):
    return jax.shard_map(
        on_device,
        mesh=mesh,
        in_specs=(
            P(("fsdp", "heads", "tensor"), None),
            P(("fsdp", "heads", "tensor"), None),
            P("fsdp"),
            P(None, None, "fsdp", ("heads", "tensor")),
            P(None, ("heads", "tensor"), "fsdp"),
            P(),
            P(),
            P(),
            P(None, "heads", "fsdp", "tensor"),
            P(None, "heads", "tensor", "fsdp"),
            P(None, "fsdp", None),
            P(None, "fsdp", None),
        ),
        out_specs=(
            P(("fsdp", "heads", "tensor"), None),
            P(("fsdp", "heads", "tensor"), None),
            P(None, None, "fsdp", ("heads", "tensor")),
            P(None, ("heads", "tensor"), "fsdp"),
            P(),
            P(),
            P(),
            P(None, "heads", "fsdp", "tensor"),
            P(None, "heads", "tensor", "fsdp"),
        ),
        check_vma=False,
    )
```

```python
import jax
import jax.numpy as jnp
from jax import lax
from jax.experimental import pallas as pl
from jax.experimental.pallas import tpu as pltpu
from jax.sharding import PartitionSpec as P

HEAD = 64
SEQ = 197
LAYERS = 1
CAP = 256


def layer_norm(value, ln_gains, ln_shift):
    centred = value - jnp.mean(value, axis=-1, keepdims=True)
    spread = jnp.mean(centred * centred, axis=-1, keepdims=True)
    return centred * lax.rsqrt(spread + 1e-06) * ln_gains + ln_shift


def gelu_exact(value):
    return jax.nn.gelu(value, approximate=False)


def with_zero_row(matrix):
    return jnp.concatenate([matrix, jnp.zeros((1,) + matrix.shape[1:], matrix.dtype)], axis=0)


def slot_tables(named_expert, slot_rows, first_expert, local_experts):
    group_rows = named_expert.shape[0]
    is_local = (
        (slot_rows >= 0)
        & (named_expert >= first_expert)
        & (named_expert < first_expert + local_experts)
    )
    places = jnp.where(
        is_local, (named_expert - first_expert) * CAP + slot_rows, local_experts * CAP
    )
    picked = jnp.full((local_experts * CAP + 1,), 2 * group_rows, jnp.int32)
    picked = picked.at[places.reshape(-1)].set(jnp.arange(2 * group_rows, dtype=jnp.int32))
    return (places, picked[: local_experts * CAP])


def joined_qkv(qkv_weight):
    head_cols = qkv_weight.shape[2]
    return jnp.transpose(qkv_weight, (1, 0, 2)).reshape(qkv_weight.shape[1], 3 * head_cols)


def forward_block(
    residual, weights, ln_gains, ln_shift, router_weight, named_expert, slot_rows, first_expert
):
    qkv_weight, out_weight, in_weight, back_weight = weights
    own_rows, widths = residual.shape
    group_rows = named_expert.shape[0]
    head_cols = qkv_weight.shape[2]
    local_experts = in_weight.shape[0]
    head_shape = (group_rows // SEQ, SEQ, head_cols // HEAD, HEAD)
    q_scale = HEAD ** (-0.5)
    flat_qkv = joined_qkv(qkv_weight)
    normed_rows = layer_norm(residual, ln_gains[0], ln_shift[0]).astype(jnp.bfloat16)
    normed = lax.all_gather(normed_rows, ("heads", "tensor"), axis=0, tiled=True)
    projected = jnp.dot(normed, flat_qkv, preferred_element_type=jnp.float32)
    queries = (projected[:, :head_cols] * q_scale).astype(jnp.bfloat16).reshape(head_shape)
    key_rows = projected[:, head_cols : 2 * head_cols].astype(jnp.bfloat16).reshape(head_shape)
    value_rows = projected[:, 2 * head_cols :].astype(jnp.bfloat16).reshape(head_shape)
    scores = jnp.einsum("bqhd,bkhd->bhqk", queries, key_rows, preferred_element_type=jnp.float32)
    log_total = jax.nn.logsumexp(scores, axis=-1)
    attn_probs = jax.nn.softmax(scores, axis=-1).astype(jnp.bfloat16)
    mixed_rows = jnp.einsum(
        "bhqk,bkhd->bqhd", attn_probs, value_rows, preferred_element_type=jnp.float32
    )
    mixed_rows = mixed_rows.reshape(group_rows, head_cols).astype(jnp.bfloat16)
    middle = residual + lax.psum_scatter(
        jnp.dot(mixed_rows, out_weight, preferred_element_type=jnp.float32),
        ("heads", "tensor"),
        scatter_dimension=0,
        tiled=True,
    )
    head_full = ()
    normed_two_rows = layer_norm(middle, ln_gains[1], ln_shift[1]).astype(jnp.bfloat16)
    normed_two = lax.all_gather(normed_two_rows, ("heads", "tensor"), axis=0, tiled=True)
    router = jax.nn.softmax(
        jnp.dot(normed_two, router_weight, preferred_element_type=jnp.float32), axis=-1
    )
    gate_values = jnp.take_along_axis(router, named_expert, axis=1) * (slot_rows >= 0)
    places, picked = slot_tables(named_expert, slot_rows, first_expert, local_experts)
    routed = with_zero_row(normed_two)[picked // 2].reshape(local_experts, CAP, widths)
    hidden = jnp.einsum("ecd,edf->ecf", routed, in_weight, preferred_element_type=jnp.float32)
    active = gelu_exact(hidden).astype(jnp.bfloat16)
    result = jnp.einsum("ecf,efd->ecd", active, back_weight, preferred_element_type=jnp.float32)
    flat_result = with_zero_row(result.reshape(local_experts * CAP, widths))
    block_out = middle + lax.psum_scatter(
        (
            flat_result[places[:, 0]] * gate_values[:, 0:1]
            + flat_result[places[:, 1]] * gate_values[:, 1:2]
        ).astype(jnp.bfloat16),
        ("heads", "tensor"),
        scatter_dimension=0,
        tiled=True,
    ).astype(jnp.float32)
    stored = (
        residual,
        middle,
        normed,
        queries,
        key_rows,
        value_rows,
        log_total,
        mixed_rows,
        normed_two_rows,
        router,
        gate_values,
        places,
        picked,
        routed,
        hidden,
        active,
        flat_result,
    )
    return (block_out, stored, head_full)


def backward_block(
    grad_rows, stored, weights, ln_gains, ln_shift, router_weight, named_expert, row_start
):
    qkv_weight, out_weight, in_weight, back_weight = weights
    (
        residual,
        middle,
        normed,
        queries,
        key_rows,
        value_rows,
        log_total,
        mixed_rows,
        normed_two_rows,
        router,
        gate_values,
        places,
        picked,
        routed,
        hidden,
        active,
        flat_result,
    ) = stored
    own_rows, widths = residual.shape
    group_rows = named_expert.shape[0]
    head_cols = qkv_weight.shape[2]
    local_experts = in_weight.shape[0]
    expert_count = router.shape[1]
    q_scale = HEAD ** (-0.5)
    flat_qkv = joined_qkv(qkv_weight)
    grad_moe = lax.all_gather(
        grad_rows.astype(jnp.bfloat16), ("heads", "tensor"), axis=0, tiled=True
    )
    back_rows = with_zero_row(grad_moe)[picked // 2].astype(jnp.float32)
    gate_slots = with_zero_row(gate_values.reshape(-1))[picked]
    gate_grad_slots = jnp.sum(back_rows * flat_result[:-1], axis=1)
    gate_grads = with_zero_row(gate_grad_slots)[places]
    expert_range = jnp.arange(expert_count, dtype=jnp.int32)
    router_part = jnp.sum(
        gate_grads[:, :, None]
        * (named_expert[:, :, None] == expert_range[None, None, :]).astype(jnp.float32),
        axis=1,
    )
    grad_result = (
        (gate_slots[:, None] * back_rows).astype(jnp.bfloat16).reshape(local_experts, CAP, widths)
    )
    grad_active = jnp.einsum(
        "ecd,efd->ecf", grad_result, back_weight, preferred_element_type=jnp.float32
    )
    gelu_value, gelu_pull = jax.vjp(gelu_exact, hidden)
    grad_hidden = gelu_pull(grad_active)[0].astype(jnp.bfloat16)
    back_grad = jnp.einsum("ecf,ecd->efd", active, grad_result, preferred_element_type=jnp.float32)
    in_grad = jnp.einsum("ecd,ecf->edf", routed, grad_hidden, preferred_element_type=jnp.float32)
    grad_routed = jnp.einsum(
        "ecf,edf->ecd", grad_hidden, in_weight, preferred_element_type=jnp.float32
    )
    grad_routed = with_zero_row(grad_routed.reshape(local_experts * CAP, widths))
    token_part = grad_routed[places[:, 0]] + grad_routed[places[:, 1]]
    grad_normed_two, router_rows = (
        lax.psum_scatter(token_part, ("heads", "tensor"), scatter_dimension=0, tiled=True),
        lax.psum_scatter(router_part, ("heads", "tensor"), scatter_dimension=0, tiled=True),
    )
    router_own = lax.dynamic_slice_in_dim(router, row_start, own_rows, 0)
    grad_logits = (
        router_own * (router_rows - jnp.sum(router_own * router_rows, axis=-1, keepdims=True))
    ).astype(jnp.bfloat16)
    router_grad = jnp.einsum(
        "td,te->de", normed_two_rows, grad_logits, preferred_element_type=jnp.float32
    )
    grad_normed_two = grad_normed_two + jnp.einsum(
        "te,de->td", grad_logits, router_weight, preferred_element_type=jnp.float32
    )
    norm_value, norm_pull = jax.vjp(layer_norm, middle, ln_gains[1], ln_shift[1])
    grad_middle, gain_two, shift_two = norm_pull(grad_normed_two)
    grad_middle = grad_middle + grad_rows
    grad_attn = lax.all_gather(
        grad_middle.astype(jnp.bfloat16), ("heads", "tensor"), axis=0, tiled=True
    )
    out_grad = jnp.einsum("tc,td->cd", mixed_rows, grad_attn, preferred_element_type=jnp.float32)
    grad_mixed = jnp.einsum("td,cd->tc", grad_attn, out_weight, preferred_element_type=jnp.float32)
    grad_mixed = grad_mixed.astype(jnp.bfloat16).reshape(queries.shape)
    scores = jnp.einsum("bqhd,bkhd->bhqk", queries, key_rows, preferred_element_type=jnp.float32)
    attn_probs = jnp.exp(scores - log_total[..., None])
    grad_values = jnp.einsum(
        "bhqk,bqhd->bkhd",
        attn_probs.astype(jnp.bfloat16),
        grad_mixed,
        preferred_element_type=jnp.float32,
    )
    grad_probs = jnp.einsum(
        "bqhd,bkhd->bhqk", grad_mixed, value_rows, preferred_element_type=jnp.float32
    )
    grad_scores = (
        attn_probs * (grad_probs - jnp.sum(attn_probs * grad_probs, axis=-1, keepdims=True))
    ).astype(jnp.bfloat16)
    grad_queries = jnp.einsum(
        "bhqk,bkhd->bqhd", grad_scores, key_rows, preferred_element_type=jnp.float32
    )
    grad_keys = jnp.einsum(
        "bhqk,bqhd->bkhd", grad_scores, queries, preferred_element_type=jnp.float32
    )
    grad_projected = jnp.concatenate(
        [
            grad_queries.reshape(group_rows, head_cols),
            grad_keys.reshape(group_rows, head_cols),
            grad_values.reshape(group_rows, head_cols),
        ],
        axis=1,
    ).astype(jnp.bfloat16)
    qkv_flat_grad = jnp.einsum(
        "td,tc->dc", normed, grad_projected, preferred_element_type=jnp.float32
    )
    column_scale = jnp.concatenate(
        [jnp.full((head_cols,), q_scale, jnp.float32), jnp.ones((2 * head_cols,), jnp.float32)]
    )
    qkv_grad = jnp.transpose(
        (qkv_flat_grad * column_scale).reshape(widths, 3, head_cols), (1, 0, 2)
    )
    query_term = (
        jnp.einsum(
            "tc,dc->td",
            grad_projected[:, :head_cols],
            flat_qkv[:, :head_cols],
            preferred_element_type=jnp.float32,
        )
        * q_scale
    )
    grad_normed = lax.psum_scatter(
        query_term
        + jnp.einsum(
            "tc,dc->td",
            grad_projected[:, head_cols:],
            flat_qkv[:, head_cols:],
            preferred_element_type=jnp.float32,
        ),
        ("heads", "tensor"),
        scatter_dimension=0,
        tiled=True,
    )
    first_value, first_pull = jax.vjp(layer_norm, residual, ln_gains[0], ln_shift[0])
    grad_input, gain_one, shift_one = first_pull(grad_normed)
    grad_input = grad_input + grad_middle
    matrix_grads = (qkv_grad, out_grad, in_grad, back_grad)
    small_grads = (jnp.stack([gain_one, gain_two]), jnp.stack([shift_one, shift_two]), router_grad)
    return (grad_input, matrix_grads, small_grads)


def on_device(
    tokens,
    cotangent,
    image_counts,
    w_qkv,
    w_out,
    ln_gain,
    ln_bias,
    w_router,
    w_in,
    w_back,
    expert_ids,
    slots,
):
    own_rows = tokens.shape[0]
    row_start = lax.axis_index(("heads", "tensor")) * own_rows
    first_expert = lax.axis_index("heads") * w_in.shape[1]
    residual = tokens.astype(jnp.float32)
    head_list = []
    block_index = 0
    weights = (
        lax.all_gather(w_qkv[block_index], "fsdp", axis=1, tiled=True),
        lax.all_gather(w_out[block_index], "fsdp", axis=1, tiled=True),
        lax.all_gather(w_in[block_index], "fsdp", axis=1, tiled=True),
        lax.all_gather(w_back[block_index], "fsdp", axis=2, tiled=True),
    )
    residual, stored, head_full = forward_block(
        residual,
        weights,
        ln_gain[block_index],
        ln_bias[block_index],
        w_router[block_index],
        expert_ids[block_index],
        slots[block_index],
        first_expert,
    )
    stored_list = [stored]
    head_list.append(head_full)
    image_index = (row_start + jnp.arange(own_rows, dtype=jnp.int32)) // SEQ
    live_rows = (image_index < image_counts[0]).astype(jnp.float32)
    grad_rows = cotangent.astype(jnp.float32) * live_rows[:, None]
    matrix_list = [None] * LAYERS
    small_list = [None] * LAYERS
    for block_index in reversed(range(LAYERS)):
        weights = (
            lax.all_gather(w_qkv[block_index], "fsdp", axis=1, tiled=True),
            lax.all_gather(w_out[block_index], "fsdp", axis=1, tiled=True),
            lax.all_gather(w_in[block_index], "fsdp", axis=1, tiled=True),
            lax.all_gather(w_back[block_index], "fsdp", axis=2, tiled=True),
        )
        grad_rows, matrix_grads, small_grads = backward_block(
            grad_rows,
            stored_list[block_index],
            weights,
            ln_gain[block_index],
            ln_bias[block_index],
            w_router[block_index],
            expert_ids[block_index],
            row_start,
        )
        matrix_list[block_index] = (
            lax.psum_scatter(matrix_grads[0], "fsdp", scatter_dimension=1, tiled=True),
            lax.psum_scatter(matrix_grads[1], "fsdp", scatter_dimension=1, tiled=True),
            lax.psum_scatter(matrix_grads[2], "fsdp", scatter_dimension=1, tiled=True),
            lax.psum_scatter(matrix_grads[3], "fsdp", scatter_dimension=2, tiled=True),
        )
        small_list[block_index] = small_grads
    gain_grads, shift_grads, router_grads = lax.psum(
        (
            jnp.stack([entry[0] for entry in small_list]),
            jnp.stack([entry[1] for entry in small_list]),
            jnp.stack([entry[2] for entry in small_list]),
        ),
        ("fsdp", "heads", "tensor"),
    )
    qkv_grads = jnp.stack([entry[0] for entry in matrix_list])
    out_grads = jnp.stack([entry[1] for entry in matrix_list])
    in_grads = jnp.stack([entry[2] for entry in matrix_list])
    back_grads = jnp.stack([entry[3] for entry in matrix_list])
    return (
        residual.astype(jnp.bfloat16),
        grad_rows,
        qkv_grads,
        out_grads,
        gain_grads,
        shift_grads,
        router_grads,
        in_grads,
        back_grads,
    )


ROWS = -(-SEQ // 16) * 16
MESH = pl.DeviceIdType.MESH
F32, BF16 = jnp.float32, jnp.bfloat16
NN, NT, TN = (((1,), (0,)), ((), ())), (((1,), (1,)), ((), ())), (((0,), (0,)), ((), ()))


def mm(left, right, dims=NN):
    return lax.dot_general(left, right, dims, preferred_element_type=F32)


def whole(index, size):
    return pl.ds(pl.multiple_of(index * size, size), size)


def normal_parts(value):
    centred = value - jnp.mean(value, axis=-1, keepdims=True)
    scale = lax.rsqrt(jnp.mean(centred * centred, axis=-1, keepdims=True) + 1e-06)
    return centred * scale, scale


def normal_pull(grad, unit, scale, gains):
    grad_unit = grad * gains
    mean_grad = jnp.mean(grad_unit, axis=-1, keepdims=True)
    mean_both = jnp.mean(grad_unit * unit, axis=-1, keepdims=True)
    return scale * (grad_unit - mean_grad - unit * mean_both)


def gelu_parts(value):
    size = jnp.abs(value)
    step = 1.0 / (1.0 + 0.3275911 * 2.0**-0.5 * size)
    bell = jnp.exp(-0.5 * (value * value))
    series = 1.061405429 * step - 1.453152027
    series = series * step + 1.421413741
    series = series * step - 0.284496736
    series = series * step + 0.254829592
    tail = 0.5 * series * step * bell
    share = jnp.where(value < 0, tail, 1.0 - tail)
    return value * share, share + value * (bell * 0.3989422804014327)


class Exchange:
    def __init__(self, source, target, device, landing, send, recv):
        self.out = pltpu.make_async_remote_copy(
            source, target, send, recv, device_id=device, device_id_type=MESH
        )
        self.into = pltpu.make_async_remote_copy(
            landing, landing, send, recv, device_id=device, device_id_type=MESH
        )

        self.open = [True, True]
        self.out.start()

    def arrived(self):
        if self.open[0]:
            self.into.wait_recv()
        self.open[0] = False

    def sent(self):
        if self.open[1]:
            self.out.wait_send()
        self.open[1] = False

    def finish(self):
        self.arrived()
        self.sent()


class Kept:
    def __init__(self, source, target, semaphore):
        self.copy = pltpu.make_async_copy(source, target, semaphore)
        self.open = True
        self.copy.start()

    def arrived(self):
        if self.open:
            self.copy.wait()
        self.open = False

    sent = finish = arrived


def block_kernel(depth_z, images, local_count, refs):
    H = depth_z
    (
        tokens, cot, counts, wq, wo, gain, bias, wr, win_hbm, wback_hbm, named_in, slots_in,
        out, tgrad, wqg, wog, lng, lnb, wrg, gin_out, gback_out,
        tgrad_held, stage, prow, wbuf, win, wback, rows_grad, rows_norm, big, wide,
        xsend, gsend, xrows, grows, xback, gback,
        normed, qkv, probs, mixed, middle, grad_mid, logit_grad,
        sib_out, sib_in, z_out, z_in, own_sum,
        att_in, plane_in, line_out, line_in,
        small_c, small_p, small_z, route_out, route_in, route_z, route_all,
        send_sems, recv_sems, local_sems,
    ) = refs
    own_rows, width = tokens.shape
    flat = -(-own_rows // 16) * 16
    half = width // 128
    f, h, t = (lax.axis_index(name) for name in ("fsdp", "heads", "tensor"))
    s = 1 - t
    fx = [f, f + 1 - 2 * lax.rem(f, 2), lax.rem(f + 2, 4), 3 - f]
    hz = [lax.rem(h + d, H) for d in range(H)]
    hfrom = [lax.rem(h + H - d, H) for d in range(H)]
    after, before, across = lax.rem(2 * h + 1, 5), lax.rem(3 * h + 2, 5), 3 - h
    counter = [0]
    pending = []

    def exchange(source, target, device, landing):
        index = counter[0]
        counter[0] += 1
        made = Exchange(
            source, target, device, landing, send_sems.at[index], recv_sems.at[index]
        )
        pending.append(made)
        return made

    local_counter = [0]

    def kept(source, target):
        made = Kept(source, target, local_sems.at[local_counter[0]])
        local_counter[0] += 1
        pending.append(made)
        return made

    barrier = pltpu.get_barrier_semaphore()
    peers = [(f, hz[d], t) for d in range(1, H)] + [(f, h, s)]
    peers += [(fx[d], h, c) for d in range(1, 4) for c in (t, s)]
    for peer in peers:
        pl.semaphore_signal(barrier, inc=1, device_id=peer, device_id_type=MESH)

    for i in range(3):
        wbuf[i, h, t, :, whole(f, 128)] = wq[i]
    wbuf[3, h, t, :, whole(f, 128)] = wo[...]
    pl.semaphore_wait(barrier, len(peers))

    first = [
        exchange(*[wbuf.at[:, h, t, :, whole(f, 128)]] * 2, (f, hz[d], t),
                 wbuf.at[:, hfrom[d], t, :, whole(f, 128)])
        for d in range(1, H)
    ]

    depth, span = win_hbm.shape[1], win_hbm.shape[2]

    def move_in(d, c):
        landing = win.at[whole(fx[d], depth), whole(c, span)]
        target = win.at[whole(f, depth), whole(t, span)]
        return exchange(win_hbm.at[fx[d] * 2 + c], target, (fx[d], h, c), landing)

    def move_back(d, c):
        landing = wback.at[whole(c, span), whole(fx[d], depth)]
        target = wback.at[whole(t, span), whole(f, depth)]
        return exchange(wback_hbm.at[fx[d] * 2 + c], target, (fx[d], h, c), landing)

    expert_moves = [move_in(d, c) for d, c in ((1, t), (2, t))]
    mine = [
        kept(win_hbm.at[f * 2 + t], win.at[whole(f, depth), whole(t, span)]),
        kept(wback_hbm.at[f * 2 + t], wback.at[whole(t, span), whole(f, depth)]),
    ]

    row_index = lax.broadcasted_iota(jnp.int32, (ROWS, 1), 0)

    def image(source, b):
        if b == 0:
            stage[0 : images * SEQ, :] = source[...].astype(F32)
        return jnp.where(row_index < SEQ, stage[b * SEQ : b * SEQ + ROWS, :], 0.0)

    flat_index = lax.broadcasted_iota(jnp.int32, (flat, 1), 0)
    flat_image = sum((flat_index >= b * SEQ).astype(jnp.int32) for b in range(1, images))
    living = (flat_index < own_rows) & ((h * 2 + t) * images + flat_image < counts[0])
    stage[0:own_rows, :] = cot[...].astype(F32)
    rows_grad[h * 2 + t, 0:flat, :] = jnp.where(living, stage[0:flat, :], 0.0).astype(BF16)

    cut = -(-flat // 32) * 16
    parts = [slice(0, cut), slice(cut, flat)]

    def hop(rows, line, part, to, source):
        here = rows.at[line * 2 + t, parts[part]]
        return exchange(here, here, (f, to, t), rows.at[source * 2 + t, parts[part]])

    def beside(rows, line):
        here = rows.at[line * 2 + t, 0:flat]
        return exchange(here, here, (f, h, s), rows.at[line * 2 + s, 0:flat])

    class Spread:
        def __init__(self, rows):
            self.rows = rows
            self.down = [hop(rows, h, 0, after, before), None]
            self.up = [None, hop(rows, h, 1, before, after)]
            self.near = [beside(rows, h)]

        def second(self):
            self.down[1] = hop(self.rows, h, 1, after, before)
            self.up[0] = hop(self.rows, h, 0, before, after)

        def relay(self):
            self.down[0].arrived()
            self.far = [hop(self.rows, before, 0, after, across)]
            self.up[1].arrived()
            self.far.append(hop(self.rows, after, 1, before, across))

        def share(self):
            self.down[1].arrived()
            self.near.append(beside(self.rows, before))
            self.up[0].arrived()
            self.near.append(beside(self.rows, after))

        def close(self):
            for move in self.far:
                move.arrived()
            self.near.append(beside(self.rows, across))

        def blocks(self):
            lines = [h, before, after, across]
            moves = self.near + [None] * (4 - len(self.near))
            return [(line * 2 + t, None) for line in lines] + [
                (line * 2 + s, move) for line, move in zip(lines, moves)
            ]

        def sent(self):
            for move in self.down + self.up + self.far + self.near:
                move.sent()

    grad_spread = Spread(rows_grad)

    for b in range(images):
        unit, _ = normal_parts(image(tokens, b))
        normed[b * ROWS : (b + 1) * ROWS, :] = (unit * gain[0:1] + bias[0:1]).astype(BF16)

    for step in first:
        step.arrived()

    def across_plane(span_i, source, to, landing):
        here = wbuf.at[span_i, :, t, :, whole(source, 128)]
        return exchange(here, here, (to, h, t), wbuf.at[span_i, :, t, :, whole(landing, 128)])

    both = [slice(0, 2), slice(2, 4)]
    second = [across_plane(slice(0, 4), f, fx[d], fx[d]) for d in (1, 2)]

    relative = named_in[...] - h * local_count
    wanted = (slots_in[...] >= 0) & (relative >= 0) & (relative < local_count)
    wanted = wanted & (lax.rem(relative + 2 * local_count, 2) == t)
    places = jnp.where(wanted, lax.div(relative, 2) * CAP + slots_in[...], -1)
    reach = -(-flat // 128) * 128 + 128
    tail = jnp.full((2, reach), -1, jnp.int32)
    places = jnp.concatenate([places, tail], axis=1)[:, 0 : places.shape[1] // 128 * 128 + reach]
    place_lane = lax.broadcasted_iota(jnp.int32, (2, reach), 1)
    for b in range(2 * H):
        begin = b * own_rows
        base = begin // 128 * 128
        window = pltpu.roll(places[:, base : base + reach], (base - begin) % reach, 1)
        rows = jnp.where(place_lane < own_rows, window, -1)
        prow[b, 0:2, :] = rows[:, 0 : prow.shape[2]]

    def mark_slots(b):
        for part in range(4):
            spot = lax.broadcasted_iota(jnp.int32, (CAP, flat), 0) + CAP * part
            named = (prow[b, 0:1, 0:flat] == spot) | (prow[b, 1:2, 0:flat] == spot)
            big[b, part * CAP : (part + 1) * CAP, 0:flat] = jnp.where(named, 1.0, 0.0).astype(BF16)

    grad_spread.second()
    pl.loop(0, 2 * H)(mark_slots)
    for d in (1, 2):
        second[d - 1].arrived()
        second.append(across_plane(both[d - 1], fx[d], fx[3 - d], fx[3]))
    grad_spread.relay()
    for step in second[2:]:
        step.arrived()
    third = exchange(*[wbuf.at[:, :, t]] * 2, (f, h, s), wbuf.at[:, :, s])

    for d, c in ((1, s), (2, s), (3, t), (3, s), (0, s)):
        expert_moves.append(move_in(d, c))
    for d, c in ((1, t), (2, t), (1, s), (2, s), (3, t), (3, s), (0, s)):
        expert_moves.append(move_back(d, c))

    grad_spread.share()
    third.arrived()

    for i in range(3):
        part = mm(normed[...], wbuf[i].reshape(width, width), NT)
        if i == 0:
            part = part * HEAD ** (-0.5)
        qkv[:, i * width : (i + 1) * width] = part.astype(BF16)
    lane = lax.broadcasted_iota(jnp.int32, (1, 128), 1)
    sides = [jnp.where(lane < HEAD, 1.0, 0.0).astype(BF16), jnp.where(lane < HEAD, 0.0, 1.0).astype(BF16)]
    key_index = lax.broadcasted_iota(jnp.int32, (1, ROWS), 1)

    def pair_of(index):
        b, pair = index // half, lax.rem(index, half)
        rows = whole(b, ROWS)
        cols = [whole(pair + i * half, 128) for i in range(3)]
        return rows, cols

    @pl.loop(0, images * half)
    def _(index):
        rows, cols = pair_of(index)
        query, key, value = (qkv[rows, col] for col in cols)
        total = jnp.zeros((ROWS, 128), F32)
        for side in range(2):
            score = mm(query * sides[side], key, NT)
            score = jnp.where(key_index < SEQ, score, -1e30)
            score = jnp.exp(score - jnp.max(score, axis=-1, keepdims=True))
            prob = score / jnp.sum(score, axis=-1, keepdims=True)
            probs[index * 2 + side] = prob
            total += mm(prob.astype(BF16), value * sides[side])
        mixed[rows, cols[0]] = total.astype(BF16)

    for b in range(images):
        rows = slice(b * ROWS, (b + 1) * ROWS)
        value = image(tokens, b) + mm(mixed[rows, :], wbuf[3].reshape(width, width))
        middle[rows, :] = value
        unit, _ = normal_parts(value)
        own_sum[0, b * SEQ : (b + 1) * SEQ, :] = (unit * gain[1:2] + bias[1:2])[0:SEQ]
    own_flat = jnp.where(flat_index < own_rows, own_sum[0, 0:flat, :], 0.0)
    rows_norm[h * 2 + t, 0:flat, :] = own_flat.astype(BF16)

    norm_spread = Spread(rows_norm)
    grad_spread.close()

    def accumulate(rows, b, begin):
        for part in range(4):
            span_rows = slice(part * CAP, (part + 1) * CAP)
            value = mm(big[b, span_rows, 0:flat], rows[b, 0:flat])
            wide[span_rows, :] = value if begin else wide[span_rows, :] + value

    def accumulate_all(spread, order):
        blocks = spread.blocks()
        for place in order:
            b, move = blocks[place]
            if move is not None:
                move.arrived()
            accumulate(spread.rows, b, place == 0)

    def pack(send):
        for part in range(4):
            send[part] = wide[part * CAP : (part + 1) * CAP, :].astype(BF16)

    def to_group(d, send, landing):
        return exchange(send.at[fx[d]], landing.at[f], (fx[d], h, t), landing.at[fx[d]])

    def dispatch(send, landing, last=4):
        landing[f] = send[f]
        return [None] + [to_group(d, send, landing) for d in range(1, last)]

    accumulate_all(grad_spread, (0, 1, 2, 3))
    norm_spread.second()
    accumulate_all(grad_spread, (4, 5, 6, 7))
    pack(gsend)
    norm_spread.relay()
    grad_moved = dispatch(gsend, grows)
    norm_spread.share()
    accumulate_all(norm_spread, (0, 1, 2, 4, 5, 6))
    norm_spread.close()
    accumulate_all(norm_spread, (3, 7))
    pack(xsend)
    norm_moved = dispatch(xsend, xrows, 3)

    expert = h * local_count + f * 2 + t
    router_lane = lax.broadcasted_iota(jnp.int32, (1, wr.shape[0]), 1)
    chosen = (router_lane == expert).astype(F32)
    chunk = 512
    chunks = win.shape[1] // chunk
    for move in mine + expert_moves:
        move.arrived()
    back_moves = []
    for d in range(4):
        group = fx[d]
        here = whole(group, CAP)
        if d:
            norm_moved[d].arrived()
        rows = xrows[group]
        piece = 256
        ahead = mm(rows, win[:, 0:piece])
        result, held = None, None
        for c in range(win.shape[1] // piece):
            here_in = slice(c * piece % chunk, c * piece % chunk + piece)
            hidden = ahead
            if c + 1 < win.shape[1] // piece:
                ahead = mm(rows, win[:, (c + 1) * piece : (c + 2) * piece])
            value, slope = gelu_parts(hidden)
            value = value.astype(BF16)
            big[c * piece // chunk, here, here_in] = value
            wide[c * piece // chunk * CAP : (c * piece // chunk + 1) * CAP, here_in] = slope
            if c:
                term = mm(held, wback[(c - 1) * piece : c * piece, :])
                result = term if c == 1 else result + term
            held = value
        result = result + mm(held, wback[win.shape[1] - piece :, :])
        logits = mm(rows, wr[...], NT)
        odds = jnp.exp(logits - jnp.max(logits, axis=-1, keepdims=True))
        odds = odds / jnp.sum(odds, axis=-1, keepdims=True)
        gate = jnp.sum(odds * chosen, axis=-1, keepdims=True)
        if d:
            grad_moved[d].finish()
            norm_moved[d].sent()
        gsend[group] = (gate * result).astype(BF16)
        row_grad = grows[group].astype(F32)
        gate_grad = jnp.sum(row_grad * result, axis=-1, keepdims=True)
        result_grad = (gate * row_grad).astype(BF16)
        grows[group] = result_grad
        logit = (gate_grad * gate * (chosen - odds)).astype(BF16)
        logit_grad[here, :] = logit
        parts_grad = []
        for c in range(chunks):
            grad = mm(result_grad, wback[c * chunk : (c + 1) * chunk, :], NT)
            grad = (grad * wide[c * CAP : (c + 1) * CAP, :]).astype(BF16)
            big[4 + c, here, :] = grad
            parts_grad.append(grad)
        total = mm(logit, wr[...]) + mm(jnp.concatenate(parts_grad, axis=1), win[...], NT)
        if d:
            xsend[group] = total.astype(BF16)
            back_moves.append(to_group(d, xsend, xback))
        else:
            xback[f] = total.astype(BF16)
        if d == 0:
            norm_moved.append(to_group(3, xsend, xrows))

    grad_spread.sent()
    norm_spread.sent()
    flat_rows = xrows[...].reshape(4 * CAP, width)
    route = mm(logit_grad[...], flat_rows, TN)
    share_rows = wr.shape[0] // 8
    for j in range(8):
        for part in range(2):
            route_out[j, part * share_rows : (part + 1) * share_rows, :] = route[
                j * share_rows : (j + 1) * share_rows, part * (width // 2) : (part + 1) * (width // 2)
            ]
    route_in[f * 2 + t] = route_out[f * 2 + t]
    plane_peers = [(d, c) for d in range(4) for c in ((t, s) if d else (s,))]
    route_moves = [
        exchange(route_out.at[fx[d] * 2 + c], route_in.at[f * 2 + t], (fx[d], h, c), route_in.at[fx[d] * 2 + c])
        for d, c in plane_peers
    ]
    flat_grad = grows[...].reshape(4 * CAP, width)
    for c in range(chunks):
        rows_grad[c] = mm(flat_rows, big[4 + c], TN).astype(BF16)
        rows_norm[c] = mm(big[c], flat_grad, TN).astype(BF16)
    for move in route_moves:
        move.arrived()
    route = route_in[0]
    for j in range(1, 8):
        route = route + route_in[j]
    route_z[h] = route
    route_line = [
        exchange(route_z.at[h], route_z.at[h], (f, hz[d], t), route_z.at[hfrom[d]]) for d in range(1, H)
    ]

    for move in back_moves:
        move.arrived()
    out_moves = dispatch(gsend, gback)[1:]

    halves = chunks // 2

    def to_owner(d, c, part, back):
        device, one = (fx[d], h, c), d == 0 and c is t
        span_part = slice(part * chunk, (part + 1) * chunk)
        if back:
            source = rows_norm.at[c * halves + part, :, whole(fx[d], depth)]
            target = gback_out.at[f * 2 + t, span_part]
            landing = gback_out.at[fx[d] * 2 + c, span_part]
        else:
            source = rows_grad.at[c * halves + part, whole(fx[d], depth), :]
            target = gin_out.at[f * 2 + t, :, span_part]
            landing = gin_out.at[fx[d] * 2 + c, :, span_part]
        if one:
            kept(source, target)
        else:
            exchange(source, target, device, landing)

    def to_owners(part, back):
        for d in (1, 2, 3, 0):
            for c in (t, s):
                to_owner(d, c, part, back)

    def share(b, back):
        spots = jnp.transpose(prow[b])[0:flat]
        slot = lax.broadcasted_iota(jnp.int32, (flat, 4 * CAP), 1)
        named = (spots[:, 0:1] == slot) | (spots[:, 1:2] == slot)
        return mm(jnp.where(named, 1.0, 0.0).astype(BF16), back[...].reshape(4 * CAP, width))

    class Gather:
        def __init__(self, which, back, near_out, far_out):
            self.which, self.back = which, back
            self.near_out, self.far_out = near_out, far_out
            self.lines = [across, after, before, h]
            self.near = []

        def give(self, place):
            line = self.lines[place]
            self.near_out(place)[...] = share(line * 2 + s, self.back).astype(BF16)
            landing = sib_in.at[self.which, place]
            self.near.append(exchange(self.near_out(place), landing, (f, h, s), landing))

        def take(self, place):
            value = share(self.lines[place] * 2 + t, self.back)
            self.near[place].arrived()
            value = value + sib_in[self.which, place].astype(F32)
            if place == 3:
                own_sum[self.which, 0:flat, :] = value
            else:
                self.far_out(place)[...] = value.astype(BF16)

        def hop(self, place, part, to, slot):
            landing = z_in.at[self.which, slot, parts[part]]
            return exchange(self.far_out(place).at[parts[part]], landing, (f, to, t), landing)

        def start(self):
            self.first = [self.hop(0, 0, after, 0), self.hop(0, 1, before, 0)]

        def direct(self, place):
            part, to = ((1, after), (0, before))[place - 1]
            self.last = getattr(self, "last", []) + [self.hop(place, part, to, place)]

        def relay(self):
            for place, part, to in ((1, 0, after), (2, 1, before)):
                self.first[part].arrived()
                rows = self.far_out(place).at[parts[part]]
                passed = z_in[self.which, 0, parts[part], :].astype(F32)
                rows[...] = (rows[...].astype(F32) + passed).astype(BF16)
                self.last.append(self.hop(place, part, to, place))

        def total(self):
            for move in self.last:
                move.arrived()
            total = own_sum[self.which, 0:flat, :]
            for slot in (1, 2):
                total = total + z_in[self.which, slot].astype(F32)
            own_sum[self.which, 0:flat, :] = total

    norm_sums = Gather(0, xback, lambda place: sib_out.at[place], lambda place: z_out.at[place])
    norm_sums.give(0)
    norm_sums.take(0)
    norm_sums.start()
    to_owners(0, True)
    norm_sums.give(1)
    norm_sums.give(2)
    norm_sums.take(1)
    norm_sums.direct(1)
    norm_sums.take(2)
    norm_sums.direct(2)
    norm_sums.give(3)
    norm_sums.take(3)
    for move in out_moves:
        move.arrived()
    to_owners(1, True)
    to_owners(0, False)
    out_sums = Gather(
        1, gback, lambda place: big.at[place, 0:flat], lambda place: big.at[4 + place, 0:flat]
    )
    out_sums.give(0)
    out_sums.take(0)
    for place in range(1, 4):
        out_sums.give(place)
    norm_sums.relay()
    for place in range(1, 4):
        out_sums.take(place)


    norm_sums.total()
    out_sums.start()
    small_c[t] = jnp.zeros(small_c.shape[1:], F32)
    for b in range(images):
        rows = slice(b * ROWS, (b + 1) * ROWS)
        grad = jnp.where(row_index < SEQ, own_sum[0, b * SEQ : b * SEQ + ROWS, :], 0.0)
        unit, scale = normal_parts(middle[rows, :])
        small_c[t, 1:2] += jnp.sum(grad * unit, axis=0, keepdims=True)
        small_c[t, 3:4] += jnp.sum(grad, axis=0, keepdims=True)
        live = ((h * 2 + t) * images + b < counts[0]).astype(F32)
        grad = normal_pull(grad, unit, scale, gain[1:2]) + image(cot, b) * live
        grad_mid[rows, :] = grad

    out_sums.direct(1)
    out_sums.direct(2)

    for move in back_moves:
        move.sent()
    low = grad_mid[...].astype(BF16)
    count = H * 2 * 64
    wide[3 * count : 4 * count, :] = mm(mixed[...], low, TN)

    def wide_rows(i, other, core):
        return whole((i * H + other) * 2 + core, 64)

    def core_sums(span_i, others):
        for i in span_i:
            for other in others:
                xsend[i, whole(other, 64), :] = wide[wide_rows(i, other, s), :].astype(BF16)
        here = (slice(span_i.start, span_i.stop), whole(others[0], 64))
        if len(others) > 1:
            here = (here[0], slice(0, H * 64))
        landing = att_in.at[here]
        return here, exchange(xsend.at[here], landing, (f, h, s), landing)

    def plane_sums(span_i, others, near):
        here, move = near
        move.finish()
        for i in span_i:
            for other in others:
                place, low_rows = wide_rows(i, other, t), whole(other, 64)
                value = wide[place, :] + att_in[i, low_rows, :].astype(F32)
                wide[place, :] = value
                xsend[i, low_rows, :] = value.astype(BF16)
        return [
            exchange(
                xsend.at[(*here, whole(fx[d], 128))], plane_in.at[(f, *here)],
                (fx[d], h, t), plane_in.at[(fx[d], *here)],
            )
            for d in range(1, 4)
        ]

    def own_columns(i, other):
        value = wide[wide_rows(i, other, t), whole(f, 128)]
        for d in range(1, 4):
            value = value + plane_in[fx[d], i, whole(other, 64), :].astype(F32)
        return value

    last_near = core_sums(range(3, 4), list(range(H)))
    mixed[...] = mm(low, wbuf[3].reshape(width, width), NT).astype(BF16)

    def attention_back(index):
        rows, cols = pair_of(index)
        query, key, value = (qkv[rows, col] for col in cols)
        pulled = mixed[rows, cols[0]]
        grads = [jnp.zeros((ROWS, 128), F32) for _ in range(3)]
        for side in range(2):
            prob = probs[index * 2 + side]
            one = pulled * sides[side]
            prob_grad = mm(one, value, NT)
            grads[2] += mm(prob.astype(BF16), one, TN)
            inner = jnp.sum(prob * prob_grad, axis=-1, keepdims=True)
            score_grad = (prob * (prob_grad - inner)).astype(BF16)
            grads[0] += mm(score_grad, key * sides[side])
            grads[1] += mm(score_grad, query * sides[side], TN)
        grads[0] = grads[0] * HEAD ** (-0.5)
        for grad, col in zip(grads, cols):
            qkv[rows, col] = grad.astype(BF16)

    order = [hz[1], hz[2], hz[3], hz[0]]
    nears, planes = [], []
    for turn, other in enumerate(order):
        pl.loop(0, images)(lambda b, other=other: attention_back(b * half + other))
        for i in range(3):
            rows = pl.ds(pl.multiple_of((i * H + other) * 128, 128), 128)
            wide[rows, :] = mm(qkv[:, whole(i * half + other, 128)], normed[...], TN)
        nears.append(core_sums(range(3), [other]))
        if turn == 0:
            last_plane = plane_sums(range(3, 4), list(range(H)), last_near)
        else:
            planes.append(plane_sums(range(3), [order[turn - 1]], nears[turn - 1]))
    out_sums.relay()

    for b in range(images):
        rows = slice(b * ROWS, (b + 1) * ROWS)
        grad = jnp.zeros((ROWS, width), F32)
        for i in range(3):
            grad += mm(qkv[rows, i * width : (i + 1) * width], wbuf[i].reshape(width, width))
        unit, scale = normal_parts(image(tokens, b))
        small_c[t, 0:1] += jnp.sum(grad * unit, axis=0, keepdims=True)
        small_c[t, 2:3] += jnp.sum(grad, axis=0, keepdims=True)
        grad = normal_pull(grad, unit, scale, gain[0:1]) + grad_mid[rows, :]
        tgrad_held[b * SEQ : (b + 1) * SEQ, :] = grad[0:SEQ]
    kept(tgrad_held, tgrad)
    small_near = exchange(small_c.at[t], small_c.at[t], (f, h, s), small_c.at[s])

    planes.append(plane_sums(range(3), [order[3]], nears[3]))
    for move in last_plane:
        move.arrived()
    line = []

    def send_line(turn):
        for move in planes[turn]:
            move.arrived()
        other = order[turn]
        for i in range(4):
            line_out[other, i] = own_columns(i, other).astype(BF16)
        landing = line_in.at[hfrom[turn + 1]]
        line.append(exchange(line_out.at[other], line_in.at[h], (f, other, t), landing))

    send_line(0)
    send_line(1)
    small_near.arrived()
    small_p[f] = small_c[0] + small_c[1]
    small_plane = [
        exchange(small_p.at[f], small_p.at[f], (fx[d], h, t), small_p.at[fx[d]]) for d in range(1, 4)
    ]
    for move in route_line:
        move.arrived()
    route = route_z[0]
    for d in range(1, H):
        route = route + route_z[d]
    route_all[f * 2 + t] = route
    route_last = [
        exchange(route_all.at[f * 2 + t], route_all.at[f * 2 + t], (fx[d], h, c), route_all.at[fx[d] * 2 + c])
        for d, c in plane_peers
    ]

    send_line(2)
    to_owners(1, False)
    for move in planes[3]:
        move.arrived()
    for move in small_plane:
        move.arrived()
    small_z[h] = (small_p[0] + small_p[1]) + (small_p[2] + small_p[3])
    small_line = [
        exchange(small_z.at[h], small_z.at[h], (f, hz[d], t), small_z.at[hfrom[d]]) for d in range(1, H)
    ]
    for move in route_last:
        move.arrived()
    for j in range(8):
        for part in range(2):
            wrg[j * share_rows : (j + 1) * share_rows, part * (width // 2) : (part + 1) * (width // 2)] = (
                route_all[j, part * share_rows : (part + 1) * share_rows, :]
            )

    out_sums.total()
    for b in range(images):
        stage[b * SEQ : (b + 1) * SEQ, :] = middle[b * ROWS : b * ROWS + SEQ, :]
    out[...] = (stage[0:own_rows, :] + own_sum[1, 0:own_rows, :]).astype(BF16)

    for move in line:
        move.arrived()
    for i in range(4):
        value = own_columns(i, h)
        for d in range(1, H):
            value = value + line_in[hfrom[d], i].astype(F32)
        if i < 3:
            wqg[i] = value
        else:
            wog[...] = value
    for move in small_line:
        move.arrived()
    total = small_z[0]
    for d in range(1, H):
        total = total + small_z[d]
    lng[...] = total[0:2]
    lnb[...] = total[2:4]

    for move in pending:
        move.finish()


def finish_kernel(*refs):
    sources, targets = refs[:9], refs[9:18]
    held, wider = refs[18:27], refs[27:29]
    in_sems, out_sems = refs[29], refs[30]
    experts = sources[7].shape[0]
    inward, outward = [], []

    def begin(source, target, semaphores, index):
        copy = pltpu.make_async_copy(source, target, semaphores.at[index])
        copy.start()
        return copy

    for e in range(experts):
        for k in (7, 8):
            index = 7 + 2 * e + k - 7
            inward.append((e, k, index, begin(sources[k].at[e], held[k].at[e], in_sems, index)))
    small = [begin(sources[k], held[k], in_sems, k) for k in range(7)]
    for e, k, index, copy in inward:
        copy.wait()
        wider[k - 7][e] = held[k][e].astype(F32)
        outward.append(begin(wider[k - 7].at[e], targets[k].at[e], out_sems, index))
    for k, copy in enumerate(small):
        copy.wait()
        outward.append(begin(held[k], targets[k], out_sems, k))
    for copy in outward:
        copy.wait()


def fast_device(
    tokens,
    cotangent,
    image_counts,
    w_qkv,
    w_out,
    ln_gain,
    ln_bias,
    w_router,
    w_in,
    w_back,
    expert_ids,
    slots,
):
    H = lax.axis_size("heads")
    own_rows, width = tokens.shape
    images = own_rows // SEQ
    own = images * ROWS
    flat = -(-own_rows // 16) * 16
    local_count, depth, span = w_in.shape[1:]
    experts = w_router.shape[2]
    hidden = span * 2
    vmem = pl.BlockSpec(memory_space=pltpu.VMEM)
    smem = pl.BlockSpec(memory_space=pltpu.SMEM)
    anywhere = pl.BlockSpec(memory_space=pl.ANY)
    shape = jax.ShapeDtypeStruct

    def low(*dims):
        return pltpu.VMEM(dims, BF16)

    def full(*dims):
        return pltpu.VMEM(dims, F32)

    outs = pl.pallas_call(
        lambda *refs: block_kernel(H, images, local_count, refs),
        out_shape=(
            shape((own_rows, width), BF16),
            shape((own_rows, width), F32),
            shape((3, 64, depth), F32),
            shape((64, depth), F32),
            shape((2, width), F32),
            shape((2, width), F32),
            shape((experts, width), F32),
            shape((local_count, depth, span), BF16),
            shape((local_count, span, depth), BF16),
        ),
        in_specs=[vmem, vmem, smem, vmem, vmem, vmem, vmem, vmem, anywhere, anywhere, vmem, vmem],
        out_specs=[vmem, anywhere] + [vmem] * 5 + [anywhere] * 2,
        scratch_shapes=[
            full(own_rows, width),
            full(images * SEQ + 16, width),
            pltpu.VMEM((2 * H, 8, -(-flat // 128) * 128), jnp.int32),
            low(4, H, 2, 64, width),
            low(width, hidden),
            low(hidden, width),
            low(2 * H, 512, width),
            low(2 * H, 512, width),
            low(8, 4 * CAP, 512),
            full(8 * CAP, width),
            low(4, CAP, width),
            low(4, CAP, width),
            low(4, CAP, width),
            low(4, CAP, width),
            low(4, CAP, width),
            low(4, CAP, width),
            low(own, width),
            low(own, 3 * width),
            full(images * width // HEAD, ROWS, ROWS),
            low(own, width),
            full(own, width),
            full(own, width),
            low(4 * CAP, experts),
            low(H, flat, width),
            low(2, H, flat, width),
            low(3, flat, width),
            low(2, 3, flat, width),
            full(2, own, width),
            low(4, H * 64, width),
            low(4, 4, H * 64, 128),
            low(H, 4, 64, 128),
            low(H, 4, 64, 128),
            full(2, 8, width),
            full(4, 8, width),
            full(H, 8, width),
            full(8, experts // 4, width // 2),
            full(8, experts // 4, width // 2),
            full(H, experts // 4, width // 2),
            full(8, experts // 4, width // 2),
            pltpu.SemaphoreType.DMA((192,)),
            pltpu.SemaphoreType.DMA((192,)),
            pltpu.SemaphoreType.DMA((16,)),
        ],
        compiler_params=pltpu.CompilerParams(
            collective_id=0, has_side_effects=True, vmem_limit_bytes=62 * 2**20
        ),
        name="block",
    )(
        tokens, cotangent, image_counts, jnp.transpose(w_qkv[0], (0, 2, 1)), w_out[0], ln_gain[0], ln_bias[0],
        jnp.transpose(w_router[0]),
        w_in[0], w_back[0], jnp.transpose(expert_ids[0]), jnp.transpose(slots[0]),
    )
    sems = pltpu.SemaphoreType.DMA((7 + 2 * local_count,))
    outs = pl.pallas_call(
        finish_kernel,
        out_shape=[shape(part.shape, F32 if i >= 7 else part.dtype) for i, part in enumerate(outs)],
        in_specs=[anywhere] * 9,
        out_specs=[anywhere] * 9,
        scratch_shapes=[pltpu.VMEM(part.shape, part.dtype) for part in outs]
        + [full(*part.shape) for part in outs[7:]]
        + [sems, sems],
        compiler_params=pltpu.CompilerParams(vmem_limit_bytes=62 * 2**20),
        name="finish",
    )(*outs)
    block_out, token_grad, qkv_grad, out_grad, gains, shifts, router, in_grad, back_grad = outs
    return (
        block_out,
        token_grad,
        jnp.transpose(qkv_grad, (0, 2, 1))[None],
        out_grad[None],
        gains[None],
        shifts[None],
        jnp.transpose(router)[None],
        in_grad[None],
        back_grad[None],
    )


def solution(mesh):
    def program(*arrays):
        sizes = dict(mesh.shape)
        devices = sizes["fsdp"] * sizes["heads"] * sizes["tensor"]
        own_rows = arrays[0].shape[0] // devices
        one_expert = sizes["fsdp"] == 4 and sizes["tensor"] == 2 and arrays[8].shape[1] == devices
        one_expert = one_expert and sizes["heads"] == 4 and own_rows % (2 * SEQ) == 0
        return placed(mesh, fast_device if one_expert else on_device)(*arrays)

    return program


def placed(mesh, on_device):
    return jax.shard_map(
        on_device,
        mesh=mesh,
        in_specs=(
            P(("fsdp", "heads", "tensor"), None),
            P(("fsdp", "heads", "tensor"), None),
            P("fsdp"),
            P(None, None, "fsdp", ("heads", "tensor")),
            P(None, ("heads", "tensor"), "fsdp"),
            P(),
            P(),
            P(),
            P(None, "heads", "fsdp", "tensor"),
            P(None, "heads", "tensor", "fsdp"),
            P(None, "fsdp", None),
            P(None, "fsdp", None),
        ),
        out_specs=(
            P(("fsdp", "heads", "tensor"), None),
            P(("fsdp", "heads", "tensor"), None),
            P(None, None, "fsdp", ("heads", "tensor")),
            P(None, ("heads", "tensor"), "fsdp"),
            P(),
            P(),
            P(),
            P(None, "heads", "fsdp", "tensor"),
            P(None, "heads", "tensor", "fsdp"),
        ),
        check_vma=False,
    )
```
